512 devices in a mesh: pitch: 32 (over x_hi, z), chan: 16 (over x_lo, y, core).
Axes of the slice: x: 4 (x_hi: 2, x_lo: 2; x = x_hi * 2 + x_lo), y: 4, z: 16, core: 2. Of those that a mesh axis runs over, the one named last changes fastest.
Arguments:
- activation: bfloat16 [32, 1024, 4096], P(None, 'chan', 'pitch'), may hold values from -6 to 6
- cotangent: bfloat16 [32, 1024, 4096], P(None, 'chan', 'pitch'), may hold values from -6 to 6
- spectral_weight: bfloat16 [128, 2, 1024, 1024], P('pitch', None, 'chan'), may hold values from -0.5 to 0.5
- out_bias: float32 [1024], P('chan'), may hold values from -3 to 3
Outputs:
- grad_input: bfloat16 [32, 1024, 4096], P(None, 'chan', 'pitch')
- grad_weight: float32 [128, 2, 1024, 1024], P('pitch', None, 'chan')
- grad_bias: float32 [1024], P('chan')
The draws below stay inside these ranges and needn't reach their ends.
All inputs are finite; a program needn't handle non-finite values.
Results may differ from the reference program's by a relative error of at most 0.025.
Values may be sent and summed in bfloat16 or wider, within the bound.
No kernel may reach another device: no remote copies, remote signals or barrier semaphores. Data moves between devices by JAX's collectives and lax.ppermute only.
A program may use at most 64 MiB of HBM per device.

```python
import math
import jax
import jax.numpy as jnp
from jax import lax

P_SIZE = 4096
C = 1024
M = 128
S = 32


def shard_levels(stream_key, extent, shards, smallest, largest):
    def one(dim, parts):
        heights = jax.random.uniform(jax.random.fold_in(jax.random.fold_in(stream_key, 6), dim), (parts,), jnp.float32, smallest / len(shards), largest / len(shards))
        return jnp.repeat(jnp.exp(heights), extent[dim] // parts).reshape((-1,) + (1,) * (len(extent) - dim - 1))

    gain = one(*shards[0])
    for cut in shards[1:]:
        gain = gain * one(*cut)
    return gain


def centred(key, dims, scale, bound, split=(), held_as=jnp.bfloat16):
    level = shard_levels(key, dims, split, -0.22, 0.18) if split else 1.0
    entries = jax.random.normal(key, dims, jnp.float32) * scale * level
    return jnp.minimum(jnp.maximum(entries, -bound), bound).astype(held_as)


def setup_inputs(seed: int = 0) -> dict:
    seeds = jax.random.split(jax.random.key(seed), 5)
    activation = centred(seeds[0], (S, C, P_SIZE), 1.0, 6.0, ((1, 16), (2, 32)))
    cotangent = centred(seeds[1], (S, C, P_SIZE), 1.0, 6.0, ((1, 16), (2, 32)))
    spectral_weight = centred(seeds[2], (M, 2, C, C), (C // 8) ** -0.5, 0.5, ((0, 32), (2, 16)))
    out_bias = centred(seeds[3], (C,), 0.5, 3.0, ((0, 16),), jnp.float32)
    return {"activation": activation, "cotangent": cotangent, "spectral_weight": spectral_weight, "out_bias": out_bias}


block_width = 64
highest = lax.Precision.HIGHEST

def spectral_table(mode_start, mode_count, point_start, point_count, doubled):
    mode_ids = mode_start + jnp.arange(mode_count, dtype=jnp.int32)
    point_ids = point_start + jnp.arange(point_count, dtype=jnp.int32)
    product = mode_ids[:, None] * point_ids[None, :] % P_SIZE
    angles = product.astype(jnp.float32) * (2.0 * math.pi / P_SIZE)
    factor = jnp.full((mode_count,), 1.0 / math.sqrt(P_SIZE), jnp.float32)
    if doubled:
        factor = jnp.where(mode_ids == 0, factor, 2.0 * factor)
    stacked = jnp.stack([jnp.cos(angles), -jnp.sin(angles)], axis=1) * factor[:, None, None]
    return stacked.reshape(2 * mode_count, point_count)

def activate(values):
    return jax.nn.gelu(values, approximate=True)

def forward_modes(grid_field, doubled):
    basis = spectral_table(0, M, 0, P_SIZE, doubled)
    width = grid_field.shape[1]
    flattened = lax.optimization_barrier(grid_field).astype(jnp.float32)
    result = jnp.einsum('scp,jp->jsc', flattened, basis, precision=highest)
    return result.reshape(M, 2, S, width)

def inverse_points(spectra, doubled):
    basis = spectral_table(0, M, 0, P_SIZE, doubled)
    width = spectra.shape[3]
    flattened = spectra.astype(jnp.float32).reshape(2 * M, S, width)
    return jnp.einsum('jsc,jp->scp', flattened, basis, precision=highest)

def block_slice(array, block_index, axis):
    return lax.dynamic_slice_in_dim(array, block_index * block_width, block_width, axis)

def reference(activation, cotangent, spectral_weight, out_bias):
    block_ids = jnp.arange(C // block_width, dtype=jnp.int32)

    def modes_block(block_index):
        return forward_modes(block_slice(activation, block_index, 1), False)
    spectra = lax.map(modes_block, block_ids)
    spectra = jnp.moveaxis(spectra, 0, 3).reshape(M, 2, S, C).astype(jnp.bfloat16)
    spectra = lax.optimization_barrier(spectra)
    real_in = spectra[:, 0].astype(jnp.float32)
    imag_in = spectra[:, 1].astype(jnp.float32)
    weight_re = spectral_weight[:, 0].astype(jnp.float32)
    weight_im = spectral_weight[:, 1].astype(jnp.float32)
    mixed_re = jnp.einsum('ksi,koi->kso', real_in, weight_re) - jnp.einsum('ksi,koi->kso', imag_in, weight_im)
    mixed_im = jnp.einsum('ksi,koi->kso', real_in, weight_im) + jnp.einsum('ksi,koi->kso', imag_in, weight_re)
    mixed = jnp.stack([mixed_re, mixed_im], axis=1).astype(jnp.bfloat16)

    def backward_block(block_index):
        response = inverse_points(block_slice(mixed, block_index, 3), True).astype(jnp.bfloat16)
        bias_block = block_slice(out_bias, block_index, 0)
        pre_act = lax.optimization_barrier(response).astype(jnp.float32) + bias_block[None, :, None]
        unused_out, pullback = jax.vjp(activate, pre_act)
        grad_pre = pullback(block_slice(cotangent, block_index, 1).astype(jnp.float32))[0]
        bias_part = lax.optimization_barrier(jnp.sum(grad_pre, axis=(0, 2)))
        modes_part = forward_modes(grad_pre.astype(jnp.bfloat16), True)
        return (bias_part, modes_part)
    bias_parts, modes_parts = lax.map(backward_block, block_ids)
    grad_bias = bias_parts.reshape(C)
    grad_modes = jnp.moveaxis(modes_parts, 0, 3).reshape(M, 2, S, C).astype(jnp.bfloat16)
    grad_modes = lax.optimization_barrier(grad_modes)
    grad_re = grad_modes[:, 0].astype(jnp.float32)
    grad_im = grad_modes[:, 1].astype(jnp.float32)
    weight_grad_re = jnp.einsum('ksi,kso->koi', real_in, grad_re) + jnp.einsum('ksi,kso->koi', imag_in, grad_im)
    weight_grad_im = jnp.einsum('ksi,kso->koi', real_in, grad_im) - jnp.einsum('ksi,kso->koi', imag_in, grad_re)
    grad_weight = jnp.stack([weight_grad_re, weight_grad_im], axis=1)
    back_re = jnp.einsum('koi,kso->ksi', weight_re, grad_re) + jnp.einsum('koi,kso->ksi', weight_im, grad_im)
    back_im = jnp.einsum('koi,kso->ksi', weight_re, grad_im) - jnp.einsum('koi,kso->ksi', weight_im, grad_re)
    input_modes = jnp.stack([back_re, back_im], axis=1).astype(jnp.bfloat16)

    def input_block(block_index):
        spatial = inverse_points(block_slice(input_modes, block_index, 3), False).astype(jnp.bfloat16)
        summed = block_slice(cotangent, block_index, 1).astype(jnp.float32) + lax.optimization_barrier(spatial).astype(jnp.float32)
        return summed.astype(jnp.bfloat16)
    pieces = lax.map(input_block, block_ids)
    grad_input = jnp.moveaxis(pieces, 0, 1).reshape(S, C, P_SIZE)
    return (grad_input, grad_weight, grad_bias)
```

```python
import functools
import math

import jax
import jax.numpy as jnp
import ml_dtypes
import numpy as np
from jax import lax
from jax.experimental import pallas as pl
from jax.experimental.pallas import tpu as pltpu
from jax.sharding import Mesh
from jax.sharding import PartitionSpec as P

P_SIZE = 4096
M = 128
R = 24
RB = 32
XH = 2
Z = 16
WIN = P_SIZE // (XH * Z)
f32 = jnp.float32
bf16 = jnp.bfloat16
NT = (((1,), (1,)), ((), ()))
NN = (((1,), (0,)), ((), ()))
TN = (((0,), (0,)), ((), ()))
VMEM_LIMIT = 24 * 1024 * 1024


def split_hi_lo(table):
    hi = table.astype(ml_dtypes.bfloat16)
    lo = (table - hi.astype(np.float64)).astype(ml_dtypes.bfloat16)
    return hi, lo


@functools.cache
def tables():
    modes = np.arange(M)
    points = np.arange(P_SIZE)
    angle = 2.0 * math.pi * (np.outer(modes, points) % P_SIZE) / P_SIZE
    forward = np.stack([np.cos(angle), -np.sin(angle)], axis=1).reshape(2 * M, P_SIZE) / math.sqrt(P_SIZE)
    scale = np.repeat(np.where(modes == 0, 1.0, 2.0), 2)[:, None]
    basis = np.linalg.svd(forward[:, :WIN])[2][:R]
    windows = forward.reshape(2 * M, XH * Z, WIN)
    coef = np.einsum("jwp,rp->wjr", windows, basis)
    out = {}
    hi, lo = split_hi_lo(basis)
    out["points"] = np.concatenate([hi, lo], axis=0)
    out["expand"] = np.concatenate([hi, lo, hi], axis=0)
    for name, factor, rows in (("plain", 1.0, R), ("doubled", scale, RB)):
        part = np.zeros((XH * Z, 2 * M, rows))
        part[:, :, :R] = coef * factor
        part = part.reshape(XH, Z, XH, 2 * M // XH, rows)
        gather = part.transpose(2, 1, 3, 0, 4).reshape(XH * Z, 2 * M // XH, XH * rows)
        out["to_" + name] = np.concatenate(split_hi_lo(gather), axis=1)
        inv = (coef * factor).reshape(XH, Z, XH, Z, 8, R)
        own = np.stack([np.stack([inv[a if q == 0 else 1 - a, :, a] for q in range(2)], axis=1) for a in range(XH)])
        wide = np.zeros((XH, Z, 2, 2, R, Z, 2, 8))
        for t2 in range(2):
            wide[:, :, :, t2, :, :, t2, :] = own.transpose(0, 1, 2, 5, 3, 4)
        wide = wide.reshape(XH * Z, 4 * R, 16 * Z)
        out["from_" + name] = np.concatenate(split_hi_lo(wide), axis=1)
    return out


def dot(left, right, dims):
    return lax.dot_general(left, right, dims, preferred_element_type=f32)


def call(kernel, out_shape, args, table=None, where=None, scratch=(), flops=0, name=None):
    def whole(shape):
        return pl.BlockSpec(shape, lambda i, w, n=len(shape): (0,) * n)

    outs = jax.tree.leaves(out_shape)
    in_specs = [whole(a.shape) for a in args]
    if table is not None:
        in_specs.append(pl.BlockSpec((1,) + table.shape[1:], lambda i, w: (w[0], 0, 0)))
        args = list(args) + [table]
    touched = sum(int(np.prod(a.shape)) * a.dtype.itemsize for a in list(args[: len(args)]) + outs)
    specs = jax.tree.map(lambda s: whole(s.shape), out_shape)
    return pl.pallas_call(
        kernel,
        out_shape=out_shape,
        grid_spec=pltpu.PrefetchScalarGridSpec(
            num_scalar_prefetch=1, grid=(1,), in_specs=in_specs, out_specs=specs, scratch_shapes=list(scratch)
        ),
        compiler_params=pltpu.CompilerParams(vmem_limit_bytes=VMEM_LIMIT),
        cost_estimate=pl.CostEstimate(flops=flops, bytes_accessed=touched, transcendentals=0),
        name=name,
    )(where, *args)


def points_kernel(w, x_ref, v_ref, y_ref):
    y = dot(v_ref[...], x_ref[...], NT)
    y_ref[...] = (y[:R] + y[R:]).astype(bf16)


def modes_kernel(w, y_ref, g_ref, out_ref):
    half = g_ref.shape[1] // 2
    for tt in range(8):
        part = dot(g_ref[0], y_ref[:, tt * 256 : (tt + 1) * 256], NN)
        part = part[:half] + part[half:]
        left = part[:, :128].reshape(Z, 8, 128)
        right = part[:, 128:].reshape(Z, 8, 128)
        out_ref[:, tt * 16 : (tt + 1) * 16, :] = jnp.concatenate([left, right], axis=1).astype(bf16)


def modes_bias_kernel(w, y_ref, g_ref, out_ref, bias_ref):
    modes_kernel(w, y_ref, g_ref, out_ref)
    first = y_ref[0:RB, 0:128].astype(f32)[R : R + 8]
    second = y_ref[RB : 2 * RB, 0:128].astype(f32)[R : R + 8]
    bias_ref[...] = first + second


def summed(ref):
    total = ref[0].astype(f32)
    for i in range(1, ref.shape[0]):
        total = total + ref[i].astype(f32)
    return total


def rows_of(scr, k, r):
    return scr[pl.ds(2 * k + r, 16, stride=8), :]


def gather_kernel(w, got_ref, out_ref, scr):
    scr[...] = summed(got_ref)
    blocks = []
    for k in range(4):
        re, im = rows_of(scr, k, 0), rows_of(scr, k, 1)
        blocks.append(jnp.concatenate([re[:, :64], im[:, :64]], axis=1))
        blocks.append(jnp.concatenate([re[:, 64:], im[:, 64:]], axis=1))
    send = jnp.concatenate(blocks, axis=0).astype(bf16)
    for i in range(out_ref.shape[0]):
        out_ref[i] = send


def put_rows(scr, k, r, block):
    scr[pl.ds(2 * k + r, 16, stride=8), :] = jnp.concatenate([block[:16], block[16:]], axis=1)


def mix_kernel(w, got_ref, weight_ref, out_ref, spec_ref, scr):
    for k in range(4):
        rows = slice(k * 32, (k + 1) * 32)
        re, im = [], []
        for q in range(8):
            one, two = got_ref[2 * q, rows, :], got_ref[2 * q + 1, rows, :]
            re.append(jnp.concatenate([one[:, :64], two[:, :64]], axis=1))
            im.append(jnp.concatenate([one[:, 64:], two[:, 64:]], axis=1))
        spec = jnp.concatenate([jnp.concatenate(re, axis=1), jnp.concatenate(im, axis=1)], axis=0)
        spec_ref[k] = spec
        out = dot(spec, weight_ref[k], NT)
        put_rows(scr, k, 0, out[:32, :64] - out[32:, 64:])
        put_rows(scr, k, 1, out[:32, 64:] + out[32:, :64])
    send = scr[...].astype(bf16)
    for i in range(out_ref.shape[0]):
        out_ref[i] = send


def window_sums(got, d_ref, own_ref, other_ref, tt):
    out = dot(d_ref[0], got, NN)
    out = out[: 4 * R] + out[4 * R :]
    lanes = slice(tt * 256, (tt + 1) * 256)
    own_ref[:, lanes] = jnp.concatenate([out[:R], out[R : 2 * R]], axis=1)
    return jnp.concatenate([out[2 * R : 3 * R], out[3 * R :]], axis=1)


def windows_kernel(w, got_ref, d_ref, own_ref, other_ref):
    for tt in range(8):
        got = got_ref[:, tt * 16 : (tt + 1) * 16, :].reshape(16 * Z, 128)
        other = window_sums(got, d_ref, own_ref, other_ref, tt)
        other_ref[:, tt * 256 : (tt + 1) * 256] = other.astype(bf16)


def hi_lo_rows(row):
    hi = row.astype(bf16).astype(f32)
    return jnp.concatenate([hi, (row - hi).astype(bf16).astype(f32)], axis=1)


def windows_bias_kernel(w, got_ref, d_ref, own_ref, other_ref, bias_ref):
    total = jnp.zeros((16, 128), f32)
    for i in range(Z):
        total = total + got_ref[i, 128:144, :].astype(f32)
    bias_ref[...] = total[:8]
    for tt in range(8):
        got = got_ref[:, tt * 16 : (tt + 1) * 16, :].reshape(16 * Z, 128)
        other = window_sums(got, d_ref, own_ref, other_ref, tt)
        other_ref[:, tt * 256 : (tt + 1) * 256] = other.astype(bf16)


def expanded(own_ref, other_ref, e_ref, tt):
    lanes = slice(tt * 256, (tt + 1) * 256)
    coef = own_ref[:, lanes] + other_ref[:, lanes].astype(f32)
    hi = coef.astype(bf16).astype(f32)
    stacked = jnp.concatenate([hi, hi, coef - hi], axis=0).astype(bf16)
    field = dot(stacked, e_ref[...], TN)
    return field.astype(bf16).astype(f32).reshape(4, 64, WIN)


def pointwise_kernel(w, own_ref, other_ref, cot_ref, bias_ref, e_ref, v_ref, y_ref):
    root = math.sqrt(2.0 / math.pi)
    bias = bias_ref[...][None]
    total = jnp.zeros((64, WIN), f32)
    for tt in range(8):
        v = expanded(own_ref, other_ref, e_ref, tt) + bias
        square = v * v
        th = jnp.tanh(root * (v + 0.044715 * (square * v)))
        slope = 0.5 * (1.0 + th) + (0.5 * root) * v * (1.0 - th * th) * (1.0 + (3.0 * 0.044715) * square)
        grad = slope * cot_ref[tt * 4 : (tt + 1) * 4].astype(f32)
        total = total + jnp.sum(grad, axis=0)
        y = dot(v_ref[...], grad.astype(bf16).reshape(256, WIN), NT)
        y = y[:R] + y[R:]
        y = jnp.concatenate([y, jnp.zeros((RB - R, 256), f32)], axis=0)
        y_ref[:, tt * 256 : (tt + 1) * 256] = y.astype(bf16)
    sums = lax.dot_general(
        jnp.ones((8, WIN), f32), total, NT, precision=lax.Precision.HIGHEST, preferred_element_type=f32
    )
    sums = hi_lo_rows(sums)
    y = y_ref[:, 0:128].astype(f32)
    y_ref[:, 0:128] = jnp.concatenate([y[:R], sums], axis=0).astype(bf16)


def back_kernel(w, got_ref, weight_ref, out_ref, grad_ref, scr):
    scr[...] = summed(got_ref).astype(bf16).astype(f32)
    for k in range(4):
        re, im = rows_of(scr, k, 0), rows_of(scr, k, 1)
        re = jnp.concatenate([re[:, :64], re[:, 64:]], axis=0)
        im = jnp.concatenate([im[:, :64], im[:, 64:]], axis=0)
        top = jnp.concatenate([re, im], axis=1)
        low = jnp.concatenate([im, -re], axis=1)
        grad = jnp.concatenate([top, low], axis=0).astype(bf16)
        grad_ref[k] = grad
        out = dot(grad, weight_ref[k], NN).astype(bf16)
        rows = slice(k * 32, (k + 1) * 32)
        for q in range(8):
            re, im = out[:32, q * 128 : (q + 1) * 128], out[32:, q * 128 : (q + 1) * 128]
            out_ref[2 * q, rows, :] = jnp.concatenate([re[:, :64], im[:, :64]], axis=1)
            out_ref[2 * q + 1, rows, :] = jnp.concatenate([re[:, 64:], im[:, 64:]], axis=1)


def weight_kernel(w, grad_ref, spec_ref, out_ref):
    for k in range(4):
        out_ref[k] = dot(grad_ref[k], spec_ref[k], TN)


def collect_kernel(w, got_ref, bias_ref, out_ref, scr):
    total = summed(got_ref)
    for k in range(4):
        block = total[k * 32 : (k + 1) * 32]
        put_rows(scr, k, 0, block[:, :64])
        put_rows(scr, k, 1, block[:, 64:])
    send = scr[...].astype(bf16)
    bias = bias_ref[...]
    bias = hi_lo_rows(bias[:, :64] + bias[:, 64:])
    tail = jnp.concatenate([bias, jnp.zeros((8, 128), f32)], axis=0).astype(bf16)
    for i in range(out_ref.shape[0]):
        out_ref[i, 0:128, :] = send
        out_ref[i, 128:144, :] = tail


def finish_kernel(w, own_ref, other_ref, cot_ref, e_ref, out_ref):
    for tt in range(8):
        field = expanded(own_ref, other_ref, e_ref, tt)
        rows = slice(tt * 4, (tt + 1) * 4)
        out_ref[rows] = (cot_ref[rows].astype(f32) + field).astype(bf16)


def exchange(blocks, axis):
    return lax.all_to_all(blocks, axis, split_axis=0, concat_axis=0, tiled=True)


def body(activation, cotangent, spectral_weight, out_bias):
    table = tables()
    where = jnp.reshape(lax.axis_index("xh") * Z + lax.axis_index("z"), (1,)).astype(jnp.int32)
    const = {name: jnp.asarray(value) for name, value in table.items()}
    shape = jax.ShapeDtypeStruct
    run = functools.partial(call, where=where)
    swap = [(0, 1), (1, 0)]
    chan = lax.axis_size("chan")
    span, width = activation.shape[0], activation.shape[1]
    lanes = span * width
    weight = spectral_weight.reshape(4, 2 * width, spectral_weight.shape[3])
    bias_wide = jnp.broadcast_to(out_bias[:, None], (width, WIN))
    square = pltpu.VMEM((128, 128), f32)
    block = shape((Z, 128, 128), bf16)

    coefs = run(points_kernel, shape((R, lanes), bf16), [activation.reshape(lanes, WIN), const["points"]], name="points")
    coefs = lax.all_gather(coefs, "xh", axis=0, tiled=True)
    parts = run(modes_kernel, block, [coefs], const["to_plain"], flops=2 * 256 * 64 * lanes, name="modes")
    parts = exchange(parts, "z")
    spectra = run(gather_kernel, shape((chan, 128, 128), bf16), [parts], scratch=[square], name="gather")
    spectra = exchange(spectra, "chan")
    mixed, spec = run(
        mix_kernel,
        (block, shape((4, 64, weight.shape[2]), bf16)),
        [spectra, weight],
        scratch=[square],
        flops=2 * 4 * 64 * 128 * weight.shape[2],
        name="mix",
    )
    mixed = exchange(mixed, "z")
    pair = (shape((R, lanes), f32), shape((R, lanes), bf16))
    own, other = run(windows_kernel, pair, [mixed], const["from_doubled"], name="windows")
    other = lax.ppermute(other, "xh", swap)
    coefs = run(
        pointwise_kernel,
        shape((RB, lanes), bf16),
        [own, other, cotangent, bias_wide, const["expand"], const["points"]],
        name="pointwise",
    )
    coefs = lax.all_gather(coefs, "xh", axis=0, tiled=True)
    parts, bias_pair = run(modes_bias_kernel, (block, shape((8, 128), f32)), [coefs], const["to_doubled"], name="modes_back")
    parts = exchange(parts, "z")
    back, grad = run(
        back_kernel,
        (shape((chan, 128, 128), bf16), shape((4, 64, 128), bf16)),
        [parts, weight],
        scratch=[square],
        name="back",
    )
    back = exchange(back, "chan")
    grad_weight = run(
        weight_kernel,
        shape((4, 2 * width, weight.shape[2]), f32),
        [grad, spec],
        flops=2 * 4 * 64 * 128 * weight.shape[2],
        name="weight",
    )
    sums = run(collect_kernel, shape((Z, 144, 128), bf16), [back, bias_pair], scratch=[square], name="collect")
    sums = exchange(sums, "z")
    own, other, bias_sum = run(
        windows_bias_kernel, pair + (shape((8, 128), f32),), [sums], const["from_plain"], name="windows_back"
    )
    other = lax.ppermute(other, "xh", swap)
    grad_input = run(
        finish_kernel, shape(activation.shape, bf16), [own, other, cotangent, const["expand"]], name="finish"
    )
    grad_bias = bias_sum[0, :width] + bias_sum[0, width:]
    return grad_input, grad_weight.reshape(spectral_weight.shape), grad_bias


def solution(mesh):
    fine = Mesh(mesh.devices.reshape(XH, Z, -1), ("xh", "z", "chan"))
    pitch = ("xh", "z")
    field = P(None, "chan", pitch)
    modes = P(pitch, None, "chan", None)
    return jax.shard_map(
        body,
        mesh=fine,
        in_specs=(field, field, modes, P("chan")),
        out_specs=(field, modes, P("chan")),
        check_vma=False,
    )
```

```python
import functools
import math

import jax
import jax.numpy as jnp
import ml_dtypes
import numpy as np
from jax import lax
from jax.experimental import pallas as pl
from jax.experimental.pallas import tpu as pltpu
from jax.sharding import PartitionSpec as P

P_SIZE = 4096
M = 128
PITCH = 32
WIN = P_SIZE // PITCH
KEPT = M // PITCH
R = 32
f32 = jnp.float32
bf16 = jnp.bfloat16
NT = (((1,), (1,)), ((), ()))
NN = (((1,), (0,)), ((), ()))
TN = (((0,), (0,)), ((), ()))
VMEM_LIMIT = 32 * 1024 * 1024


def split_hi_lo(table):
    hi = table.astype(ml_dtypes.bfloat16)
    lo = (table - hi.astype(np.float64)).astype(ml_dtypes.bfloat16)
    return hi, lo


@functools.cache
def tables():
    modes = np.arange(M)
    angle = 2.0 * math.pi * (np.outer(modes, np.arange(P_SIZE)) % P_SIZE) / P_SIZE
    forward = np.stack([np.cos(angle), -np.sin(angle)]) / math.sqrt(P_SIZE)
    doubled = forward * np.where(modes == 0, 1.0, 2.0)[:, None]
    basis = np.linalg.svd(forward[:, :, :WIN].reshape(2 * M, WIN))[2][:R]
    coef = np.einsum("akwp,xp->akwx", forward.reshape(2, M, PITCH, WIN), basis)
    coef = coef.reshape(2 * M, PITCH, 2, R // 2)
    out = {}
    hi, lo = split_hi_lo(basis)
    out["points"] = np.concatenate([hi, lo], axis=0)
    gather = coef.transpose(2, 0, 1, 3).reshape(2, 2 * M, PITCH * R // 2)
    out["modes"] = np.stack(split_hi_lo(gather), axis=1).reshape(8 * M, PITCH * R // 2)
    spread = coef.transpose(2, 1, 3, 0).reshape(PITCH * R, 2 * M)
    out["windows"] = np.concatenate(split_hi_lo(spread), axis=0)
    whole = doubled.reshape(2, PITCH, KEPT, P_SIZE).transpose(0, 2, 1, 3).reshape(2 * M, P_SIZE)
    out["doubled"] = np.stack(split_hi_lo(whole))
    return out


def dot(left, right, dims):
    return lax.dot_general(left, right, dims, preferred_element_type=f32)


def run(kernel, out_shape, *args, scratch=(), flops=0, name=None):
    touched = sum(int(np.prod(a.shape)) * a.dtype.itemsize for a in list(args) + jax.tree.leaves(out_shape))
    return pl.pallas_call(
        kernel,
        out_shape=out_shape,
        scratch_shapes=list(scratch),
        compiler_params=pltpu.CompilerParams(vmem_limit_bytes=VMEM_LIMIT),
        cost_estimate=pl.CostEstimate(flops=flops, bytes_accessed=touched, transcendentals=0),
        name=name,
    )(*args)


def halves(left, right):
    return (
        jnp.concatenate([left[:, :64], right[:, :64]], axis=1),
        jnp.concatenate([left[:, 64:], right[:, 64:]], axis=1),
    )


def points_kernel(x_ref, v_ref, out_ref):
    for t in range(16):
        field = x_ref[2 * t : 2 * t + 2].reshape(128, WIN)
        y = dot(v_ref[...], field, NT)
        y = y[:R] + y[R:]
        first, second = halves(y[:16], y[16:])
        out_ref[t * 32 : (t + 1) * 32, :] = jnp.concatenate([first, second], axis=0).astype(bf16)


def modes_kernel(got_ref, g_ref, out_ref):
    part = dot(g_ref[...], got_ref[...], NN)
    part = part[: 4 * M, :64] + part[4 * M :, 64:]
    part = part[: 2 * M] + part[2 * M :]
    out_ref[...] = jnp.concatenate([part[:M], part[M:]], axis=1).astype(bf16)


def by_mode(scr, value, count):
    scr[...] = value
    return [scr[pl.ds(k, PITCH, stride=count), :] for k in range(KEPT)]


def gather_kernel(got_ref, out_ref, scr):
    send = jnp.concatenate(by_mode(scr, got_ref[...].astype(f32), KEPT), axis=0).astype(bf16)
    for i in range(out_ref.shape[0]):
        out_ref[i] = send


def mix_kernel(got_ref, weight_ref, out_ref, spec_ref, scr):
    for k in range(KEPT):
        rows = slice(k * PITCH, (k + 1) * PITCH)
        re, im = [], []
        for q in range(got_ref.shape[0] // 2):
            first, second = halves(got_ref[2 * q, rows, :], got_ref[2 * q + 1, rows, :])
            re.append(first)
            im.append(second)
        spec = jnp.concatenate([jnp.concatenate(re, axis=1), jnp.concatenate(im, axis=1)], axis=0)
        spec_ref[k] = spec
        out = dot(spec, weight_ref[k], NT)
        real = out[:32, :64] - out[32:, 64:]
        imag = out[:32, 64:] + out[32:, :64]
        scr[pl.ds(k, PITCH, stride=KEPT), :] = jnp.concatenate([real, imag], axis=1)
    out_ref[...] = scr[...].astype(bf16)


def pointwise_kernel(got_ref, cot_ref, bias_ref, table_ref, out_ref, scr, send):
    root = math.sqrt(2.0 / math.pi)
    mixed = jnp.concatenate(by_mode(scr, got_ref[...].astype(f32), KEPT), axis=0)
    mixed = mixed.T
    mixed = jnp.concatenate([mixed[:64], mixed[64:]], axis=1).astype(bf16)
    bias = bias_ref[...]
    total = jnp.zeros((64, WIN), f32)
    modes = jnp.zeros((2 * M, 64), f32)
    for chunk in range(8):
        lanes = slice(chunk * 512, (chunk + 1) * 512)
        high, low = table_ref[0, :, lanes], table_ref[1, :, lanes]
        response = (dot(mixed, high, NN) + dot(mixed, low, NN)).astype(bf16).astype(f32)
        grads = []
        for i in range(4):
            v = response[:, i * WIN : (i + 1) * WIN] + bias
            square = v * v
            th = jnp.tanh(root * (v + 0.044715 * (square * v)))
            slope = 0.5 * (1.0 + th) + (0.5 * root) * v * (1.0 - th * th) * (1.0 + (3.0 * 0.044715) * square)
            grad = slope * cot_ref[chunk * 4 + i].astype(f32)
            total = total + grad
            grads.append(grad.astype(bf16))
        grads = jnp.concatenate(grads, axis=1)
        modes = modes + dot(high, grads, NT) + dot(low, grads, NT)
    sums = lax.dot_general(
        jnp.ones((8, WIN), f32), total, NT, precision=lax.Precision.HIGHEST, preferred_element_type=f32
    )
    high = sums.astype(bf16).astype(f32)
    sums = jnp.concatenate([high, sums - high], axis=1)
    modes = jnp.concatenate([modes[:M], modes[M:]], axis=1)
    for k in range(KEPT):
        send[pl.ds(k, PITCH, stride=8), :] = modes[k * PITCH : (k + 1) * PITCH]
    send[pl.ds(KEPT, PITCH, stride=8), :] = jnp.concatenate([sums] * (PITCH // 8), axis=0)
    for k in range(KEPT + 1, 8):
        send[pl.ds(k, PITCH, stride=8), :] = jnp.zeros((PITCH, 128), f32)
    out_ref[...] = send[...].astype(bf16)


def back_kernel(got_ref, weight_ref, out_ref, grad_ref, bias_ref, scr):
    blocks = by_mode(scr, got_ref[...].astype(f32), 8)
    sums = jnp.sum(scr[pl.ds(KEPT, PITCH, stride=8), :], axis=0, keepdims=True)
    bias_ref[...] = jnp.broadcast_to(sums[:, :64] + sums[:, 64:], (8, 64))
    for k in range(KEPT):
        top = blocks[k]
        low = jnp.concatenate([top[:, 64:], -top[:, :64]], axis=1)
        grad = jnp.concatenate([top, low], axis=0).astype(bf16)
        grad_ref[k] = grad
        out = dot(grad, weight_ref[k], NN)
        rows = slice(k * PITCH, (k + 1) * PITCH)
        for q in range(out_ref.shape[0] // 2):
            lanes = slice(q * 128, (q + 1) * 128)
            first, second = halves(out[:32, lanes], out[32:, lanes])
            out_ref[2 * q, rows, :] = first.astype(bf16)
            out_ref[2 * q + 1, rows, :] = second.astype(bf16)


def weight_kernel(grad_ref, spec_ref, out_ref):
    for k in range(KEPT):
        out_ref[k] = dot(grad_ref[k], spec_ref[k], TN)


def collect_kernel(got_ref, out_ref, scr):
    total = got_ref[0].astype(f32)
    for i in range(1, got_ref.shape[0]):
        total = total + got_ref[i].astype(f32)
    for k in range(KEPT):
        scr[pl.ds(k, PITCH, stride=KEPT), :] = total[k * PITCH : (k + 1) * PITCH]
    out_ref[...] = scr[...].astype(bf16)


def windows_kernel(got_ref, u_ref, out_ref):
    got = jnp.concatenate([got_ref[:, :64], got_ref[:, 64:]], axis=0)
    out = dot(u_ref[...], got, NN)
    half = PITCH * R
    out = out[:half] + out[half:]
    out_ref[...] = jnp.concatenate([out[: half // 2], out[half // 2 :]], axis=1).astype(bf16)


def finish_kernel(got_ref, cot_ref, v_ref, out_ref):
    for t in range(16):
        low, high = halves(got_ref[t * 32 : t * 32 + 16, :], got_ref[t * 32 + 16 : t * 32 + 32, :])
        coef = jnp.concatenate([low, high, low, high], axis=0)
        field = dot(coef, v_ref[...], TN).astype(bf16).astype(f32).reshape(2, 64, WIN)
        rows = slice(2 * t, 2 * t + 2)
        out_ref[rows] = (cot_ref[rows].astype(f32) + field).astype(bf16)


def exchange(blocks, axis):
    return lax.all_to_all(blocks, axis, split_axis=0, concat_axis=0, tiled=True)


def body(activation, cotangent, spectral_weight, out_bias):
    const = {name: jnp.asarray(value) for name, value in tables().items()}
    shape = jax.ShapeDtypeStruct
    chan = lax.axis_size("chan")
    width = activation.shape[1]
    inputs = spectral_weight.shape[3]
    weight = spectral_weight.reshape(KEPT, 2 * width, inputs)
    bias_wide = jnp.broadcast_to(out_bias[:, None], (width, WIN))
    square = pltpu.VMEM((M, 128), f32)
    tall = pltpu.VMEM((2 * M, 128), f32)
    small = shape((M, 128), bf16)
    coefs_shape = shape((PITCH * R // 2, 128), bf16)
    across = shape((chan, M, 128), bf16)
    mix_flops = 2 * KEPT * 64 * 128 * inputs

    coefs = run(points_kernel, coefs_shape, activation, const["points"], name="points")
    coefs = exchange(coefs, "pitch")
    span_cotangent = exchange(cotangent, "pitch")
    spectra = run(modes_kernel, small, coefs, const["modes"], name="modes")
    spectra = exchange(spectra, "pitch")
    spectra = run(gather_kernel, across, spectra, scratch=[square], name="gather")
    spectra = exchange(spectra, "chan")
    mixed, spec = run(
        mix_kernel,
        (small, shape((KEPT, 64, inputs), bf16)),
        spectra,
        weight,
        scratch=[square],
        flops=mix_flops,
        name="mix",
    )
    mixed = exchange(mixed, "pitch")
    grads = run(
        pointwise_kernel,
        shape((2 * M, 128), bf16),
        mixed,
        span_cotangent,
        bias_wide,
        const["doubled"],
        scratch=[square, tall],
        name="pointwise",
    )
    grads = exchange(grads, "pitch")
    back, grad, bias = run(
        back_kernel,
        (across, shape((KEPT, 64, 128), bf16), shape((8, 64), f32)),
        grads,
        weight,
        scratch=[tall],
        flops=mix_flops,
        name="back",
    )
    back = exchange(back, "chan")
    grad_weight = run(
        weight_kernel, shape((KEPT, 2 * width, inputs), f32), grad, spec, flops=mix_flops, name="weight"
    )
    back = run(collect_kernel, small, back, scratch=[square], name="collect")
    back = exchange(back, "pitch")
    coefs = run(windows_kernel, coefs_shape, back, const["windows"], name="windows")
    coefs = exchange(coefs, "pitch")
    grad_input = run(
        finish_kernel, shape(activation.shape, bf16), coefs, cotangent, const["points"], name="finish"
    )
    return grad_input, grad_weight.reshape(spectral_weight.shape), bias[0]


def solution(mesh):
    field = P(None, "chan", "pitch")
    modes = P("pitch", None, "chan", None)
    return jax.shard_map(
        body,
        mesh=mesh,
        in_specs=(field, field, modes, P("chan")),
        out_specs=(field, modes, P("chan")),
        check_vma=False,
    )
```

```python
import functools
import math

import jax
import jax.numpy as jnp
import ml_dtypes
import numpy as np
from jax import lax
from jax.experimental import pallas as pl
from jax.experimental.pallas import tpu as pltpu
from jax.sharding import PartitionSpec as P

P_SIZE = 4096
M = 128
PITCH = 32
WIN = P_SIZE // PITCH
KEPT = M // PITCH
R = 32
f32 = jnp.float32
bf16 = jnp.bfloat16
NT = (((1,), (1,)), ((), ()))
NN = (((1,), (0,)), ((), ()))
TN = (((0,), (0,)), ((), ()))
VMEM_LIMIT = 32 * 1024 * 1024
FIRST_LIMIT = 60 * 1024 * 1024


def split_hi_lo(table):
    hi = table.astype(ml_dtypes.bfloat16)
    lo = (table - hi.astype(np.float64)).astype(ml_dtypes.bfloat16)
    return hi, lo


@functools.cache
def tables():
    modes = np.arange(M)
    angle = 2.0 * math.pi * (np.outer(modes, np.arange(P_SIZE)) % P_SIZE) / P_SIZE
    forward = np.stack([np.cos(angle), -np.sin(angle)]) / math.sqrt(P_SIZE)
    basis = np.linalg.svd(forward[:, :, :WIN].reshape(2 * M, WIN))[2][:R]
    coef = np.einsum("akwp,xp->akwx", forward.reshape(2, M, PITCH, WIN), basis)
    coef = coef.reshape(2 * M, PITCH, 2, R // 2)
    out = {}
    hi, lo = split_hi_lo(basis)
    out["points"] = np.concatenate([hi, lo], axis=0)
    gather = coef.transpose(2, 0, 1, 3).reshape(2, 2 * M, PITCH * R // 2)
    out["modes"] = np.stack(split_hi_lo(gather), axis=1).reshape(8 * M, PITCH * R // 2)
    spread = coef.transpose(2, 1, 3, 0).reshape(PITCH * R, 2 * M)
    out["windows"] = np.concatenate(split_hi_lo(spread), axis=0)
    scale = np.where(modes == 0, 1.0, 2.0).reshape(1, PITCH, KEPT, 1)
    scaled = coef.reshape(2, PITCH, KEPT, PITCH * R) * scale
    out["doubled"] = np.stack(split_hi_lo(scaled.transpose(0, 2, 1, 3).reshape(2 * M, PITCH * R)))
    high, low = split_hi_lo(np.kron(np.eye(4), basis))
    out["expand"] = np.concatenate([high, high, low], axis=0)
    return out


def dot(left, right, dims):
    return lax.dot_general(left, right, dims, preferred_element_type=f32)


def run(kernel, out_shape, *args, scratch=(), flops=0, name=None, far=0, vmem=VMEM_LIMIT):
    near = [pl.BlockSpec(memory_space=pltpu.VMEM)] * (len(args) - far)
    touched = sum(int(np.prod(a.shape)) * a.dtype.itemsize for a in list(args) + jax.tree.leaves(out_shape))
    return pl.pallas_call(
        kernel,
        out_shape=out_shape,
        in_specs=near + [pl.BlockSpec(memory_space=pltpu.HBM)] * far,
        scratch_shapes=list(scratch),
        compiler_params=pltpu.CompilerParams(vmem_limit_bytes=vmem),
        cost_estimate=pl.CostEstimate(flops=flops, bytes_accessed=touched, transcendentals=0),
        name=name,
    )(*args)


def halves(left, right):
    return (
        jnp.concatenate([left[:, :64], right[:, :64]], axis=1),
        jnp.concatenate([left[:, 64:], right[:, 64:]], axis=1),
    )


def points_kernel(v_ref, x_ref, cot_ref, out_ref, field, sems):
    cot_copy = pltpu.make_async_copy(cot_ref, out_ref.at[:, R // 2 :, :], sems.at[4])
    copies = [
        pltpu.make_async_copy(x_ref.at[8 * i : 8 * i + 8], field.at[8 * i : 8 * i + 8], sems.at[i]) for i in range(4)
    ]
    for copy in copies:
        copy.start()
    cot_copy.start()
    for t in range(16):
        if t % 4 == 0:
            copies[t // 4].wait()
        y = dot(v_ref[...], field[2 * t : 2 * t + 2].reshape(128, WIN), NT)
        y = y[:R] + y[R:]
        first, second = halves(y[:16], y[16:])
        out_ref[2 * t, 0:16, :] = first.astype(bf16)
        out_ref[2 * t + 1, 0:16, :] = second.astype(bf16)
    cot_copy.wait()


def modes_kernel(got_ref, g_ref, out_ref):
    got = got_ref[:, 0 : R // 2, :].reshape(PITCH * R // 2, 128)
    part = dot(g_ref[...], got, NN)
    part = part[: 4 * M, :64] + part[4 * M :, 64:]
    part = part[: 2 * M] + part[2 * M :]
    out_ref[...] = jnp.concatenate([part[:M], part[M:]], axis=1).astype(bf16)


def by_mode(scr, value, count):
    scr[...] = value
    return [scr[pl.ds(k, PITCH, stride=count), :] for k in range(KEPT)]


def gather_kernel(got_ref, out_ref, scr):
    send = jnp.concatenate(by_mode(scr, got_ref[...].astype(f32), KEPT), axis=0).astype(bf16)
    for i in range(out_ref.shape[0]):
        out_ref[i] = send


def mix_kernel(got_ref, weight_ref, out_ref, spec_ref, scr):
    for k in range(KEPT):
        rows = slice(k * PITCH, (k + 1) * PITCH)
        re, im = [], []
        for q in range(got_ref.shape[0] // 2):
            first, second = halves(got_ref[2 * q, rows, :], got_ref[2 * q + 1, rows, :])
            re.append(first)
            im.append(second)
        spec = jnp.concatenate([jnp.concatenate(re, axis=1), jnp.concatenate(im, axis=1)], axis=0)
        spec_ref[k] = spec
        out = dot(spec, weight_ref[k], NT)
        real = out[:32, :64] - out[32:, 64:]
        imag = out[:32, 64:] + out[32:, :64]
        scr[pl.ds(k, PITCH, stride=KEPT), :] = jnp.concatenate([real, imag], axis=1)
    out_ref[...] = scr[...].astype(bf16)


def pointwise_kernel(got_ref, cot_ref, bias_ref, table_ref, e_ref, out_ref, scr, send):
    root = math.sqrt(2.0 / math.pi)
    mixed = jnp.concatenate(by_mode(scr, got_ref[...].astype(f32), KEPT), axis=0)
    mixed = mixed.T
    mixed = jnp.concatenate([mixed[:64], mixed[64:]], axis=1).astype(bf16)
    bias = bias_ref[...]
    total = jnp.zeros((64, WIN), f32)
    high, low = table_ref[0], table_ref[1]
    coef = dot(mixed, high, NN) + dot(mixed, low, NN)
    ys = []
    for half in range(2):
        groups = range(4 * half, 4 * half + 4)
        part = jnp.concatenate([coef[:, g * 128 : (g + 1) * 128] for g in groups], axis=0)
        part_high = part.astype(bf16)
        part_low = (part - part_high.astype(f32)).astype(bf16)
        response = dot(jnp.concatenate([part_high, part_low, part_high], axis=1), e_ref[...], NN)
        response = response.astype(bf16).astype(f32)
        blocks = []
        for j, g in enumerate(groups):
            grads = []
            for i in range(4):
                v = response[j * 64 : (j + 1) * 64, i * WIN : (i + 1) * WIN] + bias
                square = v * v
                th = jnp.tanh(root * (v + 0.044715 * (square * v)))
                slope = 0.5 * (1.0 + th) + (0.5 * root) * v * (1.0 - th * th) * (1.0 + (3.0 * 0.044715) * square)
                grad = slope * cot_ref[4 * g + i, R // 2 :, :].astype(f32)
                total = total + grad
                grads.append(grad.astype(bf16))
            blocks.append(jnp.concatenate(grads, axis=1))
        y = dot(jnp.concatenate(blocks, axis=0), e_ref[128:, :], NT)
        y = y[:, :128] + y[:, 128:]
        ys += [y[j * 64 : (j + 1) * 64] for j in range(4)]
    y = jnp.concatenate(ys, axis=1)
    y_high = y.astype(bf16)
    y_low = (y - y_high.astype(f32)).astype(bf16)
    modes = dot(high, jnp.concatenate([y_high, y_low], axis=0), NT)
    modes = modes[:, :64] + modes[:, 64:] + dot(low, y_high, NT)
    sums = lax.dot_general(
        jnp.ones((8, WIN), f32), total, NT, precision=lax.Precision.HIGHEST, preferred_element_type=f32
    )
    rounded = sums.astype(bf16).astype(f32)
    sums = jnp.concatenate([rounded, sums - rounded], axis=1)
    modes = jnp.concatenate([modes[:M], modes[M:]], axis=1)
    for k in range(KEPT):
        send[pl.ds(k, PITCH, stride=8), :] = modes[k * PITCH : (k + 1) * PITCH]
    send[pl.ds(KEPT, PITCH, stride=8), :] = jnp.concatenate([sums] * (PITCH // 8), axis=0)
    for k in range(KEPT + 1, 8):
        send[pl.ds(k, PITCH, stride=8), :] = jnp.zeros((PITCH, 128), f32)
    out_ref[...] = send[...].astype(bf16)


def back_kernel(got_ref, weight_ref, out_ref, grad_ref, bias_ref, scr):
    blocks = by_mode(scr, got_ref[...].astype(f32), 8)
    sums = jnp.sum(scr[pl.ds(KEPT, PITCH, stride=8), :], axis=0, keepdims=True)
    bias_ref[...] = jnp.broadcast_to(sums[:, :64] + sums[:, 64:], (8, 64))
    for k in range(KEPT):
        top = blocks[k]
        low = jnp.concatenate([top[:, 64:], -top[:, :64]], axis=1)
        grad = jnp.concatenate([top, low], axis=0).astype(bf16)
        grad_ref[k] = grad
        out = dot(grad, weight_ref[k], NN)
        rows = slice(k * PITCH, (k + 1) * PITCH)
        for q in range(out_ref.shape[0] // 2):
            lanes = slice(q * 128, (q + 1) * 128)
            first, second = halves(out[:32, lanes], out[32:, lanes])
            out_ref[2 * q, rows, :] = first.astype(bf16)
            out_ref[2 * q + 1, rows, :] = second.astype(bf16)


def weight_kernel(grad_ref, spec_ref, out_ref):
    for k in range(KEPT):
        out_ref[k] = dot(grad_ref[k], spec_ref[k], TN)


def collect_kernel(got_ref, out_ref, scr):
    total = got_ref[0].astype(f32)
    for i in range(1, got_ref.shape[0]):
        total = total + got_ref[i].astype(f32)
    for k in range(KEPT):
        scr[pl.ds(k, PITCH, stride=KEPT), :] = total[k * PITCH : (k + 1) * PITCH]
    out_ref[...] = scr[...].astype(bf16)


def windows_kernel(got_ref, u_ref, out_ref):
    got = jnp.concatenate([got_ref[:, :64], got_ref[:, 64:]], axis=0)
    out = dot(u_ref[...], got, NN)
    half = PITCH * R
    out = out[:half] + out[half:]
    out_ref[...] = jnp.concatenate([out[: half // 2], out[half // 2 :]], axis=1).astype(bf16)


def finish_kernel(got_ref, cot_ref, v_ref, out_ref):
    for t in range(16):
        low, high = halves(got_ref[t * 32 : t * 32 + 16, :], got_ref[t * 32 + 16 : t * 32 + 32, :])
        coef = jnp.concatenate([low, high, low, high], axis=0)
        field = dot(coef, v_ref[...], TN).astype(bf16).astype(f32).reshape(2, 64, WIN)
        rows = slice(2 * t, 2 * t + 2)
        out_ref[rows] = (cot_ref[rows].astype(f32) + field).astype(bf16)


def exchange(blocks, axis):
    return lax.all_to_all(blocks, axis, split_axis=0, concat_axis=0, tiled=True)


def body(activation, cotangent, spectral_weight, out_bias):
    const = {name: jnp.asarray(value) for name, value in tables().items()}
    shape = jax.ShapeDtypeStruct
    chan = lax.axis_size("chan")
    width = activation.shape[1]
    inputs = spectral_weight.shape[3]
    weight = spectral_weight.reshape(KEPT, 2 * width, inputs)
    bias_wide = jnp.broadcast_to(out_bias[:, None], (width, WIN))
    square = pltpu.VMEM((M, 128), f32)
    tall = pltpu.VMEM((2 * M, 128), f32)
    small = shape((M, 128), bf16)
    coefs_shape = shape((PITCH * R // 2, 128), bf16)
    across = shape((chan, M, 128), bf16)
    mix_flops = 2 * KEPT * 64 * 128 * inputs

    first = run(
        points_kernel,
        shape((PITCH, R // 2 + width, 128), bf16),
        const["points"],
        activation,
        cotangent,
        scratch=[pltpu.VMEM(activation.shape, bf16), pltpu.SemaphoreType.DMA((5,))],
        far=2,
        vmem=FIRST_LIMIT,
        name="points",
    )
    first = exchange(first, "pitch")
    spectra = run(modes_kernel, small, first, const["modes"], name="modes")
    spectra = exchange(spectra, "pitch")
    spectra = run(gather_kernel, across, spectra, scratch=[square], name="gather")
    spectra = exchange(spectra, "chan")
    mixed, spec = run(
        mix_kernel,
        (small, shape((KEPT, 64, inputs), bf16)),
        spectra,
        weight,
        scratch=[square],
        flops=mix_flops,
        name="mix",
    )
    mixed = exchange(mixed, "pitch")
    grads = run(
        pointwise_kernel,
        shape((2 * M, 128), bf16),
        mixed,
        first,
        bias_wide,
        const["doubled"],
        const["expand"],
        scratch=[square, tall],
        name="pointwise",
    )
    grads = exchange(grads, "pitch")
    back, grad, bias = run(
        back_kernel,
        (across, shape((KEPT, 64, 128), bf16), shape((8, 64), f32)),
        grads,
        weight,
        scratch=[tall],
        flops=mix_flops,
        name="back",
    )
    back = exchange(back, "chan")
    grad_weight = run(
        weight_kernel, shape((KEPT, 2 * width, inputs), f32), grad, spec, flops=mix_flops, name="weight"
    )
    back = run(collect_kernel, small, back, scratch=[square], name="collect")
    back = exchange(back, "pitch")
    coefs = run(windows_kernel, coefs_shape, back, const["windows"], name="windows")
    coefs = exchange(coefs, "pitch")
    grad_input = run(
        finish_kernel, shape(activation.shape, bf16), coefs, cotangent, const["points"], name="finish"
    )
    return grad_input, grad_weight.reshape(spectral_weight.shape), bias[0]


def solution(mesh):
    field = P(None, "chan", "pitch")
    modes = P("pitch", None, "chan", None)
    return jax.shard_map(
        body,
        mesh=mesh,
        in_specs=(field, field, modes, P("chan")),
        out_specs=(field, modes, P("chan")),
        check_vma=False,
    )
```

```python
import functools
import math

import jax
import jax.numpy as jnp
import ml_dtypes
import numpy as np
from jax import lax
from jax.experimental import pallas as pl
from jax.experimental.pallas import tpu as pltpu
from jax.sharding import Mesh
from jax.sharding import PartitionSpec as P

P_SIZE = 4096
M = 128
XH = 2
Z = 16
PITCH = XH * Z
WIN = P_SIZE // PITCH
KEPT = M // PITCH
R = 32
PITCH_AXES = ("xh", "z")
f32 = jnp.float32
bf16 = jnp.bfloat16
NT = (((1,), (1,)), ((), ()))
NN = (((1,), (0,)), ((), ()))
TN = (((0,), (0,)), ((), ()))
VMEM_LIMIT = 32 * 1024 * 1024
FIRST_LIMIT = 60 * 1024 * 1024


def split_hi_lo(table):
    hi = table.astype(ml_dtypes.bfloat16)
    lo = (table - hi.astype(np.float64)).astype(ml_dtypes.bfloat16)
    return hi, lo


@functools.cache
def tables():
    modes = np.arange(M)
    angle = 2.0 * math.pi * (np.outer(modes, np.arange(P_SIZE)) % P_SIZE) / P_SIZE
    forward = np.stack([np.cos(angle), -np.sin(angle)]) / math.sqrt(P_SIZE)
    basis = np.linalg.svd(forward[:, :, :WIN].reshape(2 * M, WIN))[2][:R]
    coef = np.einsum("akwp,xp->akwx", forward.reshape(2, M, PITCH, WIN), basis)
    coef = coef.reshape(2 * M, PITCH, 2, R // 2)
    out = {}
    hi, lo = split_hi_lo(basis)
    out["points"] = np.concatenate([hi, lo], axis=0)
    by_z = coef.reshape(2, XH, Z, KEPT, PITCH, 2, R // 2).transpose(5, 0, 2, 1, 3, 4, 6)
    gather = by_z.reshape(2, 2 * M, PITCH * R // 2)
    out["modes"] = np.stack(split_hi_lo(gather), axis=1).reshape(8 * M, PITCH * R // 2)
    spread = coef.transpose(1, 3, 2, 0).reshape(PITCH * R // 2, 4 * M)
    out["windows"] = np.concatenate(split_hi_lo(spread), axis=0)
    scale = np.where(modes == 0, 1.0, 2.0).reshape(1, PITCH, KEPT, 1)
    scaled = coef.reshape(2, PITCH, KEPT, PITCH * R) * scale
    out["doubled"] = np.stack(split_hi_lo(scaled.transpose(0, 2, 1, 3).reshape(2 * M, PITCH * R)))
    high, low = split_hi_lo(np.kron(np.eye(4), basis))
    out["expand"] = np.concatenate([high, high, low], axis=0)
    return out


def dot(left, right, dims):
    return lax.dot_general(left, right, dims, preferred_element_type=f32)


def run(kernel, out_shape, *args, scratch=(), flops=0, name=None, far=0, far_out=False, vmem=VMEM_LIMIT):
    out_space = pltpu.HBM if far_out else pltpu.VMEM
    near = [pl.BlockSpec(memory_space=pltpu.VMEM)] * (len(args) - far)
    touched = sum(int(np.prod(a.shape)) * a.dtype.itemsize for a in list(args) + jax.tree.leaves(out_shape))
    return pl.pallas_call(
        kernel,
        out_shape=out_shape,
        in_specs=near + [pl.BlockSpec(memory_space=pltpu.HBM)] * far,
        out_specs=jax.tree.map(lambda _: pl.BlockSpec(memory_space=out_space), out_shape),
        scratch_shapes=list(scratch),
        compiler_params=pltpu.CompilerParams(vmem_limit_bytes=vmem),
        cost_estimate=pl.CostEstimate(flops=flops, bytes_accessed=touched, transcendentals=0),
        name=name,
    )(*args)


def halves(left, right):
    return (
        jnp.concatenate([left[:, :64], right[:, :64]], axis=1),
        jnp.concatenate([left[:, 64:], right[:, 64:]], axis=1),
    )


def points_kernel(v_ref, x_ref, cot_ref, out_ref, basis, field, coefs, sems):
    copies = [pltpu.make_async_copy(v_ref, basis, sems.at[12])]
    for i in range(4):
        part = slice(8 * i, 8 * i + 8)
        copies.append(pltpu.make_async_copy(x_ref.at[part], field.at[part], sems.at[i]))
    for i in range(4):
        part = slice(8 * i, 8 * i + 8)
        copies.append(pltpu.make_async_copy(cot_ref.at[part], out_ref.at[part, R // 2 :, :], sems.at[4 + i]))
    for copy in copies:
        copy.start()
    copies[0].wait()
    sends = []
    for i in range(4):
        copies[1 + i].wait()
        for t in range(4 * i, 4 * i + 4):
            y = dot(basis[...], field[2 * t : 2 * t + 2].reshape(128, WIN), NT)
            y = y[:R] + y[R:]
            first, second = halves(y[:16], y[16:])
            coefs[2 * t] = first.astype(bf16)
            coefs[2 * t + 1] = second.astype(bf16)
        part = slice(8 * i, 8 * i + 8)
        sends.append(pltpu.make_async_copy(coefs.at[part], out_ref.at[part, 0 : R // 2, :], sems.at[8 + i]))
        sends[i].start()
    for copy in sends + copies[5:]:
        copy.wait()


def modes_kernel(got_ref, g_ref, out_ref):
    got = got_ref[:, 0 : R // 2, :].reshape(PITCH * R // 2, 128)
    part = dot(g_ref[...], got, NN)
    part = part[: 4 * M, :64] + part[4 * M :, 64:]
    part = part[: 2 * M] + part[2 * M :]
    out_ref[...] = jnp.concatenate([part[:M], part[M:]], axis=1).astype(bf16)


def by_mode(scr, value, count):
    scr[...] = value
    return [scr[pl.ds(k, PITCH, stride=count), :] for k in range(KEPT)]


def gather_kernel(got_ref, out_ref, scr):
    scr[...] = got_ref[...].astype(f32)
    each = out_ref.shape[0] // XH
    for a in range(XH):
        rows = [scr[pl.ds(a * KEPT + k, Z, stride=XH * KEPT), :] for k in range(KEPT)]
        send = jnp.concatenate(rows, axis=0).astype(bf16)
        for i in range(each):
            out_ref[a * each + i] = send


def mix_kernel(got_ref, weight_ref, out_ref, spec_ref, scr):
    for k in range(KEPT):
        rows = slice(k * Z, (k + 1) * Z)
        chan = got_ref.shape[0] // XH
        re, im = [], []
        for q in range(chan // 2):
            left, right = [
                jnp.concatenate([got_ref[c, rows, :], got_ref[chan + c, rows, :]], axis=0) for c in (2 * q, 2 * q + 1)
            ]
            first, second = halves(left, right)
            re.append(first)
            im.append(second)
        spec = jnp.concatenate([jnp.concatenate(re, axis=1), jnp.concatenate(im, axis=1)], axis=0)
        spec_ref[k] = spec
        out = dot(spec, weight_ref[k], NT)
        real = out[:32, :64] - out[32:, 64:]
        imag = out[:32, 64:] + out[32:, :64]
        scr[pl.ds(k, PITCH, stride=KEPT), :] = jnp.concatenate([real, imag], axis=1)
    out_ref[...] = scr[...].astype(bf16)


def pointwise_kernel(got_ref, cot_ref, bias_ref, table_ref, e_ref, out_ref, scr, send):
    root = math.sqrt(2.0 / math.pi)
    mixed = jnp.concatenate(by_mode(scr, got_ref[...].astype(f32), KEPT), axis=0)
    mixed = mixed.T
    mixed = jnp.concatenate([mixed[:64], mixed[64:]], axis=1).astype(bf16)
    bias = bias_ref[...]
    total = jnp.zeros((64, WIN), f32)
    high, low = table_ref[0], table_ref[1]
    coef = dot(mixed, high, NN) + dot(mixed, low, NN)
    ys = []
    for half in range(2):
        groups = range(4 * half, 4 * half + 4)
        part = jnp.concatenate([coef[:, g * 128 : (g + 1) * 128] for g in groups], axis=0)
        part_high = part.astype(bf16)
        part_low = (part - part_high.astype(f32)).astype(bf16)
        response = dot(jnp.concatenate([part_high, part_low, part_high], axis=1), e_ref[...], NN)
        response = response.astype(bf16).astype(f32)
        blocks = []
        for j, g in enumerate(groups):
            grads = []
            for i in range(4):
                v = response[j * 64 : (j + 1) * 64, i * WIN : (i + 1) * WIN] + bias
                square = v * v
                th = jnp.tanh(root * (v + 0.044715 * (square * v)))
                slope = 0.5 * (1.0 + th) + (0.5 * root) * v * (1.0 - th * th) * (1.0 + (3.0 * 0.044715) * square)
                grad = slope * cot_ref[4 * g + i, R // 2 :, :].astype(f32)
                total = total + grad
                grads.append(grad.astype(bf16))
            blocks.append(jnp.concatenate(grads, axis=1))
        y = dot(jnp.concatenate(blocks, axis=0), e_ref[128:, :], NT)
        y = y[:, :128] + y[:, 128:]
        ys += [y[j * 64 : (j + 1) * 64] for j in range(4)]
    y = jnp.concatenate(ys, axis=1)
    y_high = y.astype(bf16)
    y_low = (y - y_high.astype(f32)).astype(bf16)
    modes = dot(high, jnp.concatenate([y_high, y_low], axis=0), NT)
    modes = modes[:, :64] + modes[:, 64:] + dot(low, y_high, NT)
    sums = lax.dot_general(
        jnp.ones((8, WIN), f32), total, NT, precision=lax.Precision.HIGHEST, preferred_element_type=f32
    )
    rounded = sums.astype(bf16).astype(f32)
    sums = jnp.concatenate([rounded, sums - rounded], axis=1)
    modes = jnp.concatenate([modes[:M], modes[M:]], axis=1)
    for k in range(KEPT):
        send[pl.ds(k, PITCH, stride=8), :] = modes[k * PITCH : (k + 1) * PITCH]
    send[pl.ds(KEPT, PITCH, stride=8), :] = jnp.concatenate([sums] * (PITCH // 8), axis=0)
    for k in range(KEPT + 1, 8):
        send[pl.ds(k, PITCH, stride=8), :] = jnp.zeros((PITCH, 128), f32)
    out_ref[...] = send[...].astype(bf16)


def back_kernel(got_ref, weight_ref, out_ref, grad_ref, bias_ref, scr):
    blocks = by_mode(scr, got_ref[...].astype(f32), 8)
    sums = jnp.sum(scr[pl.ds(KEPT, PITCH, stride=8), :], axis=0, keepdims=True)
    bias_ref[...] = jnp.broadcast_to(sums[:, :64] + sums[:, 64:], (8, 64))
    for k in range(KEPT):
        top = blocks[k]
        low = jnp.concatenate([top[:, 64:], -top[:, :64]], axis=1)
        grad = jnp.concatenate([top, low], axis=0).astype(bf16)
        grad_ref[k] = grad
        out = dot(grad, weight_ref[k], NN)
        rows = slice(k * PITCH, (k + 1) * PITCH)
        for q in range(out_ref.shape[0] // 2):
            lanes = slice(q * 128, (q + 1) * 128)
            first, second = halves(out[:32, lanes], out[32:, lanes])
            out_ref[2 * q, rows, :] = first.astype(bf16)
            out_ref[2 * q + 1, rows, :] = second.astype(bf16)


def weight_kernel(grad_ref, spec_ref, out_ref):
    for k in range(KEPT):
        out_ref[k] = dot(grad_ref[k], spec_ref[k], TN)


def collect_kernel(got_ref, out_ref, scr):
    total = got_ref[0].astype(f32)
    for i in range(1, got_ref.shape[0]):
        total = total + got_ref[i].astype(f32)
    for k in range(KEPT):
        scr[pl.ds(k, PITCH, stride=KEPT), :] = total[k * PITCH : (k + 1) * PITCH]
    out_ref[...] = scr[...].astype(bf16)


def windows_kernel(got_ref, u_ref, out_ref):
    got = got_ref[...]
    turned = jnp.concatenate([got[:, 64:], got[:, :64]], axis=1)
    low = lax.broadcasted_iota(jnp.int32, got.shape, 1) < 64
    none = jnp.zeros_like(got)
    parts = [
        jnp.where(low, got, none),
        jnp.where(low, turned, none),
        jnp.where(low, none, turned),
        jnp.where(low, none, got),
    ]
    out = dot(u_ref[...], jnp.concatenate(parts, axis=0), NN)
    half = out.shape[0] // 2
    out_ref[...] = (out[:half] + out[half:]).astype(bf16)


def finish_kernel(got_ref, cot_ref, v_ref, out_ref, field, sems):
    sends = []
    for t in range(16):
        low, high = halves(got_ref[t * 32 : t * 32 + 16, :], got_ref[t * 32 + 16 : t * 32 + 32, :])
        coef = jnp.concatenate([low, high, low, high], axis=0)
        part = dot(coef, v_ref[...], TN).astype(bf16).astype(f32).reshape(2, 64, WIN)
        rows = slice(2 * t, 2 * t + 2)
        field[rows] = (cot_ref[rows].astype(f32) + part).astype(bf16)
        if t % 4 == 3:
            done = slice(2 * t - 6, 2 * t + 2)
            sends.append(pltpu.make_async_copy(field.at[done], out_ref.at[done], sems.at[t // 4]))
            sends[-1].start()
    for send in sends:
        send.wait()


def exchange(blocks, axis):
    return lax.all_to_all(blocks, axis, split_axis=0, concat_axis=0, tiled=True)


def body(activation, cotangent, spectral_weight, out_bias):
    const = {name: jnp.asarray(value) for name, value in tables().items()}
    shape = jax.ShapeDtypeStruct
    chan = lax.axis_size("chan")
    width = activation.shape[1]
    inputs = spectral_weight.shape[3]
    weight = spectral_weight.reshape(KEPT, 2 * width, inputs)
    bias_wide = jnp.broadcast_to(out_bias[:, None], (width, WIN))
    square = pltpu.VMEM((M, 128), f32)
    tall = pltpu.VMEM((2 * M, 128), f32)
    small = shape((M, 128), bf16)
    coefs_shape = shape((PITCH * R // 2, 128), bf16)
    across = shape((chan, M, 128), bf16)
    mix_flops = 2 * KEPT * 64 * 128 * inputs

    first = run(
        points_kernel,
        shape((PITCH, R // 2 + width, 128), bf16),
        const["points"],
        activation,
        cotangent,
        scratch=[
            pltpu.VMEM((2 * R, WIN), bf16),
            pltpu.VMEM(activation.shape, bf16),
            pltpu.VMEM((PITCH, R // 2, 128), bf16),
            pltpu.SemaphoreType.DMA((13,)),
        ],
        far=3,
        far_out=True,
        vmem=FIRST_LIMIT,
        name="points",
    )
    first = exchange(first, PITCH_AXES)
    spectra = run(modes_kernel, small, first, const["modes"], name="modes")
    spectra = exchange(spectra, "z")
    spectra = run(gather_kernel, shape((XH * chan, M // XH, 128), bf16), spectra, scratch=[square], name="gather")
    spectra = exchange(spectra, ("xh", "chan"))
    mixed, spec = run(
        mix_kernel,
        (small, shape((KEPT, 64, inputs), bf16)),
        spectra,
        weight,
        scratch=[square],
        flops=mix_flops,
        name="mix",
    )
    mixed = exchange(mixed, PITCH_AXES)
    grads = run(
        pointwise_kernel,
        shape((2 * M, 128), bf16),
        mixed,
        first,
        bias_wide,
        const["doubled"],
        const["expand"],
        scratch=[square, tall],
        name="pointwise",
    )
    grads = exchange(grads, PITCH_AXES)
    back, grad, bias = run(
        back_kernel,
        (across, shape((KEPT, 64, 128), bf16), shape((8, 64), f32)),
        grads,
        weight,
        scratch=[tall],
        flops=mix_flops,
        name="back",
    )
    back = exchange(back, "chan")
    grad_weight = run(
        weight_kernel, shape((KEPT, 2 * width, inputs), f32), grad, spec, flops=mix_flops, name="weight"
    )
    back = run(collect_kernel, small, back, scratch=[square], name="collect")
    back = exchange(back, PITCH_AXES)
    coefs = run(windows_kernel, coefs_shape, back, const["windows"], name="windows")
    coefs = exchange(coefs, PITCH_AXES)
    grad_input = run(
        finish_kernel,
        shape(activation.shape, bf16),
        coefs,
        cotangent,
        const["points"],
        scratch=[pltpu.VMEM(activation.shape, bf16), pltpu.SemaphoreType.DMA((4,))],
        far_out=True,
        name="finish",
    )
    return grad_input, grad_weight.reshape(spectral_weight.shape), bias[0]


def solution(mesh):
    fine = Mesh(mesh.devices.reshape(XH, Z, -1), ("xh", "z", "chan"))
    field = P(None, "chan", ("xh", "z"))
    modes = P(("xh", "z"), None, "chan", None)
    return jax.shard_map(
        body,
        mesh=fine,
        in_specs=(field, field, modes, P("chan")),
        out_specs=(field, modes, P("chan")),
        check_vma=False,
    )
```

```python
import functools
import math

import jax
import jax.numpy as jnp
import ml_dtypes
import numpy as np
from jax import lax
from jax.experimental import pallas as pl
from jax.experimental.pallas import tpu as pltpu
from jax.sharding import Mesh
from jax.sharding import PartitionSpec as P

P_SIZE = 4096
M = 128
XH = 2
Z = 16
PITCH = XH * Z
WIN = P_SIZE // PITCH
KEPT = M // PITCH
EARLY = 32
R = 32
PITCH_AXES = ("xh", "z")
f32 = jnp.float32
bf16 = jnp.bfloat16
NT = (((1,), (1,)), ((), ()))
NN = (((1,), (0,)), ((), ()))
TN = (((0,), (0,)), ((), ()))
VMEM_LIMIT = 32 * 1024 * 1024
FIRST_LIMIT = 60 * 1024 * 1024


def split_hi_lo(table):
    hi = table.astype(ml_dtypes.bfloat16)
    lo = (table - hi.astype(np.float64)).astype(ml_dtypes.bfloat16)
    return hi, lo


@functools.cache
def tables():
    modes = np.arange(M)
    angle = 2.0 * math.pi * (np.outer(modes, np.arange(P_SIZE)) % P_SIZE) / P_SIZE
    forward = np.stack([np.cos(angle), -np.sin(angle)]) / math.sqrt(P_SIZE)
    basis = np.linalg.svd(forward[:, :, :WIN].reshape(2 * M, WIN))[2][:R]
    coef = np.einsum("akwp,xp->akwx", forward.reshape(2, M, PITCH, WIN), basis)
    coef = coef.reshape(2 * M, PITCH, 2, R // 2)
    out = {}
    hi, lo = split_hi_lo(basis)
    out["points"] = np.concatenate([hi, lo], axis=0)
    by_z = coef.reshape(2, XH, Z, KEPT, PITCH, 2, R // 2).transpose(5, 0, 2, 1, 3, 4, 6)
    gather = by_z.reshape(2, 2 * M, PITCH * R // 2)
    out["modes"] = np.stack(split_hi_lo(gather), axis=1).reshape(8 * M, PITCH * R // 2)
    spread = coef.transpose(1, 3, 2, 0).reshape(PITCH * R // 2, 4 * M)
    out["windows"] = np.concatenate(split_hi_lo(spread), axis=0)
    scale = np.where(modes == 0, 1.0, 2.0).reshape(1, PITCH, KEPT, 1)
    scaled = coef.reshape(2, PITCH, KEPT, PITCH * R) * scale
    out["doubled"] = np.stack(split_hi_lo(scaled.transpose(0, 2, 1, 3).reshape(2 * M, PITCH * R)))
    high, low = split_hi_lo(np.kron(np.eye(4), basis))
    out["expand"] = np.concatenate([high, high, low], axis=0)
    return out


def dot(left, right, dims):
    return lax.dot_general(left, right, dims, preferred_element_type=f32)


def run(kernel, out_shape, *args, scratch=(), flops=0, name=None, far=0, far_out=False, vmem=VMEM_LIMIT):
    out_space = pltpu.HBM if far_out else pltpu.VMEM
    near = [pl.BlockSpec(memory_space=pltpu.VMEM)] * (len(args) - far)
    touched = sum(int(np.prod(a.shape)) * a.dtype.itemsize for a in list(args) + jax.tree.leaves(out_shape))
    return pl.pallas_call(
        kernel,
        out_shape=out_shape,
        in_specs=near + [pl.BlockSpec(memory_space=pltpu.HBM)] * far,
        out_specs=jax.tree.map(lambda _: pl.BlockSpec(memory_space=out_space), out_shape),
        scratch_shapes=list(scratch),
        compiler_params=pltpu.CompilerParams(vmem_limit_bytes=vmem),
        cost_estimate=pl.CostEstimate(flops=flops, bytes_accessed=touched, transcendentals=0),
        name=name,
    )(*args)


def halves(left, right):
    return (
        jnp.concatenate([left[:, :64], right[:, :64]], axis=1),
        jnp.concatenate([left[:, 64:], right[:, 64:]], axis=1),
    )


def points_kernel(v_ref, x_ref, cot_ref, out_ref, basis, field, message, sems):
    table = pltpu.make_async_copy(v_ref, basis, sems.at[12])
    fields, cots, sends = [], [], []
    for i in range(4):
        part = slice(8 * i, 8 * i + 8)
        fields.append(pltpu.make_async_copy(x_ref.at[part], field.at[part], sems.at[i]))
        cots.append(
            pltpu.make_async_copy(cot_ref.at[part, 0:EARLY, :], message.at[part, R // 2 :, :], sems.at[4 + i])
        )
        sends.append(pltpu.make_async_copy(message.at[part], out_ref.at[part], sems.at[8 + i]))
    table.start()
    for i in range(4):
        fields[i].start()
        cots[i].start()
    table.wait()
    for i in range(4):
        fields[i].wait()
        for t in range(4 * i, 4 * i + 4):
            y = dot(basis[...], field[2 * t : 2 * t + 2].reshape(128, WIN), NT)
            y = y[:R] + y[R:]
            first, second = halves(y[:16], y[16:])
            message[2 * t, 0:16, :] = first.astype(bf16)
            message[2 * t + 1, 0:16, :] = second.astype(bf16)
        cots[i].wait()
        sends[i].start()
    for i in range(4):
        sends[i].wait()


def modes_kernel(got_ref, g_ref, out_ref):
    got = got_ref[:, 0 : R // 2, :].reshape(PITCH * R // 2, 128)
    part = dot(g_ref[...], got, NN)
    part = part[: 4 * M, :64] + part[4 * M :, 64:]
    part = part[: 2 * M] + part[2 * M :]
    out_ref[...] = jnp.concatenate([part[:M], part[M:]], axis=1).astype(bf16)


def by_mode(scr, value, count):
    scr[...] = value
    return [scr[pl.ds(k, PITCH, stride=count), :] for k in range(KEPT)]


def gather_kernel(got_ref, out_ref, scr):
    scr[...] = got_ref[...].astype(f32)
    each = out_ref.shape[0] // XH
    for a in range(XH):
        rows = [scr[pl.ds(a * KEPT + k, Z, stride=XH * KEPT), :] for k in range(KEPT)]
        send = jnp.concatenate(rows, axis=0).astype(bf16)
        for i in range(each):
            out_ref[a * each + i] = send


def mix_kernel(got_ref, weight_ref, cot_ref, out_ref, spec_ref, scr):
    late = cot_ref.shape[1] - EARLY
    scr[...] = jnp.zeros(scr.shape, f32)
    out_ref[:, 0:late, :] = cot_ref[:, EARLY:, :]
    for k in range(KEPT):
        rows = slice(k * Z, (k + 1) * Z)
        chan = got_ref.shape[0] // XH
        re, im = [], []
        for q in range(chan // 2):
            left, right = [
                jnp.concatenate([got_ref[c, rows, :], got_ref[chan + c, rows, :]], axis=0) for c in (2 * q, 2 * q + 1)
            ]
            first, second = halves(left, right)
            re.append(first)
            im.append(second)
        spec = jnp.concatenate([jnp.concatenate(re, axis=1), jnp.concatenate(im, axis=1)], axis=0)
        spec_ref[k] = spec
        out = dot(spec, weight_ref[k], NT)
        real = out[:32, :64] - out[32:, 64:]
        imag = out[:32, 64:] + out[32:, :64]
        scr[pl.ds(k, PITCH, stride=8), :] = jnp.concatenate([real, imag], axis=1)
    out_ref[:, late:, :] = scr[...].reshape(PITCH, 8, 128).astype(bf16)


def pointwise_kernel(got_ref, early_ref, bias_ref, table_ref, e_ref, out_ref, scr, send):
    root = math.sqrt(2.0 / math.pi)
    late = got_ref.shape[1] - 8
    modes = got_ref[:, late:, :].astype(f32).reshape(8 * PITCH, 128)
    mixed = jnp.concatenate(by_mode(scr, modes, 8), axis=0)
    mixed = mixed.T
    mixed = jnp.concatenate([mixed[:64], mixed[64:]], axis=1).astype(bf16)
    bias = bias_ref[...]
    total = jnp.zeros((64, WIN), f32)
    high, low = table_ref[0], table_ref[1]
    coef = dot(mixed, high, NN) + dot(mixed, low, NN)
    ys = []
    for half in range(2):
        groups = range(4 * half, 4 * half + 4)
        part = jnp.concatenate([coef[:, g * 128 : (g + 1) * 128] for g in groups], axis=0)
        part_high = part.astype(bf16)
        part_low = (part - part_high.astype(f32)).astype(bf16)
        response = dot(jnp.concatenate([part_high, part_low, part_high], axis=1), e_ref[...], NN)
        response = response.astype(bf16).astype(f32)
        blocks = []
        for j, g in enumerate(groups):
            grads = []
            for i in range(4):
                v = response[j * 64 : (j + 1) * 64, i * WIN : (i + 1) * WIN] + bias
                square = v * v
                th = jnp.tanh(root * (v + 0.044715 * (square * v)))
                slope = 0.5 * (1.0 + th) + (0.5 * root) * v * (1.0 - th * th) * (1.0 + (3.0 * 0.044715) * square)
                cot = [early_ref[4 * g + i, R // 2 :, :], got_ref[4 * g + i, 0:late, :]]
                grad = slope * jnp.concatenate(cot, axis=0).astype(f32)
                total = total + grad
                grads.append(grad.astype(bf16))
            blocks.append(jnp.concatenate(grads, axis=1))
        y = dot(jnp.concatenate(blocks, axis=0), e_ref[128:, :], NT)
        y = y[:, :128] + y[:, 128:]
        ys += [y[j * 64 : (j + 1) * 64] for j in range(4)]
    y = jnp.concatenate(ys, axis=1)
    y_high = y.astype(bf16)
    y_low = (y - y_high.astype(f32)).astype(bf16)
    modes = dot(high, jnp.concatenate([y_high, y_low], axis=0), NT)
    modes = modes[:, :64] + modes[:, 64:] + dot(low, y_high, NT)
    sums = lax.dot_general(
        jnp.ones((8, WIN), f32), total, NT, precision=lax.Precision.HIGHEST, preferred_element_type=f32
    )
    rounded = sums.astype(bf16).astype(f32)
    sums = jnp.concatenate([rounded, sums - rounded], axis=1)
    modes = jnp.concatenate([modes[:M], modes[M:]], axis=1)
    for k in range(KEPT):
        send[pl.ds(k, PITCH, stride=8), :] = modes[k * PITCH : (k + 1) * PITCH]
    send[pl.ds(KEPT, PITCH, stride=8), :] = jnp.concatenate([sums] * (PITCH // 8), axis=0)
    for k in range(KEPT + 1, 8):
        send[pl.ds(k, PITCH, stride=8), :] = jnp.zeros((PITCH, 128), f32)
    out_ref[...] = send[...].astype(bf16)


def back_kernel(got_ref, weight_ref, out_ref, grad_ref, bias_ref, scr):
    blocks = by_mode(scr, got_ref[...].astype(f32), 8)
    sums = jnp.sum(scr[pl.ds(KEPT, PITCH, stride=8), :], axis=0, keepdims=True)
    bias_ref[...] = jnp.broadcast_to(sums[:, :64] + sums[:, 64:], (8, 64))
    for k in range(KEPT):
        top = blocks[k]
        low = jnp.concatenate([top[:, 64:], -top[:, :64]], axis=1)
        grad = jnp.concatenate([top, low], axis=0).astype(bf16)
        grad_ref[k] = grad
        out = dot(grad, weight_ref[k], NN)
        rows = slice(k * PITCH, (k + 1) * PITCH)
        for q in range(out_ref.shape[0] // 2):
            lanes = slice(q * 128, (q + 1) * 128)
            first, second = halves(out[:32, lanes], out[32:, lanes])
            out_ref[2 * q, rows, :] = first.astype(bf16)
            out_ref[2 * q + 1, rows, :] = second.astype(bf16)


def weight_kernel(grad_ref, spec_ref, out_ref):
    for k in range(KEPT):
        out_ref[k] = dot(grad_ref[k], spec_ref[k], TN)


def collect_kernel(got_ref, out_ref, scr):
    total = got_ref[0].astype(f32)
    for i in range(1, got_ref.shape[0]):
        total = total + got_ref[i].astype(f32)
    for k in range(KEPT):
        scr[pl.ds(k, PITCH, stride=KEPT), :] = total[k * PITCH : (k + 1) * PITCH]
    out_ref[...] = scr[...].astype(bf16)


def windows_kernel(got_ref, u_ref, out_ref):
    got = got_ref[...]
    turned = jnp.concatenate([got[:, 64:], got[:, :64]], axis=1)
    low = lax.broadcasted_iota(jnp.int32, got.shape, 1) < 64
    none = jnp.zeros_like(got)
    parts = [
        jnp.where(low, got, none),
        jnp.where(low, turned, none),
        jnp.where(low, none, turned),
        jnp.where(low, none, got),
    ]
    out = dot(u_ref[...], jnp.concatenate(parts, axis=0), NN)
    half = out.shape[0] // 2
    out_ref[...] = (out[:half] + out[half:]).astype(bf16)


def finish_kernel(got_ref, cot_ref, v_ref, out_ref, field, sems):
    sends = []
    for t in range(16):
        low, high = halves(got_ref[t * 32 : t * 32 + 16, :], got_ref[t * 32 + 16 : t * 32 + 32, :])
        coef = jnp.concatenate([low, high, low, high], axis=0)
        part = dot(coef, v_ref[...], TN).astype(bf16).astype(f32).reshape(2, 64, WIN)
        rows = slice(2 * t, 2 * t + 2)
        field[rows] = (cot_ref[rows].astype(f32) + part).astype(bf16)
        if t % 4 == 3:
            done = slice(2 * t - 6, 2 * t + 2)
            sends.append(pltpu.make_async_copy(field.at[done], out_ref.at[done], sems.at[t // 4]))
            sends[-1].start()
    for send in sends:
        send.wait()


def exchange(blocks, axis):
    return lax.all_to_all(blocks, axis, split_axis=0, concat_axis=0, tiled=True)


def body(activation, cotangent, spectral_weight, out_bias):
    const = {name: jnp.asarray(value) for name, value in tables().items()}
    shape = jax.ShapeDtypeStruct
    chan = lax.axis_size("chan")
    width = activation.shape[1]
    inputs = spectral_weight.shape[3]
    weight = spectral_weight.reshape(KEPT, 2 * width, inputs)
    bias_wide = jnp.broadcast_to(out_bias[:, None], (width, WIN))
    square = pltpu.VMEM((M, 128), f32)
    tall = pltpu.VMEM((2 * M, 128), f32)
    small = shape((M, 128), bf16)
    coefs_shape = shape((PITCH * R // 2, 128), bf16)
    across = shape((chan, M, 128), bf16)
    mix_flops = 2 * KEPT * 64 * 128 * inputs

    first = run(
        points_kernel,
        shape((PITCH, R // 2 + EARLY, 128), bf16),
        const["points"],
        activation,
        cotangent,
        scratch=[
            pltpu.VMEM((2 * R, WIN), bf16),
            pltpu.VMEM(activation.shape, bf16),
            pltpu.VMEM((PITCH, R // 2 + EARLY, 128), bf16),
            pltpu.SemaphoreType.DMA((13,)),
        ],
        far=3,
        far_out=True,
        vmem=FIRST_LIMIT,
        name="points",
    )
    first = exchange(first, PITCH_AXES)
    spectra = run(modes_kernel, small, first, const["modes"], name="modes")
    spectra = exchange(spectra, "z")
    spectra = run(gather_kernel, shape((XH * chan, M // XH, 128), bf16), spectra, scratch=[square], name="gather")
    spectra = exchange(spectra, ("xh", "chan"))
    mixed, spec = run(
        mix_kernel,
        (shape((PITCH, width - EARLY + 8, 128), bf16), shape((KEPT, 64, inputs), bf16)),
        spectra,
        weight,
        cotangent,
        scratch=[tall],
        flops=mix_flops,
        name="mix",
    )
    mixed = exchange(mixed, PITCH_AXES)
    grads = run(
        pointwise_kernel,
        shape((2 * M, 128), bf16),
        mixed,
        first,
        bias_wide,
        const["doubled"],
        const["expand"],
        scratch=[tall, tall],
        name="pointwise",
    )
    grads = exchange(grads, PITCH_AXES)
    back, grad, bias = run(
        back_kernel,
        (across, shape((KEPT, 64, 128), bf16), shape((8, 64), f32)),
        grads,
        weight,
        scratch=[tall],
        flops=mix_flops,
        name="back",
    )
    back = exchange(back, "chan")
    grad_weight = run(
        weight_kernel, shape((KEPT, 2 * width, inputs), f32), grad, spec, flops=mix_flops, name="weight"
    )
    back = run(collect_kernel, small, back, scratch=[square], name="collect")
    back = exchange(back, PITCH_AXES)
    coefs = run(windows_kernel, coefs_shape, back, const["windows"], name="windows")
    coefs = exchange(coefs, PITCH_AXES)
    grad_input = run(
        finish_kernel,
        shape(activation.shape, bf16),
        coefs,
        cotangent,
        const["points"],
        scratch=[pltpu.VMEM(activation.shape, bf16), pltpu.SemaphoreType.DMA((4,))],
        far_out=True,
        name="finish",
    )
    return grad_input, grad_weight.reshape(spectral_weight.shape), bias[0]


def solution(mesh):
    fine = Mesh(mesh.devices.reshape(XH, Z, -1), ("xh", "z", "chan"))
    field = P(None, "chan", ("xh", "z"))
    modes = P(("xh", "z"), None, "chan", None)
    return jax.shard_map(
        body,
        mesh=fine,
        in_specs=(field, field, modes, P("chan")),
        out_specs=(field, modes, P("chan")),
        check_vma=False,
    )
```

```python
import functools
import math

import jax
import jax.numpy as jnp
import ml_dtypes
import numpy as np
from jax import lax
from jax.experimental import pallas as pl
from jax.experimental.pallas import tpu as pltpu
from jax.sharding import Mesh
from jax.sharding import PartitionSpec as P

P_SIZE = 4096
M = 128
XH = 2
Z = 16
PITCH = XH * Z
WIN = P_SIZE // PITCH
KEPT = M // PITCH
R = 32
PITCH_AXES = ("xh", "z")
f32 = jnp.float32
bf16 = jnp.bfloat16
NT = (((1,), (1,)), ((), ()))
NN = (((1,), (0,)), ((), ()))
TN = (((0,), (0,)), ((), ()))
VMEM_LIMIT = 32 * 1024 * 1024
FIRST_LIMIT = 60 * 1024 * 1024


def split_hi_lo(table):
    hi = table.astype(ml_dtypes.bfloat16)
    lo = (table - hi.astype(np.float64)).astype(ml_dtypes.bfloat16)
    return hi, lo


@functools.cache
def tables():
    modes = np.arange(M)
    angle = 2.0 * math.pi * (np.outer(modes, np.arange(P_SIZE)) % P_SIZE) / P_SIZE
    forward = np.stack([np.cos(angle), -np.sin(angle)]) / math.sqrt(P_SIZE)
    basis = np.linalg.svd(forward[:, :, :WIN].reshape(2 * M, WIN))[2][:R]
    coef = np.einsum("akwp,xp->akwx", forward.reshape(2, M, PITCH, WIN), basis)
    coef = coef.reshape(2 * M, PITCH, 2, R // 2)
    out = {}
    hi, lo = split_hi_lo(basis)
    out["points"] = np.concatenate([hi, lo], axis=0)
    gather = coef.transpose(2, 0, 1, 3).reshape(2, 2 * M, PITCH * R // 2)
    out["modes"] = np.stack(split_hi_lo(gather), axis=1).reshape(8 * M, PITCH * R // 2)
    spread = coef.transpose(1, 3, 2, 0).reshape(PITCH * R // 2, 4 * M)
    out["windows"] = np.concatenate(split_hi_lo(spread), axis=0)
    scale = np.where(modes == 0, 1.0, 2.0).reshape(1, PITCH, KEPT, 1)
    scaled = coef.reshape(2, PITCH, KEPT, PITCH * R) * scale
    out["doubled"] = np.stack(split_hi_lo(scaled.transpose(0, 2, 1, 3).reshape(2 * M, PITCH * R)))
    high, low = split_hi_lo(np.kron(np.eye(4), basis))
    out["expand"] = np.concatenate([high, high, low], axis=0)
    return out


def dot(left, right, dims):
    return lax.dot_general(left, right, dims, preferred_element_type=f32)


def run(kernel, out_shape, *args, scratch=(), flops=0, name=None, far=0, far_out=False, vmem=VMEM_LIMIT):
    out_space = pltpu.HBM if far_out else pltpu.VMEM
    near = [pl.BlockSpec(memory_space=pltpu.VMEM)] * (len(args) - far)
    touched = sum(int(np.prod(a.shape)) * a.dtype.itemsize for a in list(args) + jax.tree.leaves(out_shape))
    return pl.pallas_call(
        kernel,
        out_shape=out_shape,
        in_specs=near + [pl.BlockSpec(memory_space=pltpu.HBM)] * far,
        out_specs=jax.tree.map(lambda _: pl.BlockSpec(memory_space=out_space), out_shape),
        scratch_shapes=list(scratch),
        compiler_params=pltpu.CompilerParams(vmem_limit_bytes=vmem),
        cost_estimate=pl.CostEstimate(flops=flops, bytes_accessed=touched, transcendentals=0),
        name=name,
    )(*args)


def halves(left, right):
    return (
        jnp.concatenate([left[:, :64], right[:, :64]], axis=1),
        jnp.concatenate([left[:, 64:], right[:, 64:]], axis=1),
    )


def points_kernel(v_ref, x_ref, out_ref, basis, field, sems):
    table = pltpu.make_async_copy(v_ref, basis, sems.at[4])
    parts = [slice(8 * i, 8 * i + 8) for i in range(4)]
    copies = [pltpu.make_async_copy(x_ref.at[part], field.at[part], sems.at[i]) for i, part in enumerate(parts)]
    table.start()
    for copy in copies:
        copy.start()
    table.wait()
    for t in range(16):
        if t % 4 == 0:
            copies[t // 4].wait()
        y = dot(basis[...], field[2 * t : 2 * t + 2].reshape(128, WIN), NT)
        y = y[:R] + y[R:]
        first, second = halves(y[:16], y[16:])
        out_ref[t * 32 : (t + 1) * 32, :] = jnp.concatenate([first, second], axis=0).astype(bf16)


def modes_kernel(got_ref, g_ref, out_ref):
    part = dot(g_ref[...], got_ref[...], NN)
    part = part[: 4 * M, :64] + part[4 * M :, 64:]
    part = part[: 2 * M] + part[2 * M :]
    out_ref[...] = jnp.concatenate([part[:M], part[M:]], axis=1).astype(bf16)


def by_mode(scr, value, count):
    scr[...] = value
    return [scr[pl.ds(k, PITCH, stride=count), :] for k in range(KEPT)]


def gather_kernel(got_ref, out_ref, scr):
    out_ref[...] = jnp.concatenate(by_mode(scr, got_ref[...].astype(f32), KEPT), axis=0).astype(bf16)


def mix_kernel(got_ref, weight_ref, moved_ref, out_ref, spec_ref, scr):
    for k in range(KEPT):
        rows = slice(k * PITCH, (k + 1) * PITCH)
        re, im = [], []
        for q in range(got_ref.shape[0] // 2):
            first, second = halves(got_ref[2 * q, rows, :], got_ref[2 * q + 1, rows, :])
            re.append(first)
            im.append(second)
        spec = jnp.concatenate([jnp.concatenate(re, axis=1), jnp.concatenate(im, axis=1)], axis=0)
        spec_ref[k] = spec
        out = dot(spec, weight_ref[k], NT)
        real = out[:32, :64] - out[32:, 64:]
        imag = out[:32, 64:] + out[32:, :64]
        scr[pl.ds(k, PITCH, stride=KEPT), :] = jnp.concatenate([real, imag], axis=1)
    out_ref[...] = scr[...].astype(bf16)


def pointwise_kernel(got_ref, cot_ref, bias_ref, table_ref, e_ref, out_ref, scr, send):
    root = math.sqrt(2.0 / math.pi)
    mixed = jnp.concatenate(by_mode(scr, got_ref[...].astype(f32), KEPT), axis=0)
    mixed = mixed.T
    mixed = jnp.concatenate([mixed[:64], mixed[64:]], axis=1).astype(bf16)
    bias = bias_ref[...]
    total = jnp.zeros((64, WIN), f32)
    high, low = table_ref[0], table_ref[1]
    coef = dot(mixed, high, NN) + dot(mixed, low, NN)
    ys = []
    for half in range(2):
        groups = range(4 * half, 4 * half + 4)
        part = jnp.concatenate([coef[:, g * 128 : (g + 1) * 128] for g in groups], axis=0)
        part_high = part.astype(bf16)
        part_low = (part - part_high.astype(f32)).astype(bf16)
        response = dot(jnp.concatenate([part_high, part_low, part_high], axis=1), e_ref[...], NN)
        response = response.astype(bf16).astype(f32)
        blocks = []
        for j, g in enumerate(groups):
            grads = []
            for i in range(4):
                v = response[j * 64 : (j + 1) * 64, i * WIN : (i + 1) * WIN] + bias
                square = v * v
                th = jnp.tanh(root * (v + 0.044715 * (square * v)))
                slope = 0.5 * (1.0 + th) + (0.5 * root) * v * (1.0 - th * th) * (1.0 + (3.0 * 0.044715) * square)
                grad = slope * cot_ref[4 * g + i].astype(f32)
                total = total + grad
                grads.append(grad.astype(bf16))
            blocks.append(jnp.concatenate(grads, axis=1))
        y = dot(jnp.concatenate(blocks, axis=0), e_ref[128:, :], NT)
        y = y[:, :128] + y[:, 128:]
        ys += [y[j * 64 : (j + 1) * 64] for j in range(4)]
    y = jnp.concatenate(ys, axis=1)
    y_high = y.astype(bf16)
    y_low = (y - y_high.astype(f32)).astype(bf16)
    modes = dot(high, jnp.concatenate([y_high, y_low], axis=0), NT)
    modes = modes[:, :64] + modes[:, 64:] + dot(low, y_high, NT)
    sums = lax.dot_general(
        jnp.ones((8, WIN), f32), total, NT, precision=lax.Precision.HIGHEST, preferred_element_type=f32
    )
    rounded = sums.astype(bf16).astype(f32)
    sums = jnp.concatenate([rounded, sums - rounded], axis=1)
    modes = jnp.concatenate([modes[:M], modes[M:]], axis=1)
    for k in range(KEPT):
        send[pl.ds(k, PITCH, stride=8), :] = modes[k * PITCH : (k + 1) * PITCH]
    send[pl.ds(KEPT, PITCH, stride=8), :] = jnp.concatenate([sums] * (PITCH // 8), axis=0)
    for k in range(KEPT + 1, 8):
        send[pl.ds(k, PITCH, stride=8), :] = jnp.zeros((PITCH, 128), f32)
    out_ref[...] = send[...].astype(bf16)


def back_kernel(got_ref, weight_ref, out_ref, grad_ref, bias_ref, scr):
    blocks = by_mode(scr, got_ref[...].astype(f32), 8)
    sums = jnp.sum(scr[pl.ds(KEPT, PITCH, stride=8), :], axis=0, keepdims=True)
    bias_ref[...] = jnp.broadcast_to(sums[:, :64] + sums[:, 64:], (8, 64))
    for k in range(KEPT):
        top = blocks[k]
        low = jnp.concatenate([top[:, 64:], -top[:, :64]], axis=1)
        grad = jnp.concatenate([top, low], axis=0).astype(bf16)
        grad_ref[k] = grad
        out = dot(grad, weight_ref[k], NN)
        rows = slice(k * PITCH, (k + 1) * PITCH)
        for q in range(out_ref.shape[0] // 2):
            lanes = slice(q * 128, (q + 1) * 128)
            first, second = halves(out[:32, lanes], out[32:, lanes])
            out_ref[2 * q, rows, :] = first.astype(bf16)
            out_ref[2 * q + 1, rows, :] = second.astype(bf16)


def weight_kernel(grad_ref, spec_ref, out_ref):
    for k in range(KEPT):
        out_ref[k] = dot(grad_ref[k], spec_ref[k], TN)


def collect_kernel(got_ref, out_ref, scr):
    total = got_ref[0].astype(f32)
    for i in range(1, got_ref.shape[0]):
        total = total + got_ref[i].astype(f32)
    for k in range(KEPT):
        scr[pl.ds(k, PITCH, stride=KEPT), :] = total[k * PITCH : (k + 1) * PITCH]
    out_ref[...] = scr[...].astype(bf16)


def windows_kernel(got_ref, u_ref, out_ref):
    got = got_ref[...]
    turned = jnp.concatenate([got[:, 64:], got[:, :64]], axis=1)
    low = lax.broadcasted_iota(jnp.int32, got.shape, 1) < 64
    none = jnp.zeros_like(got)
    parts = [
        jnp.where(low, got, none),
        jnp.where(low, turned, none),
        jnp.where(low, none, turned),
        jnp.where(low, none, got),
    ]
    out = dot(u_ref[...], jnp.concatenate(parts, axis=0), NN)
    half = out.shape[0] // 2
    out_ref[...] = (out[:half] + out[half:]).astype(bf16)


def finish_kernel(got_ref, cot_ref, v_ref, out_ref, field, sems):
    sends = []
    for t in range(16):
        low, high = halves(got_ref[t * 32 : t * 32 + 16, :], got_ref[t * 32 + 16 : t * 32 + 32, :])
        coef = jnp.concatenate([low, high, low, high], axis=0)
        part = dot(coef, v_ref[...], TN).astype(bf16).astype(f32).reshape(2, 64, WIN)
        rows = slice(2 * t, 2 * t + 2)
        field[rows] = (cot_ref[rows].astype(f32) + part).astype(bf16)
        if t % 4 == 3:
            done = slice(2 * t - 6, 2 * t + 2)
            sends.append(pltpu.make_async_copy(field.at[done], out_ref.at[done], sems.at[t // 4]))
            sends[-1].start()
    for send in sends:
        send.wait()


def exchange(blocks, axis):
    return lax.all_to_all(blocks, axis, split_axis=0, concat_axis=0, tiled=True)


def body(activation, cotangent, spectral_weight, out_bias):
    const = {name: jnp.asarray(value) for name, value in tables().items()}
    shape = jax.ShapeDtypeStruct
    chan = lax.axis_size("chan")
    width = activation.shape[1]
    inputs = spectral_weight.shape[3]
    weight = spectral_weight.reshape(KEPT, 2 * width, inputs)
    bias_wide = jnp.broadcast_to(out_bias[:, None], (width, WIN))
    square = pltpu.VMEM((M, 128), f32)
    tall = pltpu.VMEM((2 * M, 128), f32)
    small = shape((M, 128), bf16)
    coefs_shape = shape((PITCH * R // 2, 128), bf16)
    across = shape((chan, M, 128), bf16)
    mix_flops = 2 * KEPT * 64 * 128 * inputs

    coefs = run(
        points_kernel,
        coefs_shape,
        const["points"],
        activation,
        scratch=[pltpu.VMEM((2 * R, WIN), bf16), pltpu.VMEM(activation.shape, bf16), pltpu.SemaphoreType.DMA((5,))],
        far=2,
        vmem=FIRST_LIMIT,
        name="points",
    )
    coefs = exchange(coefs, PITCH_AXES)
    spectra = run(modes_kernel, small, coefs, const["modes"], name="modes")
    spectra = exchange(spectra, PITCH_AXES)
    spectra, moving = lax.optimization_barrier((spectra, cotangent))
    moving = exchange(moving, PITCH_AXES)
    spectra = run(gather_kernel, small, spectra, scratch=[square], name="gather")
    spectra = lax.all_gather(spectra, "chan", axis=0, tiled=False)
    mixed, spec = run(
        mix_kernel,
        (small, shape((KEPT, 64, inputs), bf16)),
        spectra,
        weight,
        moving,
        scratch=[square],
        far=1,
        flops=mix_flops,
        name="mix",
    )
    mixed = exchange(mixed, PITCH_AXES)
    grads = run(
        pointwise_kernel,
        shape((2 * M, 128), bf16),
        mixed,
        moving,
        bias_wide,
        const["doubled"],
        const["expand"],
        scratch=[square, tall],
        name="pointwise",
    )
    grads = exchange(grads, PITCH_AXES)
    back, grad, bias = run(
        back_kernel,
        (across, shape((KEPT, 64, 128), bf16), shape((8, 64), f32)),
        grads,
        weight,
        scratch=[tall],
        flops=mix_flops,
        name="back",
    )
    back = exchange(back, "chan")
    grad_weight = run(
        weight_kernel, shape((KEPT, 2 * width, inputs), f32), grad, spec, flops=mix_flops, name="weight"
    )
    back = run(collect_kernel, small, back, scratch=[square], name="collect")
    back = exchange(back, PITCH_AXES)
    coefs = run(windows_kernel, coefs_shape, back, const["windows"], name="windows")
    coefs = exchange(coefs, PITCH_AXES)
    grad_input = run(
        finish_kernel,
        shape(activation.shape, bf16),
        coefs,
        cotangent,
        const["points"],
        scratch=[pltpu.VMEM(activation.shape, bf16), pltpu.SemaphoreType.DMA((4,))],
        far_out=True,
        name="finish",
    )
    return grad_input, grad_weight.reshape(spectral_weight.shape), bias[0]


def solution(mesh):
    fine = Mesh(mesh.devices.reshape(XH, Z, -1), ("xh", "z", "chan"))
    field = P(None, "chan", ("xh", "z"))
    modes = P(("xh", "z"), None, "chan", None)
    return jax.shard_map(
        body,
        mesh=fine,
        in_specs=(field, field, modes, P("chan")),
        out_specs=(field, modes, P("chan")),
        check_vma=False,
    )
```

```python
import functools
import math

import jax
import jax.numpy as jnp
import ml_dtypes
import numpy as np
from jax import lax
from jax.experimental import pallas as pl
from jax.experimental.pallas import tpu as pltpu
from jax.sharding import Mesh
from jax.sharding import PartitionSpec as P

P_SIZE = 4096
M = 128
XH = 2
Z = 16
PITCH = XH * Z
WIN = P_SIZE // PITCH
KEPT = M // PITCH
BOTH = XH * KEPT
R = 32
PITCH_AXES = ("xh", "z")
f32 = jnp.float32
bf16 = jnp.bfloat16
NT = (((1,), (1,)), ((), ()))
NN = (((1,), (0,)), ((), ()))
TN = (((0,), (0,)), ((), ()))
VMEM_LIMIT = 32 * 1024 * 1024
FIRST_LIMIT = 60 * 1024 * 1024


def split_hi_lo(table):
    hi = table.astype(ml_dtypes.bfloat16)
    lo = (table - hi.astype(np.float64)).astype(ml_dtypes.bfloat16)
    return hi, lo


@functools.cache
def tables():
    modes = np.arange(M)
    angle = 2.0 * math.pi * (np.outer(modes, np.arange(P_SIZE)) % P_SIZE) / P_SIZE
    forward = np.stack([np.cos(angle), -np.sin(angle)]) / math.sqrt(P_SIZE)
    basis = np.linalg.svd(forward[:, :, :WIN].reshape(2 * M, WIN))[2][:R]
    coef = np.einsum("akwp,xp->akwx", forward.reshape(2, M, PITCH, WIN), basis)
    coef = coef.reshape(2 * M, PITCH, 2, R // 2)
    out = {}
    hi, lo = split_hi_lo(basis)
    out["points"] = np.concatenate([hi, lo], axis=0)
    by_z = coef.reshape(2, XH, Z, KEPT, PITCH, 2, R // 2).transpose(5, 0, 2, 1, 3, 4, 6)
    gather = by_z.reshape(2, 2 * M, PITCH * R // 2)
    out["modes"] = np.stack(split_hi_lo(gather), axis=1).reshape(8 * M, PITCH * R // 2)
    spread = by_z.transpose(5, 6, 0, 1, 2, 3, 4)
    spread = spread.reshape(PITCH * R // 2, 4 * M)
    out["windows"] = np.concatenate(split_hi_lo(spread), axis=0)
    scale = np.where(modes == 0, 1.0, 2.0).reshape(1, XH, Z, KEPT, 1)
    scaled = coef.reshape(2, XH, Z, KEPT, PITCH * R) * scale
    scaled = scaled.transpose(0, 1, 3, 2, 4).reshape(2 * M, PITCH * R)
    out["doubled"] = np.stack(split_hi_lo(scaled))
    high, low = split_hi_lo(np.kron(np.eye(4), basis))
    out["expand"] = np.concatenate([high, high, low], axis=0)
    return out


def dot(left, right, dims):
    return lax.dot_general(left, right, dims, preferred_element_type=f32)


def run(kernel, out_shape, *args, scratch=(), flops=0, name=None, far=0, far_out=False, vmem=VMEM_LIMIT, scalars=0):
    out_space = pltpu.HBM if far_out else pltpu.VMEM
    near = [pl.BlockSpec(memory_space=pltpu.SMEM)] * scalars
    near += [pl.BlockSpec(memory_space=pltpu.VMEM)] * (len(args) - far - scalars)
    touched = sum(int(np.prod(a.shape)) * a.dtype.itemsize for a in list(args) + jax.tree.leaves(out_shape))
    return pl.pallas_call(
        kernel,
        out_shape=out_shape,
        in_specs=near + [pl.BlockSpec(memory_space=pltpu.HBM)] * far,
        out_specs=jax.tree.map(lambda _: pl.BlockSpec(memory_space=out_space), out_shape),
        scratch_shapes=list(scratch),
        compiler_params=pltpu.CompilerParams(vmem_limit_bytes=vmem),
        cost_estimate=pl.CostEstimate(flops=flops, bytes_accessed=touched, transcendentals=0),
        name=name,
    )(*args)


def halves(left, right):
    return (
        jnp.concatenate([left[:, :64], right[:, :64]], axis=1),
        jnp.concatenate([left[:, 64:], right[:, 64:]], axis=1),
    )


def points_kernel(v_ref, x_ref, cot_ref, out_ref, basis, field, message, sems):
    table = pltpu.make_async_copy(v_ref, basis, sems.at[12])
    fields, cots, sends = [], [], []
    for i in range(4):
        part = slice(8 * i, 8 * i + 8)
        fields.append(pltpu.make_async_copy(x_ref.at[part], field.at[part], sems.at[i]))
        cots.append(
            pltpu.make_async_copy(cot_ref.at[part], message.at[part, R // 2 :, :], sems.at[4 + i])
        )
        sends.append(pltpu.make_async_copy(message.at[part], out_ref.at[part], sems.at[8 + i]))
    table.start()
    for i in range(4):
        fields[i].start()
        cots[i].start()
    table.wait()
    for i in range(4):
        fields[i].wait()
        for t in range(4 * i, 4 * i + 4):
            y = dot(basis[...], field[2 * t : 2 * t + 2].reshape(128, WIN), NT)
            y = y[:R] + y[R:]
            first, second = halves(y[:16], y[16:])
            message[2 * t, 0:16, :] = first.astype(bf16)
            message[2 * t + 1, 0:16, :] = second.astype(bf16)
        cots[i].wait()
        sends[i].start()
    for i in range(4):
        sends[i].wait()


def modes_kernel(got_ref, g_ref, out_ref):
    got = got_ref[:, 0 : R // 2, :].reshape(PITCH * R // 2, 128)
    part = dot(g_ref[...], got, NN)
    part = part[: 4 * M, :64] + part[4 * M :, 64:]
    part = part[: 2 * M] + part[2 * M :]
    out_ref[...] = jnp.concatenate([part[:M], part[M:]], axis=1).astype(bf16)


def by_mode(scr, value, count):
    scr[...] = value
    return [scr[pl.ds(k, Z, stride=count), :] for k in range(BOTH)]


def gather_kernel(got_ref, out_ref, scr):
    send = jnp.concatenate(by_mode(scr, got_ref[...].astype(f32), BOTH), axis=0).astype(bf16)
    for i in range(out_ref.shape[0]):
        out_ref[i] = send


def mix_kernel(got_ref, weight_ref, out_ref, spec_ref, scr):
    for k in range(BOTH):
        rows = slice(k * Z, (k + 1) * Z)
        re, im = [], []
        for q in range(got_ref.shape[0] // 2):
            first, second = halves(got_ref[2 * q, rows, :], got_ref[2 * q + 1, rows, :])
            re.append(first)
            im.append(second)
        spec = jnp.concatenate([jnp.concatenate(re, axis=1), jnp.concatenate(im, axis=1)], axis=0)
        spec_ref[k] = spec
        out = dot(spec, weight_ref[k], NT)
        real = out[:Z, :64] - out[Z:, 64:]
        imag = out[:Z, 64:] + out[Z:, :64]
        scr[pl.ds(k, Z, stride=BOTH), :] = jnp.concatenate([real, imag], axis=1)
    out_ref[...] = scr[...].astype(bf16)


def pointwise_kernel(got_ref, cot_ref, bias_ref, table_ref, e_ref, out_ref, scr, send):
    root = math.sqrt(2.0 / math.pi)
    mixed = jnp.concatenate(by_mode(scr, got_ref[...].astype(f32), BOTH), axis=0)
    mixed = mixed.T
    mixed = jnp.concatenate([mixed[:64], mixed[64:]], axis=1).astype(bf16)
    bias = bias_ref[...]
    total = jnp.zeros((64, WIN), f32)
    high, low = table_ref[0], table_ref[1]
    coef = dot(mixed, high, NN) + dot(mixed, low, NN)
    ys = []
    for half in range(2):
        groups = range(4 * half, 4 * half + 4)
        part = jnp.concatenate([coef[:, g * 128 : (g + 1) * 128] for g in groups], axis=0)
        part_high = part.astype(bf16)
        part_low = (part - part_high.astype(f32)).astype(bf16)
        response = dot(jnp.concatenate([part_high, part_low, part_high], axis=1), e_ref[...], NN)
        response = response.astype(bf16).astype(f32)
        blocks = []
        for j, g in enumerate(groups):
            grads = []
            for i in range(4):
                v = response[j * 64 : (j + 1) * 64, i * WIN : (i + 1) * WIN] + bias
                square = v * v
                th = jnp.tanh(root * (v + 0.044715 * (square * v)))
                slope = 0.5 * (1.0 + th) + (0.5 * root) * v * (1.0 - th * th) * (1.0 + (3.0 * 0.044715) * square)
                grad = slope * cot_ref[4 * g + i, R // 2 :, :].astype(f32)
                total = total + grad
                grads.append(grad.astype(bf16))
            blocks.append(jnp.concatenate(grads, axis=1))
        y = dot(jnp.concatenate(blocks, axis=0), e_ref[128:, :], NT)
        y = y[:, :128] + y[:, 128:]
        ys += [y[j * 64 : (j + 1) * 64] for j in range(4)]
    y = jnp.concatenate(ys, axis=1)
    y_high = y.astype(bf16)
    y_low = (y - y_high.astype(f32)).astype(bf16)
    modes = dot(high, jnp.concatenate([y_high, y_low], axis=0), NT)
    modes = modes[:, :64] + modes[:, 64:] + dot(low, y_high, NT)
    sums = lax.dot_general(
        jnp.ones((8, WIN), f32), total, NT, precision=lax.Precision.HIGHEST, preferred_element_type=f32
    )
    rounded = sums.astype(bf16).astype(f32)
    sums = jnp.concatenate([rounded, sums - rounded], axis=1)
    modes = jnp.concatenate([modes[:M], modes[M:]], axis=1)
    for k in range(BOTH):
        send[pl.ds(k, Z, stride=2 * BOTH), :] = modes[k * Z : (k + 1) * Z]
    send[pl.ds(BOTH, Z, stride=2 * BOTH), :] = jnp.concatenate([sums] * (Z // 8), axis=0)
    for k in range(BOTH + 1, 2 * BOTH):
        send[pl.ds(k, Z, stride=2 * BOTH), :] = jnp.zeros((Z, 128), f32)
    out_ref[...] = send[...].astype(bf16)


def back_kernel(got_ref, weight_ref, spec_ref, out_ref, pack_ref, scr):
    blocks = by_mode(scr, got_ref[...].astype(f32), 2 * BOTH)
    inputs = spec_ref.shape[2]
    sums = jnp.sum(scr[pl.ds(BOTH, Z, stride=2 * BOTH), :], axis=0, keepdims=True)
    sums = sums[:, :64] + sums[:, 64:]
    rounded = sums.astype(bf16).astype(f32)
    sums = jnp.concatenate([rounded, sums - rounded], axis=1)
    pack_ref[BOTH] = jnp.zeros(pack_ref.shape[1:], bf16)
    pack_ref[BOTH, :, inputs:] = jnp.broadcast_to(sums, (2 * Z, 128)).astype(bf16)
    for k in range(BOTH):
        top = blocks[k]
        low = jnp.concatenate([top[:, 64:], -top[:, :64]], axis=1)
        grad = jnp.concatenate([top, low], axis=0).astype(bf16)
        pack_ref[k, :, 0:inputs] = spec_ref[k]
        pack_ref[k, :, inputs:] = grad
        out = dot(grad, weight_ref[k], NN)
        rows = slice(k * Z, (k + 1) * Z)
        for q in range(out_ref.shape[0] // 2):
            lanes = slice(q * 128, (q + 1) * 128)
            first, second = halves(out[:Z, lanes], out[Z:, lanes])
            out_ref[2 * q, rows, :] = first.astype(bf16)
            out_ref[2 * q + 1, rows, :] = second.astype(bf16)


def weight_kernel(where_ref, pack_ref, out_ref, bias_ref):
    inputs = pack_ref.shape[3] - 128
    for k in range(KEPT):
        mode = where_ref[0] * KEPT + k
        both = [pack_ref[a, mode] for a in range(XH)]
        grad = jnp.concatenate([block[:, inputs:] for block in both], axis=0)
        spec = jnp.concatenate([block[:, :inputs] for block in both], axis=0)
        out_ref[k] = dot(grad, spec, TN)
    sums = pack_ref[0, BOTH, :, inputs:].astype(f32) + pack_ref[1, BOTH, :, inputs:].astype(f32)
    bias_ref[...] = (sums[:, :64] + sums[:, 64:])[:8]


def collect_kernel(got_ref, out_ref, scr):
    total = got_ref[0].astype(f32)
    for i in range(1, got_ref.shape[0]):
        total = total + got_ref[i].astype(f32)
    for k in range(BOTH):
        scr[pl.ds(k, Z, stride=BOTH), :] = total[k * Z : (k + 1) * Z]
    out_ref[...] = scr[...].astype(bf16)


def windows_kernel(got_ref, u_ref, out_ref):
    got = got_ref[...]
    turned = jnp.concatenate([got[:, 64:], got[:, :64]], axis=1)
    low = lax.broadcasted_iota(jnp.int32, got.shape, 1) < 64
    none = jnp.zeros_like(got)
    parts = [
        jnp.where(low, got, none),
        jnp.where(low, turned, none),
        jnp.where(low, none, turned),
        jnp.where(low, none, got),
    ]
    out = dot(u_ref[...], jnp.concatenate(parts, axis=0), NN)
    half = out.shape[0] // 2
    out_ref[...] = (out[:half] + out[half:]).astype(bf16)


def finish_kernel(got_ref, cot_ref, v_ref, bias_ref, out_ref, field, sems):
    sends = []
    for t in range(16):
        low, high = halves(got_ref[t * 32 : t * 32 + 16, :], got_ref[t * 32 + 16 : t * 32 + 32, :])
        coef = jnp.concatenate([low, high, low, high], axis=0)
        part = dot(coef, v_ref[...], TN).astype(bf16).astype(f32).reshape(2, 64, WIN)
        rows = slice(2 * t, 2 * t + 2)
        field[rows] = (cot_ref[rows].astype(f32) + part).astype(bf16)
        if t % 4 == 3:
            done = slice(2 * t - 6, 2 * t + 2)
            sends.append(pltpu.make_async_copy(field.at[done], out_ref.at[done], sems.at[t // 4]))
            sends[-1].start()
    for send in sends:
        send.wait()


def exchange(blocks, axis):
    return lax.all_to_all(blocks, axis, split_axis=0, concat_axis=0, tiled=True)


def body(activation, cotangent, spectral_weight, out_bias):
    const = {name: jnp.asarray(value) for name, value in tables().items()}
    shape = jax.ShapeDtypeStruct
    chan = lax.axis_size("chan")
    width = activation.shape[1]
    inputs = spectral_weight.shape[3]
    weight = spectral_weight.reshape(KEPT, 2 * width, inputs)
    bias_wide = jnp.broadcast_to(out_bias[:, None], (width, WIN))
    square = pltpu.VMEM((M, 128), f32)
    tall = pltpu.VMEM((2 * M, 128), f32)
    small = shape((M, 128), bf16)
    coefs_shape = shape((PITCH * R // 2, 128), bf16)
    across = shape((chan, M, 128), bf16)
    mix_flops = 2 * KEPT * 64 * 128 * inputs

    first = run(
        points_kernel,
        shape((PITCH, R // 2 + width, 128), bf16),
        const["points"],
        activation,
        cotangent,
        scratch=[
            pltpu.VMEM((2 * R, WIN), bf16),
            pltpu.VMEM(activation.shape, bf16),
            pltpu.VMEM((PITCH, R // 2 + width, 128), bf16),
            pltpu.SemaphoreType.DMA((13,)),
        ],
        far=3,
        far_out=True,
        vmem=FIRST_LIMIT,
        name="points",
    )
    first = exchange(first, PITCH_AXES)
    weights = lax.all_gather(weight, "xh", axis=0, tiled=True)
    spectra = run(modes_kernel, small, first, const["modes"], name="modes")
    spectra = exchange(spectra, "z")
    spectra = run(gather_kernel, across, spectra, scratch=[square], name="gather")
    spectra = exchange(spectra, "chan")
    mixed, spec = run(
        mix_kernel,
        (small, shape((BOTH, 2 * Z, inputs), bf16)),
        spectra,
        weights,
        scratch=[square],
        flops=mix_flops,
        name="mix",
    )
    mixed = exchange(mixed, "z")
    grads = run(
        pointwise_kernel,
        shape((2 * M, 128), bf16),
        mixed,
        first,
        bias_wide,
        const["doubled"],
        const["expand"],
        scratch=[square, tall],
        name="pointwise",
    )
    grads = exchange(grads, "z")
    back, pack = run(
        back_kernel,
        (across, shape((BOTH + 1, 2 * Z, inputs + 128), bf16)),
        grads,
        weights,
        spec,
        scratch=[tall],
        flops=mix_flops,
        name="back",
    )
    pack = lax.all_gather(pack, "xh", axis=0, tiled=False)
    back = exchange(back, "chan")
    where = jnp.reshape(lax.axis_index("xh"), (1,)).astype(jnp.int32)
    grad_weight, bias = run(
        weight_kernel,
        (shape((KEPT, 2 * width, inputs), f32), shape((8, 64), f32)),
        where,
        pack,
        scalars=1,
        flops=mix_flops,
        name="weight",
    )
    back = run(collect_kernel, small, back, scratch=[square], name="collect")
    back = exchange(back, "z")
    coefs = run(windows_kernel, coefs_shape, back, const["windows"], name="windows")
    coefs = exchange(coefs, PITCH_AXES)
    grad_input = run(
        finish_kernel,
        shape(activation.shape, bf16),
        coefs,
        cotangent,
        const["points"],
        bias,
        scratch=[pltpu.VMEM(activation.shape, bf16), pltpu.SemaphoreType.DMA((4,))],
        far_out=True,
        name="finish",
    )
    return grad_input, grad_weight.reshape(spectral_weight.shape), bias[0]


def solution(mesh):
    fine = Mesh(mesh.devices.reshape(XH, Z, -1), ("xh", "z", "chan"))
    field = P(None, "chan", ("xh", "z"))
    modes = P(("xh", "z"), None, "chan", None)
    return jax.shard_map(
        body,
        mesh=fine,
        in_specs=(field, field, modes, P("chan")),
        out_specs=(field, modes, P("chan")),
        check_vma=False,
    )
```

```python
import functools
import math

import jax
import jax.numpy as jnp
import ml_dtypes
import numpy as np
from jax import lax
from jax.experimental import pallas as pl
from jax.experimental.pallas import tpu as pltpu
from jax.sharding import Mesh
from jax.sharding import PartitionSpec as P

P_SIZE = 4096
M = 128
XH = 2
Z = 16
PITCH = XH * Z
WIN = P_SIZE // PITCH
KEPT = M // PITCH
BOTH = XH * KEPT
R = 32
PITCH_AXES = ("xh", "z")
f32 = jnp.float32
bf16 = jnp.bfloat16
NT = (((1,), (1,)), ((), ()))
NN = (((1,), (0,)), ((), ()))
TN = (((0,), (0,)), ((), ()))
VMEM_LIMIT = 32 * 1024 * 1024
FIRST_LIMIT = 60 * 1024 * 1024


def split_hi_lo(table):
    hi = table.astype(ml_dtypes.bfloat16)
    lo = (table - hi.astype(np.float64)).astype(ml_dtypes.bfloat16)
    return hi, lo


@functools.cache
def tables():
    modes = np.arange(M)
    angle = 2.0 * math.pi * (np.outer(modes, np.arange(P_SIZE)) % P_SIZE) / P_SIZE
    forward = np.stack([np.cos(angle), -np.sin(angle)]) / math.sqrt(P_SIZE)
    basis = np.linalg.svd(forward[:, :, :WIN].reshape(2 * M, WIN))[2][:R]
    coef = np.einsum("akwp,xp->akwx", forward.reshape(2, M, PITCH, WIN), basis)
    coef = coef.reshape(2 * M, PITCH, 2, R // 2)
    out = {}
    hi, lo = split_hi_lo(basis)
    out["points"] = np.concatenate([hi, lo], axis=0)
    by_z = coef.reshape(2, XH, Z, KEPT, PITCH, 2, R // 2).transpose(5, 0, 2, 1, 3, 4, 6)
    gather = by_z.reshape(2, 2 * M, PITCH * R // 2)
    out["modes"] = np.stack(split_hi_lo(gather), axis=1).reshape(8 * M, PITCH * R // 2)
    spread = by_z.transpose(5, 6, 0, 1, 2, 3, 4)
    spread = spread.reshape(PITCH * R // 2, 4 * M)
    out["windows"] = np.concatenate(split_hi_lo(spread), axis=0)
    scale = np.where(modes == 0, 1.0, 2.0).reshape(1, XH, Z, KEPT, 1)
    scaled = coef.reshape(2, XH, Z, KEPT, PITCH * R) * scale
    scaled = scaled.transpose(0, 1, 3, 2, 4).reshape(2 * M, PITCH * R)
    out["doubled"] = np.stack(split_hi_lo(scaled))
    high, low = split_hi_lo(np.kron(np.eye(4), basis))
    out["expand"] = np.concatenate([high, high, low], axis=0)
    return out


def dot(left, right, dims):
    return lax.dot_general(left, right, dims, preferred_element_type=f32)


def run(kernel, out_shape, *args, scratch=(), flops=0, name=None, far=0, far_out=False, vmem=VMEM_LIMIT, scalars=0):
    out_space = pltpu.HBM if far_out else pltpu.VMEM
    near = [pl.BlockSpec(memory_space=pltpu.SMEM)] * scalars
    near += [pl.BlockSpec(memory_space=pltpu.VMEM)] * (len(args) - far - scalars)
    touched = sum(int(np.prod(a.shape)) * a.dtype.itemsize for a in list(args) + jax.tree.leaves(out_shape))
    return pl.pallas_call(
        kernel,
        out_shape=out_shape,
        in_specs=near + [pl.BlockSpec(memory_space=pltpu.HBM)] * far,
        out_specs=jax.tree.map(lambda _: pl.BlockSpec(memory_space=out_space), out_shape),
        scratch_shapes=list(scratch),
        compiler_params=pltpu.CompilerParams(vmem_limit_bytes=vmem),
        cost_estimate=pl.CostEstimate(flops=flops, bytes_accessed=touched, transcendentals=0),
        name=name,
    )(*args)


def halves(left, right):
    return (
        jnp.concatenate([left[:, :64], right[:, :64]], axis=1),
        jnp.concatenate([left[:, 64:], right[:, 64:]], axis=1),
    )


def points_kernel(v_ref, x_ref, cot_ref, out_ref, basis, field, message, sems):
    table = pltpu.make_async_copy(v_ref, basis, sems.at[12])
    fields, cots, sends = [], [], []
    for i in range(4):
        part = slice(8 * i, 8 * i + 8)
        fields.append(pltpu.make_async_copy(x_ref.at[part], field.at[part], sems.at[i]))
        cots.append(
            pltpu.make_async_copy(cot_ref.at[part], message.at[part, R // 2 :, :], sems.at[4 + i])
        )
        sends.append(pltpu.make_async_copy(message.at[part], out_ref.at[part], sems.at[8 + i]))
    table.start()
    for i in range(4):
        fields[i].start()
        cots[i].start()
    table.wait()
    for i in range(4):
        fields[i].wait()
        for t in range(4 * i, 4 * i + 4):
            y = dot(basis[...], field[2 * t : 2 * t + 2].reshape(128, WIN), NT)
            y = y[:R] + y[R:]
            first, second = halves(y[:16], y[16:])
            message[2 * t, 0:16, :] = first.astype(bf16)
            message[2 * t + 1, 0:16, :] = second.astype(bf16)
        cots[i].wait()
        sends[i].start()
    for i in range(4):
        sends[i].wait()


def modes_kernel(where_ref, got_ref, g_ref, out_ref):
    got = got_ref[:, 0 : R // 2, :].reshape(PITCH * R // 2, 128)
    part = dot(g_ref[...], got, NN)
    part = part[: 4 * M, :64] + part[4 * M :, 64:]
    part = part[: 2 * M] + part[2 * M :]
    out_ref[...] = jnp.concatenate([part[:M], part[M:]], axis=1).astype(bf16)


def by_mode(scr, value, count):
    scr[...] = value
    return [scr[pl.ds(k, Z, stride=count), :] for k in range(BOTH)]


def gather_kernel(got_ref, arrived_ref, out_ref, scr):
    send = jnp.concatenate(by_mode(scr, got_ref[...].astype(f32), BOTH), axis=0).astype(bf16)
    for i in range(out_ref.shape[0]):
        out_ref[i] = send


def by_place(where_ref, own_ref, other_ref, step):
    for place in range(XH):
        refs = [own_ref, other_ref] if place == 0 else [other_ref, own_ref]

        @pl.when(where_ref[0] == place)
        def _(refs=refs):
            step([refs[k // KEPT].at[k % KEPT] for k in range(BOTH)])


def mix_kernel(where_ref, got_ref, own_ref, other_ref, out_ref, spec_ref, scr):
    for k in range(BOTH):
        rows = slice(k * Z, (k + 1) * Z)
        re, im = [], []
        for q in range(got_ref.shape[0] // 2):
            first, second = halves(got_ref[2 * q, rows, :], got_ref[2 * q + 1, rows, :])
            re.append(first)
            im.append(second)
        spec_ref[k] = jnp.concatenate([jnp.concatenate(re, axis=1), jnp.concatenate(im, axis=1)], axis=0)

    def step(weights):
        for k in range(BOTH):
            out = dot(spec_ref[k], weights[k][...], NT)
            real = out[:Z, :64] - out[Z:, 64:]
            imag = out[:Z, 64:] + out[Z:, :64]
            scr[pl.ds(k, Z, stride=BOTH), :] = jnp.concatenate([real, imag], axis=1)

    by_place(where_ref, own_ref, other_ref, step)
    out_ref[...] = scr[...].astype(bf16)


def pointwise_kernel(got_ref, cot_ref, bias_ref, table_ref, e_ref, out_ref, scr, send):
    root = math.sqrt(2.0 / math.pi)
    mixed = jnp.concatenate(by_mode(scr, got_ref[...].astype(f32), BOTH), axis=0)
    mixed = mixed.T
    mixed = jnp.concatenate([mixed[:64], mixed[64:]], axis=1).astype(bf16)
    bias = bias_ref[...]
    total = jnp.zeros((64, WIN), f32)
    high, low = table_ref[0], table_ref[1]
    coef = dot(mixed, high, NN) + dot(mixed, low, NN)
    ys = []
    for half in range(2):
        groups = range(4 * half, 4 * half + 4)
        part = jnp.concatenate([coef[:, g * 128 : (g + 1) * 128] for g in groups], axis=0)
        part_high = part.astype(bf16)
        part_low = (part - part_high.astype(f32)).astype(bf16)
        response = dot(jnp.concatenate([part_high, part_low, part_high], axis=1), e_ref[...], NN)
        response = response.astype(bf16).astype(f32)
        blocks = []
        for j, g in enumerate(groups):
            grads = []
            for i in range(4):
                v = response[j * 64 : (j + 1) * 64, i * WIN : (i + 1) * WIN] + bias
                square = v * v
                th = jnp.tanh(root * (v + 0.044715 * (square * v)))
                slope = 0.5 * (1.0 + th) + (0.5 * root) * v * (1.0 - th * th) * (1.0 + (3.0 * 0.044715) * square)
                grad = slope * cot_ref[4 * g + i, R // 2 :, :].astype(f32)
                total = total + grad
                grads.append(grad.astype(bf16))
            blocks.append(jnp.concatenate(grads, axis=1))
        y = dot(jnp.concatenate(blocks, axis=0), e_ref[128:, :], NT)
        y = y[:, :128] + y[:, 128:]
        ys += [y[j * 64 : (j + 1) * 64] for j in range(4)]
    y = jnp.concatenate(ys, axis=1)
    y_high = y.astype(bf16)
    y_low = (y - y_high.astype(f32)).astype(bf16)
    modes = dot(high, jnp.concatenate([y_high, y_low], axis=0), NT)
    modes = modes[:, :64] + modes[:, 64:] + dot(low, y_high, NT)
    sums = lax.dot_general(
        jnp.ones((8, WIN), f32), total, NT, precision=lax.Precision.HIGHEST, preferred_element_type=f32
    )
    rounded = sums.astype(bf16).astype(f32)
    sums = jnp.concatenate([rounded, sums - rounded], axis=1)
    modes = jnp.concatenate([modes[:M], modes[M:]], axis=1)
    for k in range(BOTH):
        send[pl.ds(k, Z, stride=2 * BOTH), :] = modes[k * Z : (k + 1) * Z]
    send[pl.ds(BOTH, Z, stride=2 * BOTH), :] = jnp.concatenate([sums] * (Z // 8), axis=0)
    for k in range(BOTH + 1, 2 * BOTH):
        send[pl.ds(k, Z, stride=2 * BOTH), :] = jnp.zeros((Z, 128), f32)
    out_ref[...] = send[...].astype(bf16)


def back_kernel(where_ref, got_ref, own_ref, other_ref, spec_ref, out_ref, grad_ref, send_ref, scr):
    blocks = by_mode(scr, got_ref[...].astype(f32), 2 * BOTH)
    inputs = spec_ref.shape[2]
    sums = jnp.sum(scr[pl.ds(BOTH, Z, stride=2 * BOTH), :], axis=0, keepdims=True)
    sums = sums[:, :64] + sums[:, 64:]
    rounded = sums.astype(bf16).astype(f32)
    sums = jnp.concatenate([rounded, sums - rounded], axis=1)
    grad_ref[BOTH] = jnp.broadcast_to(sums, (2 * Z, 128)).astype(bf16)
    for k in range(BOTH):
        top = blocks[k]
        low = jnp.concatenate([top[:, 64:], -top[:, :64]], axis=1)
        grad_ref[k] = jnp.concatenate([top, low], axis=0).astype(bf16)

    def step(weights):
        for k in range(BOTH):
            out = dot(grad_ref[k], weights[k][...], NN)
            rows = slice(k * Z, (k + 1) * Z)
            for q in range(out_ref.shape[0] // 2):
                lanes = slice(q * 128, (q + 1) * 128)
                first, second = halves(out[:Z, lanes], out[Z:, lanes])
                out_ref[2 * q, rows, :] = first.astype(bf16)
                out_ref[2 * q + 1, rows, :] = second.astype(bf16)

    by_place(where_ref, own_ref, other_ref, step)
    for k in range(KEPT):
        mode = (1 - where_ref[0]) * KEPT + k
        send_ref[k, :, 0:inputs] = spec_ref[mode]
        send_ref[k, :, inputs:] = grad_ref[mode]
    send_ref[KEPT, :, 0:inputs] = jnp.zeros((2 * Z, inputs), bf16)
    send_ref[KEPT, :, inputs:] = grad_ref[BOTH]


def weight_kernel(where_ref, grad_ref, spec_ref, got_ref, out_ref, bias_ref):
    inputs = spec_ref.shape[2]
    for k in range(KEPT):
        mode = where_ref[0] * KEPT + k
        grad = jnp.concatenate([grad_ref[mode], got_ref[k, :, inputs:]], axis=0)
        spec = jnp.concatenate([spec_ref[mode], got_ref[k, :, :inputs]], axis=0)
        out_ref[k] = dot(grad, spec, TN)
    sums = grad_ref[BOTH].astype(f32) + got_ref[KEPT, :, inputs:].astype(f32)
    bias_ref[...] = (sums[:, :64] + sums[:, 64:])[:8]


def collect_kernel(got_ref, out_ref, scr):
    total = got_ref[0].astype(f32)
    for i in range(1, got_ref.shape[0]):
        total = total + got_ref[i].astype(f32)
    for k in range(BOTH):
        scr[pl.ds(k, Z, stride=BOTH), :] = total[k * Z : (k + 1) * Z]
    out_ref[...] = scr[...].astype(bf16)


def windows_kernel(got_ref, u_ref, out_ref):
    got = got_ref[...]
    turned = jnp.concatenate([got[:, 64:], got[:, :64]], axis=1)
    low = lax.broadcasted_iota(jnp.int32, got.shape, 1) < 64
    none = jnp.zeros_like(got)
    parts = [
        jnp.where(low, got, none),
        jnp.where(low, turned, none),
        jnp.where(low, none, turned),
        jnp.where(low, none, got),
    ]
    out = dot(u_ref[...], jnp.concatenate(parts, axis=0), NN)
    half = out.shape[0] // 2
    out_ref[...] = (out[:half] + out[half:]).astype(bf16)


def finish_kernel(got_ref, cot_ref, v_ref, bias_ref, out_ref, field, sems):
    sends = []
    for t in range(16):
        low, high = halves(got_ref[t * 32 : t * 32 + 16, :], got_ref[t * 32 + 16 : t * 32 + 32, :])
        coef = jnp.concatenate([low, high, low, high], axis=0)
        part = dot(coef, v_ref[...], TN).astype(bf16).astype(f32).reshape(2, 64, WIN)
        rows = slice(2 * t, 2 * t + 2)
        field[rows] = (cot_ref[rows].astype(f32) + part).astype(bf16)
        if t % 4 == 3:
            done = slice(2 * t - 6, 2 * t + 2)
            sends.append(pltpu.make_async_copy(field.at[done], out_ref.at[done], sems.at[t // 4]))
            sends[-1].start()
    for send in sends:
        send.wait()


def exchange(blocks, axis):
    return lax.all_to_all(blocks, axis, split_axis=0, concat_axis=0, tiled=True)


def body(activation, cotangent, spectral_weight, out_bias):
    const = {name: jnp.asarray(value) for name, value in tables().items()}
    shape = jax.ShapeDtypeStruct
    chan = lax.axis_size("chan")
    width = activation.shape[1]
    inputs = spectral_weight.shape[3]
    weight = spectral_weight.reshape(KEPT, 2 * width, inputs)
    bias_wide = jnp.broadcast_to(out_bias[:, None], (width, WIN))
    where = jnp.reshape(lax.axis_index("xh"), (1,)).astype(jnp.int32)
    pairs = [(0, 1), (1, 0)]
    partner = lax.ppermute(weight, "xh", pairs)
    square = pltpu.VMEM((M, 128), f32)
    tall = pltpu.VMEM((2 * M, 128), f32)
    small = shape((M, 128), bf16)
    coefs_shape = shape((PITCH * R // 2, 128), bf16)
    across = shape((chan, M, 128), bf16)
    mix_flops = 2 * KEPT * 64 * 128 * inputs

    first = run(
        points_kernel,
        shape((PITCH, R // 2 + width, 128), bf16),
        const["points"],
        activation,
        cotangent,
        scratch=[
            pltpu.VMEM((2 * R, WIN), bf16),
            pltpu.VMEM(activation.shape, bf16),
            pltpu.VMEM((PITCH, R // 2 + width, 128), bf16),
            pltpu.SemaphoreType.DMA((13,)),
        ],
        far=3,
        far_out=True,
        vmem=FIRST_LIMIT,
        name="points",
    )
    first = exchange(first, PITCH_AXES)
    spectra = run(modes_kernel, small, where, first, const["modes"], scalars=1, name="modes")
    spectra = exchange(spectra, "z")
    spectra = run(gather_kernel, across, spectra, partner, scratch=[square], far=1, name="gather")
    spectra = exchange(spectra, "chan")
    mixed, spec = run(
        mix_kernel,
        (small, shape((BOTH, 2 * Z, inputs), bf16)),
        where,
        spectra,
        weight,
        partner,
        scalars=1,
        scratch=[square],
        flops=mix_flops,
        name="mix",
    )
    mixed = exchange(mixed, "z")
    grads = run(
        pointwise_kernel,
        shape((2 * M, 128), bf16),
        mixed,
        first,
        bias_wide,
        const["doubled"],
        const["expand"],
        scratch=[square, tall],
        name="pointwise",
    )
    grads = exchange(grads, "z")
    back, grad, send = run(
        back_kernel,
        (
            across,
            shape((BOTH + 1, 2 * Z, 128), bf16),
            shape((KEPT + 1, 2 * Z, inputs + 128), bf16),
        ),
        where,
        grads,
        weight,
        partner,
        spec,
        scalars=1,
        scratch=[tall],
        flops=mix_flops,
        name="back",
    )
    received = lax.ppermute(send, "xh", pairs)
    back = exchange(back, "chan")
    grad_weight, bias = run(
        weight_kernel,
        (shape((KEPT, 2 * width, inputs), f32), shape((8, 64), f32)),
        where,
        grad,
        spec,
        received,
        scalars=1,
        flops=mix_flops,
        name="weight",
    )
    back = run(collect_kernel, small, back, scratch=[square], name="collect")
    back = exchange(back, "z")
    coefs = run(windows_kernel, coefs_shape, back, const["windows"], name="windows")
    coefs = exchange(coefs, PITCH_AXES)
    grad_input = run(
        finish_kernel,
        shape(activation.shape, bf16),
        coefs,
        cotangent,
        const["points"],
        bias,
        scratch=[pltpu.VMEM(activation.shape, bf16), pltpu.SemaphoreType.DMA((4,))],
        far_out=True,
        name="finish",
    )
    return grad_input, grad_weight.reshape(spectral_weight.shape), bias[0]


def solution(mesh):
    fine = Mesh(mesh.devices.reshape(XH, Z, -1), ("xh", "z", "chan"))
    field = P(None, "chan", ("xh", "z"))
    modes = P(("xh", "z"), None, "chan", None)
    return jax.shard_map(
        body,
        mesh=fine,
        in_specs=(field, field, modes, P("chan")),
        out_specs=(field, modes, P("chan")),
        check_vma=False,
    )
```

```python
import functools
import math

import jax
import jax.numpy as jnp
import ml_dtypes
import numpy as np
from jax import lax
from jax.experimental import pallas as pl
from jax.experimental.pallas import tpu as pltpu
from jax.sharding import Mesh
from jax.sharding import PartitionSpec as P

P_SIZE = 4096
M = 128
XH = 2
Z = 16
PITCH = XH * Z
WIN = P_SIZE // PITCH
KEPT = M // PITCH
BOTH = XH * KEPT
R = 32
PITCH_AXES = ("xh", "z")
f32 = jnp.float32
bf16 = jnp.bfloat16
NT = (((1,), (1,)), ((), ()))
NN = (((1,), (0,)), ((), ()))
TN = (((0,), (0,)), ((), ()))
VMEM_LIMIT = 32 * 1024 * 1024
FIRST_LIMIT = 60 * 1024 * 1024


def split_hi_lo(table):
    hi = table.astype(ml_dtypes.bfloat16)
    lo = (table - hi.astype(np.float64)).astype(ml_dtypes.bfloat16)
    return hi, lo


@functools.cache
def tables():
    modes = np.arange(M)
    angle = 2.0 * math.pi * (np.outer(modes, np.arange(P_SIZE)) % P_SIZE) / P_SIZE
    forward = np.stack([np.cos(angle), -np.sin(angle)]) / math.sqrt(P_SIZE)
    basis = np.linalg.svd(forward[:, :, :WIN].reshape(2 * M, WIN))[2][:R]
    coef = np.einsum("akwp,xp->akwx", forward.reshape(2, M, PITCH, WIN), basis)
    coef = coef.reshape(2 * M, PITCH, 2, R // 2)
    out = {}
    hi, lo = split_hi_lo(basis)
    out["points"] = np.concatenate([hi, lo], axis=0)
    by_z = coef.reshape(2, XH, Z, KEPT, PITCH, 2, R // 2).transpose(5, 0, 2, 1, 3, 4, 6)
    gather = by_z.reshape(2, 2 * M, PITCH * R // 2)
    out["modes"] = np.stack(split_hi_lo(gather), axis=1).reshape(8 * M, PITCH * R // 2)
    spread = by_z.transpose(5, 6, 0, 1, 2, 3, 4)
    spread = spread.reshape(PITCH * R // 2, 4 * M)
    out["windows"] = np.concatenate(split_hi_lo(spread), axis=0)
    scale = np.where(modes == 0, 1.0, 2.0).reshape(1, XH, Z, KEPT, 1)
    scaled = coef.reshape(2, XH, Z, KEPT, PITCH * R) * scale
    scaled = scaled.transpose(0, 1, 3, 2, 4).reshape(2 * M, PITCH * R)
    out["doubled"] = np.stack(split_hi_lo(scaled))
    high, low = split_hi_lo(np.kron(np.eye(4), basis))
    out["expand"] = np.concatenate([high, high, low], axis=0)
    return out


def dot(left, right, dims):
    return lax.dot_general(left, right, dims, preferred_element_type=f32)


def run(kernel, out_shape, *args, scratch=(), flops=0, name=None, far=0, far_out=False, vmem=VMEM_LIMIT, scalars=0):
    out_space = pltpu.HBM if far_out else pltpu.VMEM
    near = [pl.BlockSpec(memory_space=pltpu.SMEM)] * scalars
    near += [pl.BlockSpec(memory_space=pltpu.VMEM)] * (len(args) - far - scalars)
    touched = sum(int(np.prod(a.shape)) * a.dtype.itemsize for a in list(args) + jax.tree.leaves(out_shape))
    return pl.pallas_call(
        kernel,
        out_shape=out_shape,
        in_specs=near + [pl.BlockSpec(memory_space=pltpu.HBM)] * far,
        out_specs=jax.tree.map(lambda _: pl.BlockSpec(memory_space=out_space), out_shape),
        scratch_shapes=list(scratch),
        compiler_params=pltpu.CompilerParams(vmem_limit_bytes=vmem),
        cost_estimate=pl.CostEstimate(flops=flops, bytes_accessed=touched, transcendentals=0),
        name=name,
    )(*args)


def halves(left, right):
    return (
        jnp.concatenate([left[:, :64], right[:, :64]], axis=1),
        jnp.concatenate([left[:, 64:], right[:, 64:]], axis=1),
    )


def points_kernel(v_ref, x_ref, cot_ref, out_ref, basis, field, message, sems):
    table = pltpu.make_async_copy(v_ref, basis, sems.at[12])
    fields, cots, sends = [], [], []
    for i in range(4):
        part = slice(8 * i, 8 * i + 8)
        fields.append(pltpu.make_async_copy(x_ref.at[part], field.at[part], sems.at[i]))
        cots.append(
            pltpu.make_async_copy(cot_ref.at[part], message.at[part, R // 2 :, :], sems.at[4 + i])
        )
        sends.append(pltpu.make_async_copy(message.at[part], out_ref.at[part], sems.at[8 + i]))
    table.start()
    for i in range(4):
        fields[i].start()
        cots[i].start()
    table.wait()
    for i in range(4):
        fields[i].wait()
        for t in range(4 * i, 4 * i + 4):
            y = dot(basis[...], field[2 * t : 2 * t + 2].reshape(128, WIN), NT)
            y = y[:R] + y[R:]
            first, second = halves(y[:16], y[16:])
            message[2 * t, 0:16, :] = first.astype(bf16)
            message[2 * t + 1, 0:16, :] = second.astype(bf16)
        cots[i].wait()
        sends[i].start()
    for i in range(4):
        sends[i].wait()


def modes_kernel(where_ref, got_ref, g_ref, arrived_ref, out_ref):
    got = got_ref[:, 0 : R // 2, :].reshape(PITCH * R // 2, 128)
    part = dot(g_ref[...], got, NN)
    part = part[: 4 * M, :64] + part[4 * M :, 64:]
    part = part[: 2 * M] + part[2 * M :]
    out_ref[...] = jnp.concatenate([part[:M], part[M:]], axis=1).astype(bf16)


def by_mode(scr, value, count):
    scr[...] = value
    return [scr[pl.ds(k, Z, stride=count), :] for k in range(BOTH)]


def gather_kernel(got_ref, out_ref, scr):
    send = jnp.concatenate(by_mode(scr, got_ref[...].astype(f32), BOTH), axis=0).astype(bf16)
    for i in range(out_ref.shape[0]):
        out_ref[i] = send


def by_place(where_ref, own_ref, other_ref, step):
    for place in range(XH):
        refs = [own_ref, other_ref] if place == 0 else [other_ref, own_ref]

        @pl.when(where_ref[0] == place)
        def _(refs=refs):
            step([refs[k // KEPT].at[k % KEPT] for k in range(BOTH)])


def mix_kernel(where_ref, got_ref, own_ref, other_ref, out_ref, spec_ref, scr):
    for k in range(BOTH):
        rows = slice(k * Z, (k + 1) * Z)
        re, im = [], []
        for q in range(got_ref.shape[0] // 2):
            first, second = halves(got_ref[2 * q, rows, :], got_ref[2 * q + 1, rows, :])
            re.append(first)
            im.append(second)
        spec_ref[k] = jnp.concatenate([jnp.concatenate(re, axis=1), jnp.concatenate(im, axis=1)], axis=0)

    def step(weights):
        for k in range(BOTH):
            out = dot(spec_ref[k], weights[k][...], NT)
            real = out[:Z, :64] - out[Z:, 64:]
            imag = out[:Z, 64:] + out[Z:, :64]
            scr[pl.ds(k, Z, stride=BOTH), :] = jnp.concatenate([real, imag], axis=1)

    by_place(where_ref, own_ref, other_ref, step)
    out_ref[...] = scr[...].astype(bf16)


def pointwise_kernel(got_ref, cot_ref, bias_ref, table_ref, e_ref, out_ref, scr, send):
    root = math.sqrt(2.0 / math.pi)
    mixed = jnp.concatenate(by_mode(scr, got_ref[...].astype(f32), BOTH), axis=0)
    mixed = mixed.T
    mixed = jnp.concatenate([mixed[:64], mixed[64:]], axis=1).astype(bf16)
    bias = bias_ref[...]
    total = jnp.zeros((64, WIN), f32)
    high, low = table_ref[0], table_ref[1]
    coef = dot(mixed, high, NN) + dot(mixed, low, NN)
    ys = []
    for half in range(2):
        groups = range(4 * half, 4 * half + 4)
        part = jnp.concatenate([coef[:, g * 128 : (g + 1) * 128] for g in groups], axis=0)
        part_high = part.astype(bf16)
        part_low = (part - part_high.astype(f32)).astype(bf16)
        response = dot(jnp.concatenate([part_high, part_low, part_high], axis=1), e_ref[...], NN)
        response = response.astype(bf16).astype(f32)
        blocks = []
        for j, g in enumerate(groups):
            grads = []
            for i in range(4):
                v = response[j * 64 : (j + 1) * 64, i * WIN : (i + 1) * WIN] + bias
                square = v * v
                th = jnp.tanh(root * (v + 0.044715 * (square * v)))
                slope = 0.5 * (1.0 + th) + (0.5 * root) * v * (1.0 - th * th) * (1.0 + (3.0 * 0.044715) * square)
                grad = slope * cot_ref[4 * g + i, R // 2 :, :].astype(f32)
                total = total + grad
                grads.append(grad.astype(bf16))
            blocks.append(jnp.concatenate(grads, axis=1))
        y = dot(jnp.concatenate(blocks, axis=0), e_ref[128:, :], NT)
        y = y[:, :128] + y[:, 128:]
        ys += [y[j * 64 : (j + 1) * 64] for j in range(4)]
    y = jnp.concatenate(ys, axis=1)
    y_high = y.astype(bf16)
    y_low = (y - y_high.astype(f32)).astype(bf16)
    modes = dot(high, jnp.concatenate([y_high, y_low], axis=0), NT)
    modes = modes[:, :64] + modes[:, 64:] + dot(low, y_high, NT)
    sums = lax.dot_general(
        jnp.ones((8, WIN), f32), total, NT, precision=lax.Precision.HIGHEST, preferred_element_type=f32
    )
    rounded = sums.astype(bf16).astype(f32)
    sums = jnp.concatenate([rounded, sums - rounded], axis=1)
    modes = jnp.concatenate([modes[:M], modes[M:]], axis=1)
    for k in range(BOTH):
        send[pl.ds(k, Z, stride=2 * BOTH), :] = modes[k * Z : (k + 1) * Z]
    send[pl.ds(BOTH, Z, stride=2 * BOTH), :] = jnp.concatenate([sums] * (Z // 8), axis=0)
    for k in range(BOTH + 1, 2 * BOTH):
        send[pl.ds(k, Z, stride=2 * BOTH), :] = jnp.zeros((Z, 128), f32)
    out_ref[...] = send[...].astype(bf16)


def back_kernel(where_ref, got_ref, own_ref, other_ref, spec_ref, out_ref, grad_ref, scr):
    blocks = by_mode(scr, got_ref[...].astype(f32), 2 * BOTH)
    sums = jnp.sum(scr[pl.ds(BOTH, Z, stride=2 * BOTH), :], axis=0, keepdims=True)
    sums = sums[:, :64] + sums[:, 64:]
    rounded = sums.astype(bf16).astype(f32)
    sums = jnp.concatenate([rounded, sums - rounded], axis=1)
    grad_ref[BOTH] = jnp.broadcast_to(sums, (2 * Z, 128)).astype(bf16)
    for k in range(BOTH):
        top = blocks[k]
        low = jnp.concatenate([top[:, 64:], -top[:, :64]], axis=1)
        grad_ref[k] = jnp.concatenate([top, low], axis=0).astype(bf16)

    def step(weights):
        for k in range(BOTH):
            out = dot(grad_ref[k], weights[k][...], NN)
            rows = slice(k * Z, (k + 1) * Z)
            for q in range(out_ref.shape[0] // 2):
                lanes = slice(q * 128, (q + 1) * 128)
                first, second = halves(out[:Z, lanes], out[Z:, lanes])
                out_ref[2 * q, rows, :] = first.astype(bf16)
                out_ref[2 * q + 1, rows, :] = second.astype(bf16)

    by_place(where_ref, own_ref, other_ref, step)


def pack_kernel(where_ref, grad_ref, spec_ref, before_ref, send_ref):
    inputs = spec_ref.shape[2]
    for k in range(KEPT):
        mode = (1 - where_ref[0]) * KEPT + k
        send_ref[k, :, 0:inputs] = spec_ref[mode]
        send_ref[k, :, inputs:] = grad_ref[mode]
    send_ref[KEPT, :, 0:inputs] = jnp.zeros((2 * Z, inputs), bf16)
    send_ref[KEPT, :, inputs:] = grad_ref[BOTH]


def weight_kernel(where_ref, grad_ref, spec_ref, got_ref, out_ref, bias_ref):
    inputs = spec_ref.shape[2]
    for k in range(KEPT):
        mode = where_ref[0] * KEPT + k
        grad = jnp.concatenate([grad_ref[mode], got_ref[k, :, inputs:]], axis=0)
        spec = jnp.concatenate([spec_ref[mode], got_ref[k, :, :inputs]], axis=0)
        out_ref[k] = dot(grad, spec, TN)
    sums = grad_ref[BOTH].astype(f32) + got_ref[KEPT, :, inputs:].astype(f32)
    bias_ref[...] = (sums[:, :64] + sums[:, 64:])[:8]


def collect_kernel(got_ref, out_ref, scr):
    total = got_ref[0].astype(f32)
    for i in range(1, got_ref.shape[0]):
        total = total + got_ref[i].astype(f32)
    for k in range(BOTH):
        scr[pl.ds(k, Z, stride=BOTH), :] = total[k * Z : (k + 1) * Z]
    out_ref[...] = scr[...].astype(bf16)


def windows_kernel(got_ref, u_ref, out_ref):
    got = got_ref[...]
    turned = jnp.concatenate([got[:, 64:], got[:, :64]], axis=1)
    low = lax.broadcasted_iota(jnp.int32, got.shape, 1) < 64
    none = jnp.zeros_like(got)
    parts = [
        jnp.where(low, got, none),
        jnp.where(low, turned, none),
        jnp.where(low, none, turned),
        jnp.where(low, none, got),
    ]
    out = dot(u_ref[...], jnp.concatenate(parts, axis=0), NN)
    half = out.shape[0] // 2
    out_ref[...] = (out[:half] + out[half:]).astype(bf16)


def finish_kernel(got_ref, cot_ref, v_ref, bias_ref, out_ref, field, sems):
    sends = []
    for t in range(16):
        low, high = halves(got_ref[t * 32 : t * 32 + 16, :], got_ref[t * 32 + 16 : t * 32 + 32, :])
        coef = jnp.concatenate([low, high, low, high], axis=0)
        part = dot(coef, v_ref[...], TN).astype(bf16).astype(f32).reshape(2, 64, WIN)
        rows = slice(2 * t, 2 * t + 2)
        field[rows] = (cot_ref[rows].astype(f32) + part).astype(bf16)
        if t % 4 == 3:
            done = slice(2 * t - 6, 2 * t + 2)
            sends.append(pltpu.make_async_copy(field.at[done], out_ref.at[done], sems.at[t // 4]))
            sends[-1].start()
    for send in sends:
        send.wait()


def exchange(blocks, axis):
    return lax.all_to_all(blocks, axis, split_axis=0, concat_axis=0, tiled=True)


def body(activation, cotangent, spectral_weight, out_bias):
    const = {name: jnp.asarray(value) for name, value in tables().items()}
    shape = jax.ShapeDtypeStruct
    chan = lax.axis_size("chan")
    width = activation.shape[1]
    inputs = spectral_weight.shape[3]
    weight = spectral_weight.reshape(KEPT, 2 * width, inputs)
    bias_wide = jnp.broadcast_to(out_bias[:, None], (width, WIN))
    where = jnp.reshape(lax.axis_index("xh"), (1,)).astype(jnp.int32)
    pairs = [(0, 1), (1, 0)]
    partner = lax.ppermute(weight, "xh", pairs)
    square = pltpu.VMEM((M, 128), f32)
    tall = pltpu.VMEM((2 * M, 128), f32)
    small = shape((M, 128), bf16)
    coefs_shape = shape((PITCH * R // 2, 128), bf16)
    across = shape((chan, M, 128), bf16)
    mix_flops = 2 * KEPT * 64 * 128 * inputs

    first = run(
        points_kernel,
        shape((PITCH, R // 2 + width, 128), bf16),
        const["points"],
        activation,
        cotangent,
        scratch=[
            pltpu.VMEM((2 * R, WIN), bf16),
            pltpu.VMEM(activation.shape, bf16),
            pltpu.VMEM((PITCH, R // 2 + width, 128), bf16),
            pltpu.SemaphoreType.DMA((13,)),
        ],
        far=3,
        far_out=True,
        vmem=FIRST_LIMIT,
        name="points",
    )
    first = exchange(first, PITCH_AXES)
    spectra = run(modes_kernel, small, where, first, const["modes"], partner, scalars=1, far=1, name="modes")
    spectra = exchange(spectra, "z")
    spectra = run(gather_kernel, across, spectra, scratch=[square], name="gather")
    spectra = exchange(spectra, "chan")
    mixed, spec = run(
        mix_kernel,
        (small, shape((BOTH, 2 * Z, inputs), bf16)),
        where,
        spectra,
        weight,
        partner,
        scalars=1,
        scratch=[square],
        flops=mix_flops,
        name="mix",
    )
    mixed = exchange(mixed, "z")
    grads = run(
        pointwise_kernel,
        shape((2 * M, 128), bf16),
        mixed,
        first,
        bias_wide,
        const["doubled"],
        const["expand"],
        scratch=[square, tall],
        name="pointwise",
    )
    grads = exchange(grads, "z")
    back, grad = run(
        back_kernel,
        (
            across,
            shape((BOTH + 1, 2 * Z, 128), bf16),
        ),
        where,
        grads,
        weight,
        partner,
        spec,
        scalars=1,
        scratch=[tall],
        flops=mix_flops,
        name="back",
    )
    back = exchange(back, "chan")
    back = run(collect_kernel, small, back, scratch=[square], name="collect")
    send = run(
        pack_kernel,
        shape((KEPT + 1, 2 * Z, inputs + 128), bf16),
        where,
        grad,
        spec,
        back,
        scalars=1,
        far=1,
        name="pack",
    )
    back = exchange(back, "z")
    coefs = run(windows_kernel, coefs_shape, back, const["windows"], name="windows")
    received = lax.ppermute(send, "xh", pairs)
    grad_weight, bias = run(
        weight_kernel,
        (shape((KEPT, 2 * width, inputs), f32), shape((8, 64), f32)),
        where,
        grad,
        spec,
        received,
        scalars=1,
        flops=mix_flops,
        name="weight",
    )
    coefs = exchange(coefs, PITCH_AXES)
    grad_input = run(
        finish_kernel,
        shape(activation.shape, bf16),
        coefs,
        cotangent,
        const["points"],
        bias,
        scratch=[pltpu.VMEM(activation.shape, bf16), pltpu.SemaphoreType.DMA((4,))],
        far_out=True,
        name="finish",
    )
    return grad_input, grad_weight.reshape(spectral_weight.shape), bias[0]


def solution(mesh):
    fine = Mesh(mesh.devices.reshape(XH, Z, -1), ("xh", "z", "chan"))
    field = P(None, "chan", ("xh", "z"))
    modes = P(("xh", "z"), None, "chan", None)
    return jax.shard_map(
        body,
        mesh=fine,
        in_specs=(field, field, modes, P("chan")),
        out_specs=(field, modes, P("chan")),
        check_vma=False,
    )
```

```python
import functools
import math

import jax
import jax.numpy as jnp
import ml_dtypes
import numpy as np
from jax import lax
from jax.experimental import pallas as pl
from jax.experimental.pallas import tpu as pltpu
from jax.sharding import Mesh
from jax.sharding import PartitionSpec as P

P_SIZE = 4096
M = 128
XH = 2
Z = 16
PITCH = XH * Z
WIN = P_SIZE // PITCH
KEPT = M // PITCH
BOTH = XH * KEPT
R = 32
PITCH_AXES = ("xh", "z")
f32 = jnp.float32
bf16 = jnp.bfloat16
NT = (((1,), (1,)), ((), ()))
NN = (((1,), (0,)), ((), ()))
TN = (((0,), (0,)), ((), ()))
VMEM_LIMIT = 32 * 1024 * 1024
FIRST_LIMIT = 60 * 1024 * 1024


def split_hi_lo(table):
    hi = table.astype(ml_dtypes.bfloat16)
    lo = (table - hi.astype(np.float64)).astype(ml_dtypes.bfloat16)
    return hi, lo


@functools.cache
def tables():
    modes = np.arange(M)
    angle = 2.0 * math.pi * (np.outer(modes, np.arange(P_SIZE)) % P_SIZE) / P_SIZE
    forward = np.stack([np.cos(angle), -np.sin(angle)]) / math.sqrt(P_SIZE)
    basis = np.linalg.svd(forward[:, :, :WIN].reshape(2 * M, WIN))[2][:R]
    coef = np.einsum("akwp,xp->akwx", forward.reshape(2, M, PITCH, WIN), basis)
    coef = coef.reshape(2 * M, PITCH, 2, R // 2)
    out = {}
    hi, lo = split_hi_lo(basis)
    out["points"] = np.concatenate([hi, lo], axis=0)
    by_z = coef.reshape(2, XH, Z, KEPT, PITCH, 2, R // 2).transpose(5, 0, 2, 1, 3, 4, 6)
    gather = by_z.reshape(2, 2 * M, PITCH * R // 2)
    out["modes"] = np.stack(split_hi_lo(gather), axis=1).reshape(8 * M, PITCH * R // 2)
    spread = by_z.transpose(5, 6, 0, 1, 2, 3, 4)
    spread = spread.reshape(PITCH * R // 2, 4 * M)
    out["windows"] = np.concatenate(split_hi_lo(spread), axis=0)
    scale = np.where(modes == 0, 1.0, 2.0).reshape(1, XH, Z, KEPT, 1)
    scaled = coef.reshape(2, XH, Z, KEPT, PITCH * R) * scale
    scaled = scaled.transpose(0, 1, 3, 2, 4).reshape(2 * M, PITCH * R)
    out["doubled"] = np.stack(split_hi_lo(scaled))
    high, low = split_hi_lo(np.kron(np.eye(4), basis))
    out["expand"] = np.concatenate([high, high, low], axis=0)
    return out


def dot(left, right, dims):
    return lax.dot_general(left, right, dims, preferred_element_type=f32)


def run(kernel, out_shape, *args, scratch=(), flops=0, name=None, far=0, far_out=False, vmem=VMEM_LIMIT, scalars=0):
    out_space = pltpu.HBM if far_out else pltpu.VMEM
    near = [pl.BlockSpec(memory_space=pltpu.SMEM)] * scalars
    near += [pl.BlockSpec(memory_space=pltpu.VMEM)] * (len(args) - far - scalars)
    touched = sum(int(np.prod(a.shape)) * a.dtype.itemsize for a in list(args) + jax.tree.leaves(out_shape))
    return pl.pallas_call(
        kernel,
        out_shape=out_shape,
        in_specs=near + [pl.BlockSpec(memory_space=pltpu.HBM)] * far,
        out_specs=jax.tree.map(lambda _: pl.BlockSpec(memory_space=out_space), out_shape),
        scratch_shapes=list(scratch),
        compiler_params=pltpu.CompilerParams(vmem_limit_bytes=vmem),
        cost_estimate=pl.CostEstimate(flops=flops, bytes_accessed=touched, transcendentals=0),
        name=name,
    )(*args)


def halves(left, right):
    return (
        jnp.concatenate([left[:, :64], right[:, :64]], axis=1),
        jnp.concatenate([left[:, 64:], right[:, 64:]], axis=1),
    )


def points_kernel(v_ref, x_ref, cot_ref, out_ref, basis, field, message, sems):
    table = pltpu.make_async_copy(v_ref, basis, sems.at[12])
    fields, cots, sends = [], [], []
    for i in range(4):
        part = slice(8 * i, 8 * i + 8)
        fields.append(pltpu.make_async_copy(x_ref.at[part], field.at[part], sems.at[i]))
        cots.append(
            pltpu.make_async_copy(cot_ref.at[part], message.at[part, R // 2 :, :], sems.at[4 + i])
        )
        sends.append(pltpu.make_async_copy(message.at[part], out_ref.at[part], sems.at[8 + i]))
    table.start()
    for i in range(4):
        fields[i].start()
        cots[i].start()
    table.wait()
    for i in range(4):
        fields[i].wait()
        for t in range(4 * i, 4 * i + 4):
            y = dot(basis[...], field[2 * t : 2 * t + 2].reshape(128, WIN), NT)
            y = y[:R] + y[R:]
            first, second = halves(y[:16], y[16:])
            message[2 * t, 0:16, :] = first.astype(bf16)
            message[2 * t + 1, 0:16, :] = second.astype(bf16)
        cots[i].wait()
        sends[i].start()
    for i in range(4):
        sends[i].wait()


def modes_kernel(where_ref, got_ref, g_ref, out_ref):
    got = got_ref[:, 0 : R // 2, :].reshape(PITCH * R // 2, 128)
    part = dot(g_ref[...], got, NN)
    part = part[: 4 * M, :64] + part[4 * M :, 64:]
    part = part[: 2 * M] + part[2 * M :]
    out_ref[...] = jnp.concatenate([part[:M], part[M:]], axis=1).astype(bf16)


def by_mode(scr, value, count):
    scr[...] = value
    return [scr[pl.ds(k, Z, stride=count), :] for k in range(BOTH)]


def gather_kernel(got_ref, arrived_ref, out_ref, scr):
    send = jnp.concatenate(by_mode(scr, got_ref[...].astype(f32), BOTH), axis=0).astype(bf16)
    for i in range(out_ref.shape[0]):
        out_ref[i] = send


def by_place(where_ref, own_ref, other_ref, step):
    for place in range(XH):
        refs = [own_ref, other_ref] if place == 0 else [other_ref, own_ref]

        @pl.when(where_ref[0] == place)
        def _(refs=refs):
            step([refs[k // KEPT].at[k % KEPT] for k in range(BOTH)])


def mix_kernel(where_ref, got_ref, own_ref, other_ref, out_ref, spec_ref, send_ref, scr):
    for k in range(BOTH):
        rows = slice(k * Z, (k + 1) * Z)
        re, im = [], []
        for q in range(got_ref.shape[0] // 2):
            first, second = halves(got_ref[2 * q, rows, :], got_ref[2 * q + 1, rows, :])
            re.append(first)
            im.append(second)
        spec_ref[k] = jnp.concatenate([jnp.concatenate(re, axis=1), jnp.concatenate(im, axis=1)], axis=0)

    def step(weights):
        for k in range(BOTH):
            out = dot(spec_ref[k], weights[k][...], NT)
            real = out[:Z, :64] - out[Z:, 64:]
            imag = out[:Z, 64:] + out[Z:, :64]
            scr[pl.ds(k, Z, stride=BOTH), :] = jnp.concatenate([real, imag], axis=1)

    by_place(where_ref, own_ref, other_ref, step)
    out_ref[...] = scr[...].astype(bf16)
    for k in range(KEPT):
        send_ref[k] = spec_ref[(1 - where_ref[0]) * KEPT + k]


def pointwise_kernel(got_ref, cot_ref, bias_ref, table_ref, e_ref, out_ref, scr, send):
    root = math.sqrt(2.0 / math.pi)
    mixed = jnp.concatenate(by_mode(scr, got_ref[...].astype(f32), BOTH), axis=0)
    mixed = mixed.T
    mixed = jnp.concatenate([mixed[:64], mixed[64:]], axis=1).astype(bf16)
    bias = bias_ref[...]
    total = jnp.zeros((64, WIN), f32)
    high, low = table_ref[0], table_ref[1]
    coef = dot(mixed, high, NN) + dot(mixed, low, NN)
    ys = []
    for half in range(2):
        groups = range(4 * half, 4 * half + 4)
        part = jnp.concatenate([coef[:, g * 128 : (g + 1) * 128] for g in groups], axis=0)
        part_high = part.astype(bf16)
        part_low = (part - part_high.astype(f32)).astype(bf16)
        response = dot(jnp.concatenate([part_high, part_low, part_high], axis=1), e_ref[...], NN)
        response = response.astype(bf16).astype(f32)
        blocks = []
        for j, g in enumerate(groups):
            grads = []
            for i in range(4):
                v = response[j * 64 : (j + 1) * 64, i * WIN : (i + 1) * WIN] + bias
                square = v * v
                th = jnp.tanh(root * (v + 0.044715 * (square * v)))
                slope = 0.5 * (1.0 + th) + (0.5 * root) * v * (1.0 - th * th) * (1.0 + (3.0 * 0.044715) * square)
                grad = slope * cot_ref[4 * g + i, R // 2 :, :].astype(f32)
                total = total + grad
                grads.append(grad.astype(bf16))
            blocks.append(jnp.concatenate(grads, axis=1))
        y = dot(jnp.concatenate(blocks, axis=0), e_ref[128:, :], NT)
        y = y[:, :128] + y[:, 128:]
        ys += [y[j * 64 : (j + 1) * 64] for j in range(4)]
    y = jnp.concatenate(ys, axis=1)
    y_high = y.astype(bf16)
    y_low = (y - y_high.astype(f32)).astype(bf16)
    modes = dot(high, jnp.concatenate([y_high, y_low], axis=0), NT)
    modes = modes[:, :64] + modes[:, 64:] + dot(low, y_high, NT)
    sums = lax.dot_general(
        jnp.ones((8, WIN), f32), total, NT, precision=lax.Precision.HIGHEST, preferred_element_type=f32
    )
    rounded = sums.astype(bf16).astype(f32)
    sums = jnp.concatenate([rounded, sums - rounded], axis=1)
    modes = jnp.concatenate([modes[:M], modes[M:]], axis=1)
    for k in range(BOTH):
        send[pl.ds(k, Z, stride=2 * BOTH), :] = modes[k * Z : (k + 1) * Z]
    send[pl.ds(BOTH, Z, stride=2 * BOTH), :] = jnp.concatenate([sums] * (Z // 8), axis=0)
    for k in range(BOTH + 1, 2 * BOTH):
        send[pl.ds(k, Z, stride=2 * BOTH), :] = jnp.zeros((Z, 128), f32)
    out_ref[...] = send[...].astype(bf16)


def back_kernel(where_ref, got_ref, own_ref, other_ref, out_ref, grad_ref, send_ref, scr):
    blocks = by_mode(scr, got_ref[...].astype(f32), 2 * BOTH)
    sums = jnp.sum(scr[pl.ds(BOTH, Z, stride=2 * BOTH), :], axis=0, keepdims=True)
    sums = sums[:, :64] + sums[:, 64:]
    rounded = sums.astype(bf16).astype(f32)
    sums = jnp.concatenate([rounded, sums - rounded], axis=1)
    grad_ref[BOTH] = jnp.broadcast_to(sums, (2 * Z, 128)).astype(bf16)
    for k in range(BOTH):
        top = blocks[k]
        low = jnp.concatenate([top[:, 64:], -top[:, :64]], axis=1)
        grad_ref[k] = jnp.concatenate([top, low], axis=0).astype(bf16)

    def step(weights):
        for k in range(BOTH):
            out = dot(grad_ref[k], weights[k][...], NN)
            rows = slice(k * Z, (k + 1) * Z)
            for q in range(out_ref.shape[0] // 2):
                lanes = slice(q * 128, (q + 1) * 128)
                first, second = halves(out[:Z, lanes], out[Z:, lanes])
                out_ref[2 * q, rows, :] = first.astype(bf16)
                out_ref[2 * q + 1, rows, :] = second.astype(bf16)

    by_place(where_ref, own_ref, other_ref, step)
    for k in range(KEPT):
        send_ref[k] = grad_ref[(1 - where_ref[0]) * KEPT + k]
    send_ref[KEPT] = grad_ref[BOTH]


def weight_kernel(where_ref, grad_ref, spec_ref, other_grad_ref, other_spec_ref, out_ref, bias_ref):
    for k in range(KEPT):
        mode = where_ref[0] * KEPT + k
        grad = jnp.concatenate([grad_ref[mode], other_grad_ref[k]], axis=0)
        spec = jnp.concatenate([spec_ref[mode], other_spec_ref[k]], axis=0)
        out_ref[k] = dot(grad, spec, TN)
    sums = grad_ref[BOTH].astype(f32) + other_grad_ref[KEPT].astype(f32)
    bias_ref[...] = (sums[:, :64] + sums[:, 64:])[:8]


def collect_kernel(got_ref, out_ref, scr):
    total = got_ref[0].astype(f32)
    for i in range(1, got_ref.shape[0]):
        total = total + got_ref[i].astype(f32)
    for k in range(BOTH):
        scr[pl.ds(k, Z, stride=BOTH), :] = total[k * Z : (k + 1) * Z]
    out_ref[...] = scr[...].astype(bf16)


def windows_kernel(got_ref, u_ref, out_ref):
    got = got_ref[...]
    turned = jnp.concatenate([got[:, 64:], got[:, :64]], axis=1)
    low = lax.broadcasted_iota(jnp.int32, got.shape, 1) < 64
    none = jnp.zeros_like(got)
    parts = [
        jnp.where(low, got, none),
        jnp.where(low, turned, none),
        jnp.where(low, none, turned),
        jnp.where(low, none, got),
    ]
    out = dot(u_ref[...], jnp.concatenate(parts, axis=0), NN)
    half = out.shape[0] // 2
    out_ref[...] = (out[:half] + out[half:]).astype(bf16)


def finish_kernel(got_ref, cot_ref, v_ref, bias_ref, out_ref, field, sems):
    sends = []
    for t in range(16):
        low, high = halves(got_ref[t * 32 : t * 32 + 16, :], got_ref[t * 32 + 16 : t * 32 + 32, :])
        coef = jnp.concatenate([low, high, low, high], axis=0)
        part = dot(coef, v_ref[...], TN).astype(bf16).astype(f32).reshape(2, 64, WIN)
        rows = slice(2 * t, 2 * t + 2)
        field[rows] = (cot_ref[rows].astype(f32) + part).astype(bf16)
        if t % 4 == 3:
            done = slice(2 * t - 6, 2 * t + 2)
            sends.append(pltpu.make_async_copy(field.at[done], out_ref.at[done], sems.at[t // 4]))
            sends[-1].start()
    for send in sends:
        send.wait()


def exchange(blocks, axis):
    return lax.all_to_all(blocks, axis, split_axis=0, concat_axis=0, tiled=True)


def body(activation, cotangent, spectral_weight, out_bias):
    const = {name: jnp.asarray(value) for name, value in tables().items()}
    shape = jax.ShapeDtypeStruct
    chan = lax.axis_size("chan")
    width = activation.shape[1]
    inputs = spectral_weight.shape[3]
    weight = spectral_weight.reshape(KEPT, 2 * width, inputs)
    bias_wide = jnp.broadcast_to(out_bias[:, None], (width, WIN))
    where = jnp.reshape(lax.axis_index("xh"), (1,)).astype(jnp.int32)
    pairs = [(0, 1), (1, 0)]
    partner = lax.ppermute(weight, "xh", pairs)
    square = pltpu.VMEM((M, 128), f32)
    tall = pltpu.VMEM((2 * M, 128), f32)
    small = shape((M, 128), bf16)
    coefs_shape = shape((PITCH * R // 2, 128), bf16)
    across = shape((chan, M, 128), bf16)
    mix_flops = 2 * KEPT * 64 * 128 * inputs

    first = run(
        points_kernel,
        shape((PITCH, R // 2 + width, 128), bf16),
        const["points"],
        activation,
        cotangent,
        scratch=[
            pltpu.VMEM((2 * R, WIN), bf16),
            pltpu.VMEM(activation.shape, bf16),
            pltpu.VMEM((PITCH, R // 2 + width, 128), bf16),
            pltpu.SemaphoreType.DMA((13,)),
        ],
        far=3,
        far_out=True,
        vmem=FIRST_LIMIT,
        name="points",
    )
    first = exchange(first, PITCH_AXES)
    spectra = run(modes_kernel, small, where, first, const["modes"], scalars=1, name="modes")
    spectra = exchange(spectra, "z")
    spectra = run(gather_kernel, across, spectra, partner, scratch=[square], far=1, name="gather")
    spectra = exchange(spectra, "chan")
    mixed, spec, send = run(
        mix_kernel,
        (small, shape((BOTH, 2 * Z, inputs), bf16), shape((KEPT, 2 * Z, inputs), bf16)),
        where,
        spectra,
        weight,
        partner,
        scalars=1,
        scratch=[square],
        flops=mix_flops,
        name="mix",
    )
    other_spec = lax.ppermute(send, "xh", pairs)
    mixed = exchange(mixed, "z")
    grads = run(
        pointwise_kernel,
        shape((2 * M, 128), bf16),
        mixed,
        first,
        bias_wide,
        const["doubled"],
        const["expand"],
        scratch=[square, tall],
        name="pointwise",
    )
    grads = exchange(grads, "z")
    back, grad, send = run(
        back_kernel,
        (
            across,
            shape((BOTH + 1, 2 * Z, 128), bf16),
            shape((KEPT + 1, 2 * Z, 128), bf16),
        ),
        where,
        grads,
        weight,
        partner,
        scalars=1,
        scratch=[tall],
        flops=mix_flops,
        name="back",
    )
    other_grad = lax.ppermute(send, "xh", pairs)
    back = exchange(back, "chan")
    grad_weight, bias = run(
        weight_kernel,
        (shape((KEPT, 2 * width, inputs), f32), shape((8, 64), f32)),
        where,
        grad,
        spec,
        other_grad,
        other_spec,
        scalars=1,
        flops=mix_flops,
        name="weight",
    )
    back = run(collect_kernel, small, back, scratch=[square], name="collect")
    back = exchange(back, "z")
    coefs = run(windows_kernel, coefs_shape, back, const["windows"], name="windows")
    coefs = exchange(coefs, PITCH_AXES)
    grad_input = run(
        finish_kernel,
        shape(activation.shape, bf16),
        coefs,
        cotangent,
        const["points"],
        bias,
        scratch=[pltpu.VMEM(activation.shape, bf16), pltpu.SemaphoreType.DMA((4,))],
        far_out=True,
        name="finish",
    )
    return grad_input, grad_weight.reshape(spectral_weight.shape), bias[0]


def solution(mesh):
    fine = Mesh(mesh.devices.reshape(XH, Z, -1), ("xh", "z", "chan"))
    field = P(None, "chan", ("xh", "z"))
    modes = P(("xh", "z"), None, "chan", None)
    return jax.shard_map(
        body,
        mesh=fine,
        in_specs=(field, field, modes, P("chan")),
        out_specs=(field, modes, P("chan")),
        check_vma=False,
    )
```

```python
import functools
import math

import jax
import jax.numpy as jnp
import ml_dtypes
import numpy as np
from jax import lax
from jax.experimental import pallas as pl
from jax.experimental.pallas import tpu as pltpu
from jax.sharding import Mesh
from jax.sharding import PartitionSpec as P

P_SIZE = 4096
M = 128
XH = 2
Z = 16
PITCH = XH * Z
WIN = P_SIZE // PITCH
KEPT = M // PITCH
BOTH = XH * KEPT
R = 32
PITCH_AXES = ("xh", "z")
f32 = jnp.float32
bf16 = jnp.bfloat16
NT = (((1,), (1,)), ((), ()))
NN = (((1,), (0,)), ((), ()))
TN = (((0,), (0,)), ((), ()))
VMEM_LIMIT = 32 * 1024 * 1024
FIRST_LIMIT = 60 * 1024 * 1024
MODES_LIMIT = 53 * 1024 * 1024


def split_hi_lo(table):
    hi = table.astype(ml_dtypes.bfloat16)
    lo = (table - hi.astype(np.float64)).astype(ml_dtypes.bfloat16)
    return hi, lo


@functools.cache
def tables():
    modes = np.arange(M)
    angle = 2.0 * math.pi * (np.outer(modes, np.arange(P_SIZE)) % P_SIZE) / P_SIZE
    forward = np.stack([np.cos(angle), -np.sin(angle)]) / math.sqrt(P_SIZE)
    basis = np.linalg.svd(forward[:, :, :WIN].reshape(2 * M, WIN))[2][:R]
    coef = np.einsum("akwp,xp->akwx", forward.reshape(2, M, PITCH, WIN), basis)
    coef = coef.reshape(2 * M, PITCH, 2, R // 2)
    out = {}
    hi, lo = split_hi_lo(basis)
    out["points"] = np.concatenate([hi, lo], axis=0)
    by_z = coef.reshape(2, XH, Z, KEPT, PITCH, 2, R // 2).transpose(5, 0, 2, 1, 3, 4, 6)
    gather = by_z.reshape(2, 2 * M, PITCH * R // 2)
    out["modes"] = np.stack(split_hi_lo(gather), axis=1).reshape(8 * M, PITCH * R // 2)
    spread = by_z.transpose(5, 6, 0, 1, 2, 3, 4)
    spread = spread.reshape(PITCH * R // 2, 4 * M)
    out["windows"] = np.concatenate(split_hi_lo(spread), axis=0)
    scale = np.where(modes == 0, 1.0, 2.0).reshape(1, XH, Z, KEPT, 1)
    scaled = coef.reshape(2, XH, Z, KEPT, PITCH * R) * scale
    scaled = scaled.transpose(0, 1, 3, 2, 4).reshape(2 * M, PITCH * R)
    out["doubled"] = np.stack(split_hi_lo(scaled))
    high, low = split_hi_lo(np.kron(np.eye(4), basis))
    out["expand"] = np.concatenate([high, high, low], axis=0)
    return out


def dot(left, right, dims):
    return lax.dot_general(left, right, dims, preferred_element_type=f32)


def run(kernel, out_shape, *args, scratch=(), flops=0, name=None, far=0, far_out=False, vmem=VMEM_LIMIT, scalars=0):
    out_space = pltpu.HBM if far_out else pltpu.VMEM
    near = [pl.BlockSpec(memory_space=pltpu.SMEM)] * scalars
    near += [pl.BlockSpec(memory_space=pltpu.VMEM)] * (len(args) - far - scalars)
    touched = sum(int(np.prod(a.shape)) * a.dtype.itemsize for a in list(args) + jax.tree.leaves(out_shape))
    return pl.pallas_call(
        kernel,
        out_shape=out_shape,
        in_specs=near + [pl.BlockSpec(memory_space=pltpu.HBM)] * far,
        out_specs=jax.tree.map(lambda _: pl.BlockSpec(memory_space=out_space), out_shape),
        scratch_shapes=list(scratch),
        compiler_params=pltpu.CompilerParams(vmem_limit_bytes=vmem),
        cost_estimate=pl.CostEstimate(flops=flops, bytes_accessed=touched, transcendentals=0),
        name=name,
    )(*args)


def halves(left, right):
    return (
        jnp.concatenate([left[:, :64], right[:, :64]], axis=1),
        jnp.concatenate([left[:, 64:], right[:, 64:]], axis=1),
    )


def points_kernel(v_ref, x_ref, cot_ref, out_ref, basis, field, message, sems):
    table = pltpu.make_async_copy(v_ref, basis, sems.at[12])
    fields, cots, sends = [], [], []
    for i in range(4):
        part = slice(8 * i, 8 * i + 8)
        fields.append(pltpu.make_async_copy(x_ref.at[part], field.at[part], sems.at[i]))
        cots.append(
            pltpu.make_async_copy(cot_ref.at[part], message.at[part, R // 2 :, :], sems.at[4 + i])
        )
        sends.append(pltpu.make_async_copy(message.at[part], out_ref.at[part], sems.at[8 + i]))
    table.start()
    for i in range(4):
        fields[i].start()
        cots[i].start()
    table.wait()
    for i in range(4):
        fields[i].wait()
        for t in range(4 * i, 4 * i + 4):
            y = dot(basis[...], field[2 * t : 2 * t + 2].reshape(128, WIN), NT)
            y = y[:R] + y[R:]
            first, second = halves(y[:16], y[16:])
            message[2 * t, 0:16, :] = first.astype(bf16)
            message[2 * t + 1, 0:16, :] = second.astype(bf16)
        cots[i].wait()
        sends[i].start()
    for i in range(4):
        sends[i].wait()


def modes_kernel(where_ref, got_ref, g_ref, out_ref, table, sems):
    copies = []
    for i in range(4):
        rows = slice(i * 2 * M, (i + 1) * 2 * M)
        copies.append(pltpu.make_async_copy(g_ref.at[rows], table.at[rows], sems.at[i]))
        copies[i].start()
    got = got_ref[:, 0 : R // 2, :].reshape(PITCH * R // 2, 128)
    parts = []
    for i in range(4):
        copies[i].wait()
        parts.append(dot(table[i * 2 * M : (i + 1) * 2 * M, :], got, NN))
    part = (parts[0] + parts[1])[:, :64] + (parts[2] + parts[3])[:, 64:]
    out_ref[...] = jnp.concatenate([part[:M], part[M:]], axis=1).astype(bf16)


def by_mode(scr, value, count):
    scr[...] = value
    return [scr[pl.ds(k, Z, stride=count), :] for k in range(BOTH)]


def gather_kernel(got_ref, arrived_ref, out_ref, scr):
    send = jnp.concatenate(by_mode(scr, got_ref[...].astype(f32), BOTH), axis=0).astype(bf16)
    for i in range(out_ref.shape[0]):
        out_ref[i] = send


def by_place(where_ref, own_ref, other_ref, step):
    for place in range(XH):
        refs = [own_ref, other_ref] if place == 0 else [other_ref, own_ref]

        @pl.when(where_ref[0] == place)
        def _(refs=refs):
            step([refs[k // KEPT].at[k % KEPT] for k in range(BOTH)])


def mix_kernel(where_ref, got_ref, own_ref, other_ref, out_ref, spec_ref, send_ref, scr):
    for k in range(BOTH):
        rows = slice(k * Z, (k + 1) * Z)
        re, im = [], []
        for q in range(got_ref.shape[0] // 2):
            first, second = halves(got_ref[2 * q, rows, :], got_ref[2 * q + 1, rows, :])
            re.append(first)
            im.append(second)
        spec_ref[k] = jnp.concatenate([jnp.concatenate(re, axis=1), jnp.concatenate(im, axis=1)], axis=0)

    def step(weights):
        for k in range(BOTH):
            out = dot(spec_ref[k], weights[k][...], NT)
            real = out[:Z, :64] - out[Z:, 64:]
            imag = out[:Z, 64:] + out[Z:, :64]
            scr[pl.ds(k, Z, stride=BOTH), :] = jnp.concatenate([real, imag], axis=1)

    by_place(where_ref, own_ref, other_ref, step)
    out_ref[...] = scr[...].astype(bf16)
    for k in range(KEPT):
        send_ref[k] = spec_ref[(1 - where_ref[0]) * KEPT + k]


def pointwise_kernel(got_ref, cot_ref, bias_ref, table_ref, e_ref, out_ref, scr, send):
    root = math.sqrt(2.0 / math.pi)
    mixed = jnp.concatenate(by_mode(scr, got_ref[...].astype(f32), BOTH), axis=0)
    mixed = mixed.T
    mixed = jnp.concatenate([mixed[:64], mixed[64:]], axis=1).astype(bf16)
    bias = bias_ref[...]
    total = jnp.zeros((64, WIN), f32)
    high, low = table_ref[0], table_ref[1]
    coef = dot(mixed, high, NN) + dot(mixed, low, NN)
    ys = []
    for half in range(2):
        groups = range(4 * half, 4 * half + 4)
        part = jnp.concatenate([coef[:, g * 128 : (g + 1) * 128] for g in groups], axis=0)
        part_high = part.astype(bf16)
        part_low = (part - part_high.astype(f32)).astype(bf16)
        response = dot(jnp.concatenate([part_high, part_low, part_high], axis=1), e_ref[...], NN)
        response = response.astype(bf16).astype(f32)
        blocks = []
        for j, g in enumerate(groups):
            grads = []
            for i in range(4):
                v = response[j * 64 : (j + 1) * 64, i * WIN : (i + 1) * WIN] + bias
                square = v * v
                th = jnp.tanh(root * (v + 0.044715 * (square * v)))
                slope = 0.5 * (1.0 + th) + (0.5 * root) * v * (1.0 - th * th) * (1.0 + (3.0 * 0.044715) * square)
                grad = slope * cot_ref[4 * g + i, R // 2 :, :].astype(f32)
                total = total + grad
                grads.append(grad.astype(bf16))
            blocks.append(jnp.concatenate(grads, axis=1))
        y = dot(jnp.concatenate(blocks, axis=0), e_ref[128:, :], NT)
        y = y[:, :128] + y[:, 128:]
        ys += [y[j * 64 : (j + 1) * 64] for j in range(4)]
    y = jnp.concatenate(ys, axis=1)
    y_high = y.astype(bf16)
    y_low = (y - y_high.astype(f32)).astype(bf16)
    modes = dot(high, jnp.concatenate([y_high, y_low], axis=0), NT)
    modes = modes[:, :64] + modes[:, 64:] + dot(low, y_high, NT)
    sums = lax.dot_general(
        jnp.ones((8, WIN), f32), total, NT, precision=lax.Precision.HIGHEST, preferred_element_type=f32
    )
    rounded = sums.astype(bf16).astype(f32)
    sums = jnp.concatenate([rounded, sums - rounded], axis=1)
    modes = jnp.concatenate([modes[:M], modes[M:]], axis=1)
    for k in range(BOTH):
        send[pl.ds(k, Z, stride=2 * BOTH), :] = modes[k * Z : (k + 1) * Z]
    send[pl.ds(BOTH, Z, stride=2 * BOTH), :] = jnp.concatenate([sums] * (Z // 8), axis=0)
    for k in range(BOTH + 1, 2 * BOTH):
        send[pl.ds(k, Z, stride=2 * BOTH), :] = jnp.zeros((Z, 128), f32)
    out_ref[...] = send[...].astype(bf16)


def back_kernel(where_ref, got_ref, own_ref, other_ref, out_ref, grad_ref, send_ref, scr):
    blocks = by_mode(scr, got_ref[...].astype(f32), 2 * BOTH)
    sums = jnp.sum(scr[pl.ds(BOTH, Z, stride=2 * BOTH), :], axis=0, keepdims=True)
    sums = sums[:, :64] + sums[:, 64:]
    rounded = sums.astype(bf16).astype(f32)
    sums = jnp.concatenate([rounded, sums - rounded], axis=1)
    grad_ref[BOTH] = jnp.broadcast_to(sums, (2 * Z, 128)).astype(bf16)
    for k in range(BOTH):
        top = blocks[k]
        low = jnp.concatenate([top[:, 64:], -top[:, :64]], axis=1)
        grad_ref[k] = jnp.concatenate([top, low], axis=0).astype(bf16)

    def step(weights):
        for k in range(BOTH):
            out = dot(grad_ref[k], weights[k][...], NN)
            rows = slice(k * Z, (k + 1) * Z)
            for q in range(out_ref.shape[0] // 2):
                lanes = slice(q * 128, (q + 1) * 128)
                first, second = halves(out[:Z, lanes], out[Z:, lanes])
                out_ref[2 * q, rows, :] = first.astype(bf16)
                out_ref[2 * q + 1, rows, :] = second.astype(bf16)

    by_place(where_ref, own_ref, other_ref, step)
    for k in range(KEPT):
        send_ref[k] = grad_ref[(1 - where_ref[0]) * KEPT + k]
    send_ref[KEPT] = grad_ref[BOTH]


def weight_kernel(where_ref, grad_ref, spec_ref, other_grad_ref, other_spec_ref, out_ref, bias_ref):
    for k in range(KEPT):
        mode = where_ref[0] * KEPT + k
        grad = jnp.concatenate([grad_ref[mode], other_grad_ref[k]], axis=0)
        spec = jnp.concatenate([spec_ref[mode], other_spec_ref[k]], axis=0)
        out_ref[k] = dot(grad, spec, TN)
    sums = grad_ref[BOTH].astype(f32) + other_grad_ref[KEPT].astype(f32)
    bias_ref[...] = (sums[:, :64] + sums[:, 64:])[:8]


def collect_kernel(got_ref, out_ref, scr):
    total = got_ref[0].astype(f32)
    for i in range(1, got_ref.shape[0]):
        total = total + got_ref[i].astype(f32)
    for k in range(BOTH):
        scr[pl.ds(k, Z, stride=BOTH), :] = total[k * Z : (k + 1) * Z]
    out_ref[...] = scr[...].astype(bf16)


def windows_kernel(got_ref, u_ref, out_ref):
    got = got_ref[...]
    turned = jnp.concatenate([got[:, 64:], got[:, :64]], axis=1)
    low = lax.broadcasted_iota(jnp.int32, got.shape, 1) < 64
    none = jnp.zeros_like(got)
    parts = [
        jnp.where(low, got, none),
        jnp.where(low, turned, none),
        jnp.where(low, none, turned),
        jnp.where(low, none, got),
    ]
    out = dot(u_ref[...], jnp.concatenate(parts, axis=0), NN)
    half = out.shape[0] // 2
    out_ref[...] = (out[:half] + out[half:]).astype(bf16)


def finish_kernel(got_ref, cot_ref, v_ref, bias_ref, out_ref, field, sems):
    sends = []
    for t in range(16):
        low, high = halves(got_ref[t * 32 : t * 32 + 16, :], got_ref[t * 32 + 16 : t * 32 + 32, :])
        coef = jnp.concatenate([low, high, low, high], axis=0)
        part = dot(coef, v_ref[...], TN).astype(bf16).astype(f32).reshape(2, 64, WIN)
        rows = slice(2 * t, 2 * t + 2)
        field[rows] = (cot_ref[rows].astype(f32) + part).astype(bf16)
        if t % 4 == 3:
            done = slice(2 * t - 6, 2 * t + 2)
            sends.append(pltpu.make_async_copy(field.at[done], out_ref.at[done], sems.at[t // 4]))
            sends[-1].start()
    for send in sends:
        send.wait()


def exchange(blocks, axis):
    return lax.all_to_all(blocks, axis, split_axis=0, concat_axis=0, tiled=True)


def body(activation, cotangent, spectral_weight, out_bias):
    const = {name: jnp.asarray(value) for name, value in tables().items()}
    shape = jax.ShapeDtypeStruct
    chan = lax.axis_size("chan")
    width = activation.shape[1]
    inputs = spectral_weight.shape[3]
    weight = spectral_weight.reshape(KEPT, 2 * width, inputs)
    bias_wide = jnp.broadcast_to(out_bias[:, None], (width, WIN))
    where = jnp.reshape(lax.axis_index("xh"), (1,)).astype(jnp.int32)
    pairs = [(0, 1), (1, 0)]
    partner = lax.ppermute(weight, "xh", pairs)
    square = pltpu.VMEM((M, 128), f32)
    tall = pltpu.VMEM((2 * M, 128), f32)
    small = shape((M, 128), bf16)
    coefs_shape = shape((PITCH * R // 2, 128), bf16)
    across = shape((chan, M, 128), bf16)
    mix_flops = 2 * KEPT * 64 * 128 * inputs

    first = run(
        points_kernel,
        shape((PITCH, R // 2 + width, 128), bf16),
        const["points"],
        activation,
        cotangent,
        scratch=[
            pltpu.VMEM((2 * R, WIN), bf16),
            pltpu.VMEM(activation.shape, bf16),
            pltpu.VMEM((PITCH, R // 2 + width, 128), bf16),
            pltpu.SemaphoreType.DMA((13,)),
        ],
        far=3,
        far_out=True,
        vmem=FIRST_LIMIT,
        name="points",
    )
    first = exchange(first, PITCH_AXES)
    spectra = run(
        modes_kernel,
        small,
        where,
        first,
        const["modes"],
        scalars=1,
        far=1,
        scratch=[pltpu.VMEM((8 * M, PITCH * R // 2), bf16), pltpu.SemaphoreType.DMA((4,))],
        vmem=MODES_LIMIT,
        name="modes",
    )
    spectra = exchange(spectra, "z")
    spectra = run(gather_kernel, across, spectra, partner, scratch=[square], far=1, name="gather")
    spectra = exchange(spectra, "chan")
    mixed, spec, send = run(
        mix_kernel,
        (small, shape((BOTH, 2 * Z, inputs), bf16), shape((KEPT, 2 * Z, inputs), bf16)),
        where,
        spectra,
        weight,
        partner,
        scalars=1,
        scratch=[square],
        flops=mix_flops,
        name="mix",
    )
    other_spec = lax.ppermute(send, "xh", pairs)
    mixed = exchange(mixed, "z")
    grads = run(
        pointwise_kernel,
        shape((2 * M, 128), bf16),
        mixed,
        first,
        bias_wide,
        const["doubled"],
        const["expand"],
        scratch=[square, tall],
        name="pointwise",
    )
    grads = exchange(grads, "z")
    back, grad, send = run(
        back_kernel,
        (
            across,
            shape((BOTH + 1, 2 * Z, 128), bf16),
            shape((KEPT + 1, 2 * Z, 128), bf16),
        ),
        where,
        grads,
        weight,
        partner,
        scalars=1,
        scratch=[tall],
        flops=mix_flops,
        name="back",
    )
    other_grad = lax.ppermute(send, "xh", pairs)
    back = exchange(back, "chan")
    grad_weight, bias = run(
        weight_kernel,
        (shape((KEPT, 2 * width, inputs), f32), shape((8, 64), f32)),
        where,
        grad,
        spec,
        other_grad,
        other_spec,
        scalars=1,
        flops=mix_flops,
        name="weight",
    )
    back = run(collect_kernel, small, back, scratch=[square], name="collect")
    back = exchange(back, "z")
    coefs = run(windows_kernel, coefs_shape, back, const["windows"], name="windows")
    coefs = exchange(coefs, PITCH_AXES)
    grad_input = run(
        finish_kernel,
        shape(activation.shape, bf16),
        coefs,
        cotangent,
        const["points"],
        bias,
        scratch=[pltpu.VMEM(activation.shape, bf16), pltpu.SemaphoreType.DMA((4,))],
        far_out=True,
        name="finish",
    )
    return grad_input, grad_weight.reshape(spectral_weight.shape), bias[0]


def solution(mesh):
    fine = Mesh(mesh.devices.reshape(XH, Z, -1), ("xh", "z", "chan"))
    field = P(None, "chan", ("xh", "z"))
    modes = P(("xh", "z"), None, "chan", None)
    return jax.shard_map(
        body,
        mesh=fine,
        in_specs=(field, field, modes, P("chan")),
        out_specs=(field, modes, P("chan")),
        check_vma=False,
    )
```

```python
import functools
import math

import jax
import jax.numpy as jnp
import ml_dtypes
import numpy as np
from jax import lax
from jax.experimental import pallas as pl
from jax.experimental.pallas import tpu as pltpu
from jax.sharding import Mesh
from jax.sharding import PartitionSpec as P

P_SIZE = 4096
M = 128
XH = 2
Z = 16
PITCH = XH * Z
WIN = P_SIZE // PITCH
KEPT = M // PITCH
BOTH = XH * KEPT
R = 32
PITCH_AXES = ("xh", "z")
f32 = jnp.float32
bf16 = jnp.bfloat16
NT = (((1,), (1,)), ((), ()))
NN = (((1,), (0,)), ((), ()))
TN = (((0,), (0,)), ((), ()))
VMEM_LIMIT = 32 * 1024 * 1024
FIRST_LIMIT = 60 * 1024 * 1024


def split_hi_lo(table):
    hi = table.astype(ml_dtypes.bfloat16)
    lo = (table - hi.astype(np.float64)).astype(ml_dtypes.bfloat16)
    return hi, lo


@functools.cache
def tables():
    modes = np.arange(M)
    angle = 2.0 * math.pi * (np.outer(modes, np.arange(P_SIZE)) % P_SIZE) / P_SIZE
    forward = np.stack([np.cos(angle), -np.sin(angle)]) / math.sqrt(P_SIZE)
    basis = np.linalg.svd(forward[:, :, :WIN].reshape(2 * M, WIN))[2][:R]
    coef = np.einsum("akwp,xp->akwx", forward.reshape(2, M, PITCH, WIN), basis)
    coef = coef.reshape(2 * M, PITCH, 2, R // 2)
    out = {}
    hi, lo = split_hi_lo(basis)
    out["points"] = np.concatenate([hi, lo], axis=0)
    by_z = coef.reshape(2, XH, Z, KEPT, PITCH, 2, R // 2).transpose(5, 0, 2, 1, 3, 4, 6)
    gather = by_z.reshape(2, 2 * M, PITCH * R // 2)
    out["modes"] = gather.astype(ml_dtypes.bfloat16).reshape(4 * M, PITCH * R // 2)
    spread = by_z.transpose(5, 6, 0, 1, 2, 3, 4)
    spread = spread.reshape(PITCH * R // 2, 4 * M)
    out["windows"] = np.concatenate(split_hi_lo(spread), axis=0)
    scale = np.where(modes == 0, 1.0, 2.0).reshape(1, XH, Z, KEPT, 1)
    scaled = coef.reshape(2, XH, Z, KEPT, PITCH * R) * scale
    scaled = scaled.transpose(0, 1, 3, 2, 4).reshape(2 * M, PITCH * R)
    out["doubled"] = np.stack(split_hi_lo(scaled))
    high, low = split_hi_lo(np.kron(np.eye(4), basis))
    out["expand"] = np.concatenate([high, high, low], axis=0)
    return out


def dot(left, right, dims):
    return lax.dot_general(left, right, dims, preferred_element_type=f32)


def run(kernel, out_shape, *args, scratch=(), flops=0, name=None, far=0, far_out=False, vmem=VMEM_LIMIT, scalars=0):
    out_space = pltpu.HBM if far_out else pltpu.VMEM
    near = [pl.BlockSpec(memory_space=pltpu.SMEM)] * scalars
    near += [pl.BlockSpec(memory_space=pltpu.VMEM)] * (len(args) - far - scalars)
    touched = sum(int(np.prod(a.shape)) * a.dtype.itemsize for a in list(args) + jax.tree.leaves(out_shape))
    return pl.pallas_call(
        kernel,
        out_shape=out_shape,
        in_specs=near + [pl.BlockSpec(memory_space=pltpu.HBM)] * far,
        out_specs=jax.tree.map(lambda _: pl.BlockSpec(memory_space=out_space), out_shape),
        scratch_shapes=list(scratch),
        compiler_params=pltpu.CompilerParams(vmem_limit_bytes=vmem),
        cost_estimate=pl.CostEstimate(flops=flops, bytes_accessed=touched, transcendentals=0),
        name=name,
    )(*args)


def halves(left, right):
    return (
        jnp.concatenate([left[:, :64], right[:, :64]], axis=1),
        jnp.concatenate([left[:, 64:], right[:, 64:]], axis=1),
    )


def points_kernel(v_ref, x_ref, cot_ref, out_ref, basis, field, message, sems):
    table = pltpu.make_async_copy(v_ref, basis, sems.at[12])
    fields, cots, sends = [], [], []
    for i in range(4):
        part = slice(8 * i, 8 * i + 8)
        fields.append(pltpu.make_async_copy(x_ref.at[part], field.at[part], sems.at[i]))
        cots.append(
            pltpu.make_async_copy(cot_ref.at[part], message.at[part, R // 2 :, :], sems.at[4 + i])
        )
        sends.append(pltpu.make_async_copy(message.at[part], out_ref.at[part], sems.at[8 + i]))
    table.start()
    for i in range(4):
        fields[i].start()
        cots[i].start()
    table.wait()
    for i in range(4):
        fields[i].wait()
        for t in range(4 * i, 4 * i + 4):
            y = dot(basis[...], field[2 * t : 2 * t + 2].reshape(128, WIN), NT)
            y = y[:R] + y[R:]
            first, second = halves(y[:16], y[16:])
            message[2 * t, 0:16, :] = first.astype(bf16)
            message[2 * t + 1, 0:16, :] = second.astype(bf16)
        cots[i].wait()
        sends[i].start()
    for i in range(4):
        sends[i].wait()


def modes_kernel(where_ref, got_ref, g_ref, out_ref):
    got = got_ref[:, 0 : R // 2, :].reshape(PITCH * R // 2, 128)
    part = dot(g_ref[...], got, NN)
    part = part[: 2 * M, :64] + part[2 * M :, 64:]
    out_ref[...] = jnp.concatenate([part[:M], part[M:]], axis=1).astype(bf16)


def by_mode(scr, value, count):
    scr[...] = value
    return [scr[pl.ds(k, Z, stride=count), :] for k in range(BOTH)]


def gather_kernel(got_ref, arrived_ref, out_ref, scr):
    send = jnp.concatenate(by_mode(scr, got_ref[...].astype(f32), BOTH), axis=0).astype(bf16)
    for i in range(out_ref.shape[0]):
        out_ref[i] = send


def by_place(where_ref, own_ref, other_ref, step):
    for place in range(XH):
        refs = [own_ref, other_ref] if place == 0 else [other_ref, own_ref]

        @pl.when(where_ref[0] == place)
        def _(refs=refs):
            step([refs[k // KEPT].at[k % KEPT] for k in range(BOTH)])


def mix_kernel(where_ref, got_ref, own_ref, other_ref, out_ref, spec_ref, send_ref, scr):
    for k in range(BOTH):
        rows = slice(k * Z, (k + 1) * Z)
        re, im = [], []
        for q in range(got_ref.shape[0] // 2):
            first, second = halves(got_ref[2 * q, rows, :], got_ref[2 * q + 1, rows, :])
            re.append(first)
            im.append(second)
        spec_ref[k] = jnp.concatenate([jnp.concatenate(re, axis=1), jnp.concatenate(im, axis=1)], axis=0)

    def step(weights):
        for k in range(BOTH):
            out = dot(spec_ref[k], weights[k][...], NT)
            real = out[:Z, :64] - out[Z:, 64:]
            imag = out[:Z, 64:] + out[Z:, :64]
            scr[pl.ds(k, Z, stride=BOTH), :] = jnp.concatenate([real, imag], axis=1)

    by_place(where_ref, own_ref, other_ref, step)
    out_ref[...] = scr[...].astype(bf16)
    for k in range(KEPT):
        send_ref[k] = spec_ref[(1 - where_ref[0]) * KEPT + k]


def pointwise_kernel(got_ref, cot_ref, bias_ref, table_ref, e_ref, out_ref, scr, send):
    root = math.sqrt(2.0 / math.pi)
    mixed = jnp.concatenate(by_mode(scr, got_ref[...].astype(f32), BOTH), axis=0)
    mixed = mixed.T
    mixed = jnp.concatenate([mixed[:64], mixed[64:]], axis=1).astype(bf16)
    bias = bias_ref[...]
    total = jnp.zeros((64, WIN), f32)
    high, low = table_ref[0], table_ref[1]
    coef = dot(mixed, high, NN) + dot(mixed, low, NN)
    ys = []
    for half in range(2):
        groups = range(4 * half, 4 * half + 4)
        part = jnp.concatenate([coef[:, g * 128 : (g + 1) * 128] for g in groups], axis=0)
        part_high = part.astype(bf16)
        part_low = (part - part_high.astype(f32)).astype(bf16)
        response = dot(jnp.concatenate([part_high, part_low, part_high], axis=1), e_ref[...], NN)
        response = response.astype(bf16).astype(f32)
        blocks = []
        for j, g in enumerate(groups):
            grads = []
            for i in range(4):
                v = response[j * 64 : (j + 1) * 64, i * WIN : (i + 1) * WIN] + bias
                square = v * v
                th = jnp.tanh(root * (v + 0.044715 * (square * v)))
                slope = 0.5 * (1.0 + th) + (0.5 * root) * v * (1.0 - th * th) * (1.0 + (3.0 * 0.044715) * square)
                grad = slope * cot_ref[4 * g + i, R // 2 :, :].astype(f32)
                total = total + grad
                grads.append(grad.astype(bf16))
            blocks.append(jnp.concatenate(grads, axis=1))
        y = dot(jnp.concatenate(blocks, axis=0), e_ref[128:, :], NT)
        y = y[:, :128] + y[:, 128:]
        ys += [y[j * 64 : (j + 1) * 64] for j in range(4)]
    y = jnp.concatenate(ys, axis=1)
    y_high = y.astype(bf16)
    y_low = (y - y_high.astype(f32)).astype(bf16)
    modes = dot(high, jnp.concatenate([y_high, y_low], axis=0), NT)
    modes = modes[:, :64] + modes[:, 64:] + dot(low, y_high, NT)
    sums = lax.dot_general(
        jnp.ones((8, WIN), f32), total, NT, precision=lax.Precision.HIGHEST, preferred_element_type=f32
    )
    rounded = sums.astype(bf16).astype(f32)
    sums = jnp.concatenate([rounded, sums - rounded], axis=1)
    modes = jnp.concatenate([modes[:M], modes[M:]], axis=1)
    for k in range(BOTH):
        send[pl.ds(k, Z, stride=2 * BOTH), :] = modes[k * Z : (k + 1) * Z]
    send[pl.ds(BOTH, Z, stride=2 * BOTH), :] = jnp.concatenate([sums] * (Z // 8), axis=0)
    for k in range(BOTH + 1, 2 * BOTH):
        send[pl.ds(k, Z, stride=2 * BOTH), :] = jnp.zeros((Z, 128), f32)
    out_ref[...] = send[...].astype(bf16)


def back_kernel(where_ref, got_ref, own_ref, other_ref, out_ref, grad_ref, send_ref, scr):
    blocks = by_mode(scr, got_ref[...].astype(f32), 2 * BOTH)
    sums = jnp.sum(scr[pl.ds(BOTH, Z, stride=2 * BOTH), :], axis=0, keepdims=True)
    sums = sums[:, :64] + sums[:, 64:]
    rounded = sums.astype(bf16).astype(f32)
    sums = jnp.concatenate([rounded, sums - rounded], axis=1)
    grad_ref[BOTH] = jnp.broadcast_to(sums, (2 * Z, 128)).astype(bf16)
    for k in range(BOTH):
        top = blocks[k]
        low = jnp.concatenate([top[:, 64:], -top[:, :64]], axis=1)
        grad_ref[k] = jnp.concatenate([top, low], axis=0).astype(bf16)

    def step(weights):
        for k in range(BOTH):
            out = dot(grad_ref[k], weights[k][...], NN)
            rows = slice(k * Z, (k + 1) * Z)
            for q in range(out_ref.shape[0] // 2):
                lanes = slice(q * 128, (q + 1) * 128)
                first, second = halves(out[:Z, lanes], out[Z:, lanes])
                out_ref[2 * q, rows, :] = first.astype(bf16)
                out_ref[2 * q + 1, rows, :] = second.astype(bf16)

    by_place(where_ref, own_ref, other_ref, step)
    for k in range(KEPT):
        send_ref[k] = grad_ref[(1 - where_ref[0]) * KEPT + k]
    send_ref[KEPT] = grad_ref[BOTH]


def weight_kernel(where_ref, grad_ref, spec_ref, other_grad_ref, other_spec_ref, out_ref, bias_ref):
    for k in range(KEPT):
        mode = where_ref[0] * KEPT + k
        grad = jnp.concatenate([grad_ref[mode], other_grad_ref[k]], axis=0)
        spec = jnp.concatenate([spec_ref[mode], other_spec_ref[k]], axis=0)
        out_ref[k] = dot(grad, spec, TN)
    sums = grad_ref[BOTH].astype(f32) + other_grad_ref[KEPT].astype(f32)
    bias_ref[...] = (sums[:, :64] + sums[:, 64:])[:8]


def collect_kernel(got_ref, out_ref, scr):
    total = got_ref[0].astype(f32)
    for i in range(1, got_ref.shape[0]):
        total = total + got_ref[i].astype(f32)
    for k in range(BOTH):
        scr[pl.ds(k, Z, stride=BOTH), :] = total[k * Z : (k + 1) * Z]
    out_ref[...] = scr[...].astype(bf16)


def windows_kernel(got_ref, u_ref, out_ref):
    got = got_ref[...]
    turned = jnp.concatenate([got[:, 64:], got[:, :64]], axis=1)
    low = lax.broadcasted_iota(jnp.int32, got.shape, 1) < 64
    none = jnp.zeros_like(got)
    parts = [
        jnp.where(low, got, none),
        jnp.where(low, turned, none),
        jnp.where(low, none, turned),
        jnp.where(low, none, got),
    ]
    out = dot(u_ref[...], jnp.concatenate(parts, axis=0), NN)
    half = out.shape[0] // 2
    out_ref[...] = (out[:half] + out[half:]).astype(bf16)


def finish_kernel(got_ref, cot_ref, v_ref, bias_ref, out_ref, field, sems):
    sends = []
    for t in range(16):
        low, high = halves(got_ref[t * 32 : t * 32 + 16, :], got_ref[t * 32 + 16 : t * 32 + 32, :])
        coef = jnp.concatenate([low, high, low, high], axis=0)
        part = dot(coef, v_ref[...], TN).astype(bf16).astype(f32).reshape(2, 64, WIN)
        rows = slice(2 * t, 2 * t + 2)
        field[rows] = (cot_ref[rows].astype(f32) + part).astype(bf16)
        if t % 4 == 3:
            done = slice(2 * t - 6, 2 * t + 2)
            sends.append(pltpu.make_async_copy(field.at[done], out_ref.at[done], sems.at[t // 4]))
            sends[-1].start()
    for send in sends:
        send.wait()


def exchange(blocks, axis):
    return lax.all_to_all(blocks, axis, split_axis=0, concat_axis=0, tiled=True)


def body(activation, cotangent, spectral_weight, out_bias):
    const = {name: jnp.asarray(value) for name, value in tables().items()}
    shape = jax.ShapeDtypeStruct
    chan = lax.axis_size("chan")
    width = activation.shape[1]
    inputs = spectral_weight.shape[3]
    weight = spectral_weight.reshape(KEPT, 2 * width, inputs)
    bias_wide = jnp.broadcast_to(out_bias[:, None], (width, WIN))
    where = jnp.reshape(lax.axis_index("xh"), (1,)).astype(jnp.int32)
    pairs = [(0, 1), (1, 0)]
    partner = lax.ppermute(weight, "xh", pairs)
    square = pltpu.VMEM((M, 128), f32)
    tall = pltpu.VMEM((2 * M, 128), f32)
    small = shape((M, 128), bf16)
    coefs_shape = shape((PITCH * R // 2, 128), bf16)
    across = shape((chan, M, 128), bf16)
    mix_flops = 2 * KEPT * 64 * 128 * inputs

    first = run(
        points_kernel,
        shape((PITCH, R // 2 + width, 128), bf16),
        const["points"],
        activation,
        cotangent,
        scratch=[
            pltpu.VMEM((2 * R, WIN), bf16),
            pltpu.VMEM(activation.shape, bf16),
            pltpu.VMEM((PITCH, R // 2 + width, 128), bf16),
            pltpu.SemaphoreType.DMA((13,)),
        ],
        far=3,
        far_out=True,
        vmem=FIRST_LIMIT,
        name="points",
    )
    first = exchange(first, PITCH_AXES)
    spectra = run(modes_kernel, small, where, first, const["modes"], scalars=1, name="modes")
    spectra = exchange(spectra, "z")
    spectra = run(gather_kernel, across, spectra, partner, scratch=[square], far=1, name="gather")
    spectra = exchange(spectra, "chan")
    mixed, spec, send = run(
        mix_kernel,
        (small, shape((BOTH, 2 * Z, inputs), bf16), shape((KEPT, 2 * Z, inputs), bf16)),
        where,
        spectra,
        weight,
        partner,
        scalars=1,
        scratch=[square],
        flops=mix_flops,
        name="mix",
    )
    other_spec = lax.ppermute(send, "xh", pairs)
    mixed = exchange(mixed, "z")
    grads = run(
        pointwise_kernel,
        shape((2 * M, 128), bf16),
        mixed,
        first,
        bias_wide,
        const["doubled"],
        const["expand"],
        scratch=[square, tall],
        name="pointwise",
    )
    grads = exchange(grads, "z")
    back, grad, send = run(
        back_kernel,
        (
            across,
            shape((BOTH + 1, 2 * Z, 128), bf16),
            shape((KEPT + 1, 2 * Z, 128), bf16),
        ),
        where,
        grads,
        weight,
        partner,
        scalars=1,
        scratch=[tall],
        flops=mix_flops,
        name="back",
    )
    other_grad = lax.ppermute(send, "xh", pairs)
    back = exchange(back, "chan")
    grad_weight, bias = run(
        weight_kernel,
        (shape((KEPT, 2 * width, inputs), f32), shape((8, 64), f32)),
        where,
        grad,
        spec,
        other_grad,
        other_spec,
        scalars=1,
        flops=mix_flops,
        name="weight",
    )
    back = run(collect_kernel, small, back, scratch=[square], name="collect")
    back = exchange(back, "z")
    coefs = run(windows_kernel, coefs_shape, back, const["windows"], name="windows")
    coefs = exchange(coefs, PITCH_AXES)
    grad_input = run(
        finish_kernel,
        shape(activation.shape, bf16),
        coefs,
        cotangent,
        const["points"],
        bias,
        scratch=[pltpu.VMEM(activation.shape, bf16), pltpu.SemaphoreType.DMA((4,))],
        far_out=True,
        name="finish",
    )
    return grad_input, grad_weight.reshape(spectral_weight.shape), bias[0]


def solution(mesh):
    fine = Mesh(mesh.devices.reshape(XH, Z, -1), ("xh", "z", "chan"))
    field = P(None, "chan", ("xh", "z"))
    modes = P(("xh", "z"), None, "chan", None)
    return jax.shard_map(
        body,
        mesh=fine,
        in_specs=(field, field, modes, P("chan")),
        out_specs=(field, modes, P("chan")),
        check_vma=False,
    )
```

```python
import functools
import math

import jax
import jax.numpy as jnp
import ml_dtypes
import numpy as np
from jax import lax
from jax.experimental import pallas as pl
from jax.experimental.pallas import tpu as pltpu
from jax.sharding import Mesh
from jax.sharding import PartitionSpec as P

P_SIZE = 4096
M = 128
XH = 2
Z = 16
PITCH = XH * Z
WIN = P_SIZE // PITCH
KEPT = M // PITCH
BOTH = XH * KEPT
R = 32
PITCH_AXES = ("xh", "z")
f32 = jnp.float32
bf16 = jnp.bfloat16
NT = (((1,), (1,)), ((), ()))
NN = (((1,), (0,)), ((), ()))
TN = (((0,), (0,)), ((), ()))
VMEM_LIMIT = 32 * 1024 * 1024
FIRST_LIMIT = 60 * 1024 * 1024


def split_hi_lo(table):
    hi = table.astype(ml_dtypes.bfloat16)
    lo = (table - hi.astype(np.float64)).astype(ml_dtypes.bfloat16)
    return hi, lo


@functools.cache
def tables():
    modes = np.arange(M)
    angle = 2.0 * math.pi * (np.outer(modes, np.arange(P_SIZE)) % P_SIZE) / P_SIZE
    forward = np.stack([np.cos(angle), -np.sin(angle)]) / math.sqrt(P_SIZE)
    basis = np.linalg.svd(forward[:, :, :WIN].reshape(2 * M, WIN))[2][:R]
    coef = np.einsum("akwp,xp->akwx", forward.reshape(2, M, PITCH, WIN), basis)
    coef = coef.reshape(2 * M, PITCH, 2, R // 2)
    out = {}
    hi, lo = split_hi_lo(basis)
    out["points"] = np.concatenate([hi, lo], axis=0)
    by_z = coef.reshape(2, XH, Z, KEPT, PITCH, 2, R // 2).transpose(5, 0, 2, 1, 3, 4, 6)
    gather = by_z.reshape(2, 2 * M, PITCH * R // 2)
    out["modes"] = gather.astype(ml_dtypes.bfloat16).reshape(4 * M, PITCH * R // 2)
    spread = by_z.transpose(5, 6, 0, 1, 2, 3, 4)
    spread = spread.reshape(PITCH * R // 2, 4 * M)
    out["windows"] = np.concatenate(split_hi_lo(spread), axis=0)
    scale = np.where(modes == 0, 1.0, 2.0).reshape(1, XH, Z, KEPT, 1)
    scaled = coef.reshape(2, XH, Z, KEPT, PITCH * R) * scale
    scaled = scaled.transpose(0, 1, 3, 2, 4).reshape(2 * M, PITCH * R)
    out["doubled"] = np.stack(split_hi_lo(scaled))
    high, low = split_hi_lo(np.kron(np.eye(4), basis))
    out["expand"] = np.concatenate([high, high, low], axis=0)
    return out


def dot(left, right, dims):
    return lax.dot_general(left, right, dims, preferred_element_type=f32)


def run(kernel, out_shape, *args, scratch=(), flops=0, name=None, far=0, far_out=False, vmem=VMEM_LIMIT, scalars=0):
    out_space = pltpu.HBM if far_out else pltpu.VMEM
    near = [pl.BlockSpec(memory_space=pltpu.SMEM)] * scalars
    near += [pl.BlockSpec(memory_space=pltpu.VMEM)] * (len(args) - far - scalars)
    touched = sum(int(np.prod(a.shape)) * a.dtype.itemsize for a in list(args) + jax.tree.leaves(out_shape))
    return pl.pallas_call(
        kernel,
        out_shape=out_shape,
        in_specs=near + [pl.BlockSpec(memory_space=pltpu.HBM)] * far,
        out_specs=jax.tree.map(lambda _: pl.BlockSpec(memory_space=out_space), out_shape),
        scratch_shapes=list(scratch),
        compiler_params=pltpu.CompilerParams(vmem_limit_bytes=vmem),
        cost_estimate=pl.CostEstimate(flops=flops, bytes_accessed=touched, transcendentals=0),
        name=name,
    )(*args)


def halves(left, right):
    return (
        jnp.concatenate([left[:, :64], right[:, :64]], axis=1),
        jnp.concatenate([left[:, 64:], right[:, 64:]], axis=1),
    )


def points_kernel(v_ref, x_ref, cot_ref, out_ref, basis, field, message, sems):
    table = pltpu.make_async_copy(v_ref, basis, sems.at[24])
    fields, cots, sends = [], [], []
    for i in range(8):
        part = slice(4 * i, 4 * i + 4)
        fields.append(pltpu.make_async_copy(x_ref.at[part], field.at[part], sems.at[i]))
        cots.append(
            pltpu.make_async_copy(cot_ref.at[part], message.at[part, R // 2 :, :], sems.at[8 + i])
        )
        sends.append(pltpu.make_async_copy(message.at[part], out_ref.at[part], sems.at[16 + i]))
    table.start()
    for i in range(8):
        fields[i].start()
        cots[i].start()
    table.wait()
    for i in range(8):
        fields[i].wait()
        for t in range(2 * i, 2 * i + 2):
            y = dot(basis[...], field[2 * t : 2 * t + 2].reshape(128, WIN), NT)
            y = y[:R] + y[R:]
            first, second = halves(y[:16], y[16:])
            message[2 * t, 0:16, :] = first.astype(bf16)
            message[2 * t + 1, 0:16, :] = second.astype(bf16)
        cots[i].wait()
        sends[i].start()
    for i in range(8):
        sends[i].wait()


def modes_kernel(where_ref, got_ref, g_ref, out_ref):
    got = got_ref[:, 0 : R // 2, :].reshape(PITCH * R // 2, 128)
    part = dot(g_ref[...], got, NN)
    part = part[: 2 * M, :64] + part[2 * M :, 64:]
    out_ref[...] = jnp.concatenate([part[:M], part[M:]], axis=1).astype(bf16)


def by_mode(scr, value, count):
    scr[...] = value
    return [scr[pl.ds(k, Z, stride=count), :] for k in range(BOTH)]


def gather_kernel(got_ref, arrived_ref, out_ref, scr):
    send = jnp.concatenate(by_mode(scr, got_ref[...].astype(f32), BOTH), axis=0).astype(bf16)
    for i in range(out_ref.shape[0]):
        out_ref[i] = send


def by_place(where_ref, own_ref, other_ref, step):
    for place in range(XH):
        refs = [own_ref, other_ref] if place == 0 else [other_ref, own_ref]

        @pl.when(where_ref[0] == place)
        def _(refs=refs):
            step([refs[k // KEPT].at[k % KEPT] for k in range(BOTH)])


def mix_kernel(where_ref, got_ref, own_ref, other_ref, out_ref, spec_ref, send_ref, scr):
    for k in range(BOTH):
        rows = slice(k * Z, (k + 1) * Z)
        re, im = [], []
        for q in range(got_ref.shape[0] // 2):
            first, second = halves(got_ref[2 * q, rows, :], got_ref[2 * q + 1, rows, :])
            re.append(first)
            im.append(second)
        spec_ref[k] = jnp.concatenate([jnp.concatenate(re, axis=1), jnp.concatenate(im, axis=1)], axis=0)

    def step(weights):
        for k in range(BOTH):
            out = dot(spec_ref[k], weights[k][...], NT)
            real = out[:Z, :64] - out[Z:, 64:]
            imag = out[:Z, 64:] + out[Z:, :64]
            scr[pl.ds(k, Z, stride=BOTH), :] = jnp.concatenate([real, imag], axis=1)

    by_place(where_ref, own_ref, other_ref, step)
    out_ref[...] = scr[...].astype(bf16)
    for k in range(KEPT):
        send_ref[k] = spec_ref[(1 - where_ref[0]) * KEPT + k]


def pointwise_kernel(got_ref, cot_ref, bias_ref, table_ref, e_ref, out_ref, scr, send):
    root = math.sqrt(2.0 / math.pi)
    mixed = jnp.concatenate(by_mode(scr, got_ref[...].astype(f32), BOTH), axis=0)
    mixed = mixed.T
    mixed = jnp.concatenate([mixed[:64], mixed[64:]], axis=1).astype(bf16)
    bias = bias_ref[...]
    total = jnp.zeros((64, WIN), f32)
    high, low = table_ref[0], table_ref[1]
    coef = dot(mixed, high, NN) + dot(mixed, low, NN)
    ys = []
    for half in range(2):
        groups = range(4 * half, 4 * half + 4)
        part = jnp.concatenate([coef[:, g * 128 : (g + 1) * 128] for g in groups], axis=0)
        part_high = part.astype(bf16)
        part_low = (part - part_high.astype(f32)).astype(bf16)
        response = dot(jnp.concatenate([part_high, part_low, part_high], axis=1), e_ref[...], NN)
        response = response.astype(bf16).astype(f32)
        blocks = []
        for j, g in enumerate(groups):
            grads = []
            for i in range(4):
                v = response[j * 64 : (j + 1) * 64, i * WIN : (i + 1) * WIN] + bias
                square = v * v
                th = jnp.tanh(root * (v + 0.044715 * (square * v)))
                slope = 0.5 * (1.0 + th) + (0.5 * root) * v * (1.0 - th * th) * (1.0 + (3.0 * 0.044715) * square)
                grad = slope * cot_ref[4 * g + i, R // 2 :, :].astype(f32)
                total = total + grad
                grads.append(grad.astype(bf16))
            blocks.append(jnp.concatenate(grads, axis=1))
        y = dot(jnp.concatenate(blocks, axis=0), e_ref[128:, :], NT)
        y = y[:, :128] + y[:, 128:]
        ys += [y[j * 64 : (j + 1) * 64] for j in range(4)]
    y = jnp.concatenate(ys, axis=1)
    y_high = y.astype(bf16)
    y_low = (y - y_high.astype(f32)).astype(bf16)
    modes = dot(high, jnp.concatenate([y_high, y_low], axis=0), NT)
    modes = modes[:, :64] + modes[:, 64:] + dot(low, y_high, NT)
    sums = lax.dot_general(
        jnp.ones((8, WIN), f32), total, NT, precision=lax.Precision.HIGHEST, preferred_element_type=f32
    )
    rounded = sums.astype(bf16).astype(f32)
    sums = jnp.concatenate([rounded, sums - rounded], axis=1)
    modes = jnp.concatenate([modes[:M], modes[M:]], axis=1)
    for k in range(BOTH):
        send[pl.ds(k, Z, stride=2 * BOTH), :] = modes[k * Z : (k + 1) * Z]
    send[pl.ds(BOTH, Z, stride=2 * BOTH), :] = jnp.concatenate([sums] * (Z // 8), axis=0)
    for k in range(BOTH + 1, 2 * BOTH):
        send[pl.ds(k, Z, stride=2 * BOTH), :] = jnp.zeros((Z, 128), f32)
    out_ref[...] = send[...].astype(bf16)


def back_kernel(where_ref, got_ref, own_ref, other_ref, out_ref, grad_ref, send_ref, scr):
    blocks = by_mode(scr, got_ref[...].astype(f32), 2 * BOTH)
    sums = jnp.sum(scr[pl.ds(BOTH, Z, stride=2 * BOTH), :], axis=0, keepdims=True)
    sums = sums[:, :64] + sums[:, 64:]
    rounded = sums.astype(bf16).astype(f32)
    sums = jnp.concatenate([rounded, sums - rounded], axis=1)
    grad_ref[BOTH] = jnp.broadcast_to(sums, (2 * Z, 128)).astype(bf16)
    for k in range(BOTH):
        top = blocks[k]
        low = jnp.concatenate([top[:, 64:], -top[:, :64]], axis=1)
        grad_ref[k] = jnp.concatenate([top, low], axis=0).astype(bf16)

    def step(weights):
        for k in range(BOTH):
            out = dot(grad_ref[k], weights[k][...], NN)
            rows = slice(k * Z, (k + 1) * Z)
            for q in range(out_ref.shape[0] // 2):
                lanes = slice(q * 128, (q + 1) * 128)
                first, second = halves(out[:Z, lanes], out[Z:, lanes])
                out_ref[2 * q, rows, :] = first.astype(bf16)
                out_ref[2 * q + 1, rows, :] = second.astype(bf16)

    by_place(where_ref, own_ref, other_ref, step)
    for k in range(KEPT):
        send_ref[k] = grad_ref[(1 - where_ref[0]) * KEPT + k]
    send_ref[KEPT] = grad_ref[BOTH]


def weight_kernel(where_ref, grad_ref, spec_ref, other_grad_ref, other_spec_ref, out_ref, bias_ref):
    for k in range(KEPT):
        mode = where_ref[0] * KEPT + k
        grad = jnp.concatenate([grad_ref[mode], other_grad_ref[k]], axis=0)
        spec = jnp.concatenate([spec_ref[mode], other_spec_ref[k]], axis=0)
        out_ref[k] = dot(grad, spec, TN)
    sums = grad_ref[BOTH].astype(f32) + other_grad_ref[KEPT].astype(f32)
    bias_ref[...] = (sums[:, :64] + sums[:, 64:])[:8]


def collect_kernel(got_ref, out_ref, scr):
    total = got_ref[0].astype(f32)
    for i in range(1, got_ref.shape[0]):
        total = total + got_ref[i].astype(f32)
    for k in range(BOTH):
        scr[pl.ds(k, Z, stride=BOTH), :] = total[k * Z : (k + 1) * Z]
    out_ref[...] = scr[...].astype(bf16)


def windows_kernel(got_ref, u_ref, out_ref):
    got = got_ref[...]
    turned = jnp.concatenate([got[:, 64:], got[:, :64]], axis=1)
    low = lax.broadcasted_iota(jnp.int32, got.shape, 1) < 64
    none = jnp.zeros_like(got)
    parts = [
        jnp.where(low, got, none),
        jnp.where(low, turned, none),
        jnp.where(low, none, turned),
        jnp.where(low, none, got),
    ]
    out = dot(u_ref[...], jnp.concatenate(parts, axis=0), NN)
    half = out.shape[0] // 2
    out_ref[...] = (out[:half] + out[half:]).astype(bf16)


def finish_kernel(got_ref, cot_ref, v_ref, bias_ref, out_ref, field, sems):
    sends = []
    for t in range(16):
        low, high = halves(got_ref[t * 32 : t * 32 + 16, :], got_ref[t * 32 + 16 : t * 32 + 32, :])
        coef = jnp.concatenate([low, high, low, high], axis=0)
        part = dot(coef, v_ref[...], TN).astype(bf16).astype(f32).reshape(2, 64, WIN)
        rows = slice(2 * t, 2 * t + 2)
        field[rows] = (cot_ref[rows].astype(f32) + part).astype(bf16)
        if t % 4 == 3:
            done = slice(2 * t - 6, 2 * t + 2)
            sends.append(pltpu.make_async_copy(field.at[done], out_ref.at[done], sems.at[t // 4]))
            sends[-1].start()
    for send in sends:
        send.wait()


def exchange(blocks, axis):
    return lax.all_to_all(blocks, axis, split_axis=0, concat_axis=0, tiled=True)


def body(activation, cotangent, spectral_weight, out_bias):
    const = {name: jnp.asarray(value) for name, value in tables().items()}
    shape = jax.ShapeDtypeStruct
    chan = lax.axis_size("chan")
    width = activation.shape[1]
    inputs = spectral_weight.shape[3]
    weight = spectral_weight.reshape(KEPT, 2 * width, inputs)
    bias_wide = jnp.broadcast_to(out_bias[:, None], (width, WIN))
    where = jnp.reshape(lax.axis_index("xh"), (1,)).astype(jnp.int32)
    pairs = [(0, 1), (1, 0)]
    partner = lax.ppermute(weight, "xh", pairs)
    square = pltpu.VMEM((M, 128), f32)
    tall = pltpu.VMEM((2 * M, 128), f32)
    small = shape((M, 128), bf16)
    coefs_shape = shape((PITCH * R // 2, 128), bf16)
    across = shape((chan, M, 128), bf16)
    mix_flops = 2 * KEPT * 64 * 128 * inputs

    first = run(
        points_kernel,
        shape((PITCH, R // 2 + width, 128), bf16),
        const["points"],
        activation,
        cotangent,
        scratch=[
            pltpu.VMEM((2 * R, WIN), bf16),
            pltpu.VMEM(activation.shape, bf16),
            pltpu.VMEM((PITCH, R // 2 + width, 128), bf16),
            pltpu.SemaphoreType.DMA((25,)),
        ],
        far=3,
        far_out=True,
        vmem=FIRST_LIMIT,
        name="points",
    )
    first = exchange(first, PITCH_AXES)
    spectra = run(modes_kernel, small, where, first, const["modes"], scalars=1, name="modes")
    spectra = exchange(spectra, "z")
    spectra = run(gather_kernel, across, spectra, partner, scratch=[square], far=1, name="gather")
    spectra = exchange(spectra, "chan")
    mixed, spec, send = run(
        mix_kernel,
        (small, shape((BOTH, 2 * Z, inputs), bf16), shape((KEPT, 2 * Z, inputs), bf16)),
        where,
        spectra,
        weight,
        partner,
        scalars=1,
        scratch=[square],
        flops=mix_flops,
        name="mix",
    )
    other_spec = lax.ppermute(send, "xh", pairs)
    mixed = exchange(mixed, "z")
    grads = run(
        pointwise_kernel,
        shape((2 * M, 128), bf16),
        mixed,
        first,
        bias_wide,
        const["doubled"],
        const["expand"],
        scratch=[square, tall],
        name="pointwise",
    )
    grads = exchange(grads, "z")
    back, grad, send = run(
        back_kernel,
        (
            across,
            shape((BOTH + 1, 2 * Z, 128), bf16),
            shape((KEPT + 1, 2 * Z, 128), bf16),
        ),
        where,
        grads,
        weight,
        partner,
        scalars=1,
        scratch=[tall],
        flops=mix_flops,
        name="back",
    )
    other_grad = lax.ppermute(send, "xh", pairs)
    back = exchange(back, "chan")
    grad_weight, bias = run(
        weight_kernel,
        (shape((KEPT, 2 * width, inputs), f32), shape((8, 64), f32)),
        where,
        grad,
        spec,
        other_grad,
        other_spec,
        scalars=1,
        flops=mix_flops,
        name="weight",
    )
    back = run(collect_kernel, small, back, scratch=[square], name="collect")
    back = exchange(back, "z")
    coefs = run(windows_kernel, coefs_shape, back, const["windows"], name="windows")
    coefs = exchange(coefs, PITCH_AXES)
    grad_input = run(
        finish_kernel,
        shape(activation.shape, bf16),
        coefs,
        cotangent,
        const["points"],
        bias,
        scratch=[pltpu.VMEM(activation.shape, bf16), pltpu.SemaphoreType.DMA((4,))],
        far_out=True,
        name="finish",
    )
    return grad_input, grad_weight.reshape(spectral_weight.shape), bias[0]


def solution(mesh):
    fine = Mesh(mesh.devices.reshape(XH, Z, -1), ("xh", "z", "chan"))
    field = P(None, "chan", ("xh", "z"))
    modes = P(("xh", "z"), None, "chan", None)
    return jax.shard_map(
        body,
        mesh=fine,
        in_specs=(field, field, modes, P("chan")),
        out_specs=(field, modes, P("chan")),
        check_vma=False,
    )
```
